512 devices in a mesh: ctx: 64 (over z, x), head: 8 (over y, core).
Axes of the slice: x: 4, y: 4, z: 16, core: 2. Of those that a mesh axis runs over, the one named last changes fastest.
Arguments:
- qk_vectors: bfloat16 [16384, 1024], P('ctx', 'head'), may hold values from -10 to 10
- token_values: bfloat16 [16384, 1024], P('ctx', 'head'), may hold values from -6 to 6
- grad_output: bfloat16 [16384, 1024], P('ctx', 'head'), may hold values from -6 to 6
- out_weight: bfloat16 [1024, 1024], P('head'), may hold values from -0.1875 to 0.1875
- global_ids: int32 [2], replicated, may hold values from 0 to 63
- pair_active: int32 [4, 32], replicated, may hold values 0 or 1
Outputs:
- projected: bfloat16 [16384, 1024], P('ctx', 'head')
- grad_qk: bfloat16 [16384, 1024], P('ctx', 'head')
- grad_val: bfloat16 [16384, 1024], P('ctx', 'head')
- grad_weight: float32 [1024, 1024], P('head')
The draws below stay inside these ranges and needn't reach their ends.
All inputs are finite; a program needn't handle non-finite values.
Results may differ from the reference program's by a relative error of at most 0.014.
Values may be sent and summed in bfloat16 or wider, within the bound.
No kernel may reach another device: no remote copies, remote signals or barrier semaphores. Data moves between devices by JAX's collectives and lax.ppermute only.
A program may use at most 64 MiB of HBM per device.

```python
import math
import jax
import jax.numpy as jnp
from jax import lax

H = 16
HD = 64
BLOCK = 256
NGLOB = 2
ROUNDS = 4
D = 1024
TOKENS = 16384
PAIR_SLOTS = 32
N_CTX = 64


def draw_qk_vectors(key, part):
    key = jax.random.fold_in(key, 11)
    key_base = jax.random.fold_in(key, 0)
    result = jnp.clip(0.7 * jax.random.normal(key_base, (TOKENS, H * HD), jnp.float32), -4.0, 4.0)
    return result.astype(jnp.bfloat16)


def plant(values, key, smallest, high):
    index_at = [jax.random.randint(jax.random.fold_in(key, axis), (), 0, length) for axis, length in enumerate(values.shape)]
    longest = values.shape.index(max(values.shape))
    beside = index_at[:longest] + [(index_at[longest] + 1) % values.shape[longest]] + index_at[longest + 1:]
    return values.at[tuple(index_at)].set(smallest).at[tuple(beside)].set(high)


def block_levels(own_key, shape, cuts, low, largest):
    def one(dim, blocks):
        steps = jax.random.uniform(jax.random.fold_in(jax.random.fold_in(own_key, 6), dim), (blocks,), jnp.float32, low / len(cuts), largest / len(cuts))
        return jnp.repeat(jnp.exp(steps), shape[dim] // blocks).reshape((-1,) + (1,) * (len(shape) - dim - 1))

    gain = one(*cuts[0])
    for cut in cuts[1:]:
        gain = gain * one(*cut)
    return gain


def normal_values(rng, dims, deviation, reach, cuts=(), kind=jnp.bfloat16):
    array = jax.random.normal(rng, dims, jnp.float32) * deviation
    if len(cuts) > 0:
        array = block_levels(rng, dims, cuts, -0.22, 0.18) * array
    return jnp.clip(array, min=-reach, max=reach).astype(kind)


def setup_inputs(seed: int = 0) -> dict:
    keys = jax.random.split(jax.random.key(seed), 7)
    return {
        "qk_vectors": draw_qk_vectors(jax.random.fold_in(keys[6], 71), 0),
        "token_values": normal_values(keys[1], (TOKENS, D), 1.0, 6.0, ((0, 64), (1, 8))),
        "grad_output": normal_values(keys[2], (TOKENS, D), 1.0, 6.0, ((0, 64), (1, 8))),
        "out_weight": normal_values(keys[3], (D, D), D ** -0.5, 0.1875, ((0, 8),)),
        "global_ids": jax.random.randint(keys[4], (NGLOB,), 0, N_CTX).astype(jnp.int32),
        "pair_active": plant((jax.random.randint(keys[5], (ROUNDS, PAIR_SLOTS), 0, 2) < 1).astype(jnp.int32), jax.random.fold_in(keys[5], 1), 0, 1),
    }


def key_table(global_ids, pair_active):
    blocks = jnp.arange(N_CTX, dtype=jnp.int32)
    columns = [jnp.maximum(blocks - 1, 0), blocks, jnp.minimum(blocks + 1, N_CTX - 1)]
    marks = [(blocks > 0).astype(jnp.float32), jnp.ones((N_CTX,), jnp.float32), (blocks < N_CTX - 1).astype(jnp.float32)]
    for g in range(NGLOB):
        columns.append(jnp.zeros_like(blocks) + global_ids[g])
        marks.append(jnp.ones((N_CTX,), jnp.float32))
    for k in range(ROUNDS):
        stride = 1 << k
        lowest = jnp.bitwise_and(blocks, N_CTX - 1 - stride)
        pair_slot = jnp.right_shift(lowest, k + 1) * stride + jnp.bitwise_and(lowest, stride - 1)
        columns.append(jnp.bitwise_xor(blocks, stride))
        marks.append(pair_active[k][pair_slot].astype(jnp.float32))
    return (jnp.stack(columns, axis=1), jnp.stack(marks, axis=1))

def block_weights(query, key_rows, value_rows, allowed_keys):
    head_count = query.shape[1] // HD
    scaling = 1.0 / math.sqrt(HD)
    query_heads = query.reshape(BLOCK, head_count, HD).astype(jnp.float32)
    key_heads = key_rows.reshape(-1, BLOCK, head_count, HD).astype(jnp.float32)
    value_heads = value_rows.reshape(-1, BLOCK, head_count, HD).astype(jnp.float32)
    scores = jnp.einsum('qhd,jkhd->hqjk', query_heads, key_heads) * scaling
    allowed = (allowed_keys > 0.0)[None, None, :, None]
    highest = lax.optimization_barrier(jnp.max(jnp.where(allowed, scores, -1e+30), axis=(2, 3), keepdims=True))
    summed = lax.optimization_barrier(jnp.sum(jnp.where(allowed, jnp.exp(scores - highest), 0.0), axis=(2, 3), keepdims=True))
    log_total = highest + jnp.log(summed)
    weights = jnp.where(allowed, jnp.exp(scores - log_total), 0.0)
    rounded = lax.optimization_barrier(weights.astype(jnp.bfloat16)).astype(jnp.float32)
    return (query_heads, key_heads, value_heads, weights, rounded)

def block_forward(query, key_rows, value_rows, allowed_keys):
    head_count = query.shape[1] // HD
    parts = block_weights(query, key_rows, value_rows, allowed_keys)
    attended = jnp.einsum('hqjk,jkhd->qhd', parts[4], parts[2])
    return attended.reshape(BLOCK, head_count * HD)

def block_backward(query, key_rows, value_rows, allowed_keys, grad_rows, attended):
    head_count = query.shape[1] // HD
    scaling = 1.0 / math.sqrt(HD)
    query_heads, key_heads, value_heads, weights, rounded = block_weights(query, key_rows, value_rows, allowed_keys)
    grad_heads = grad_rows.reshape(BLOCK, head_count, HD).astype(jnp.float32)
    row_dot = lax.optimization_barrier(jnp.sum(grad_heads * attended.reshape(BLOCK, head_count, HD), axis=2))
    grad_weights = jnp.einsum('qhd,jkhd->hqjk', grad_heads, value_heads)
    grad_scores = weights * (grad_weights - row_dot.T[:, :, None, None])
    grad_scores = lax.optimization_barrier(grad_scores.astype(jnp.bfloat16)).astype(jnp.float32)
    grad_query = jnp.einsum('hqjk,jkhd->qhd', grad_scores, key_heads) * scaling
    grad_keys = jnp.einsum('hqjk,qhd->jkhd', grad_scores, query_heads) * scaling
    grad_values = jnp.einsum('hqjk,qhd->jkhd', rounded, grad_heads)
    width = head_count * HD
    return (grad_query.reshape(BLOCK, width), grad_keys.reshape(-1, BLOCK, width), grad_values.reshape(-1, BLOCK, width))

def reference(qk_vectors, token_values, grad_output, out_weight, global_ids, pair_active):
    width = H * HD
    key_index, allowed_all = key_table(global_ids, pair_active)
    qk_blocks = qk_vectors.reshape(N_CTX, BLOCK, width)
    value_blocks = token_values.reshape(N_CTX, BLOCK, width)

    def forward_one(block_index):
        key_rows = key_index[block_index]
        return block_forward(qk_blocks[block_index], qk_blocks[key_rows], value_blocks[key_rows], allowed_all[block_index])
    attended = lax.map(forward_one, jnp.arange(N_CTX, dtype=jnp.int32))
    attended_b = attended.reshape(TOKENS, width).astype(jnp.bfloat16)
    projected = jnp.dot(attended_b, out_weight, preferred_element_type=jnp.float32).astype(jnp.bfloat16)
    grad_attended = lax.dot_general(grad_output, out_weight, (((1,), (1,)), ((), ())), preferred_element_type=jnp.float32).astype(jnp.bfloat16)
    grad_weight = lax.dot_general(attended_b, grad_output, (((0,), (0,)), ((), ())), preferred_element_type=jnp.float32)
    grad_blocks = grad_attended.reshape(N_CTX, BLOCK, width)

    def backward_step(accums, block_index):
        key_acc, value_acc = accums
        key_rows = key_index[block_index]
        grad_query, grad_keys, grad_values = block_backward(qk_blocks[block_index], qk_blocks[key_rows], value_blocks[key_rows], allowed_all[block_index], grad_blocks[block_index], attended[block_index])
        key_acc = key_acc.at[key_rows].add(grad_keys)
        value_acc = value_acc.at[key_rows].add(grad_values)
        return ((key_acc, value_acc), grad_query)
    empty_acc = jnp.zeros((N_CTX, BLOCK, width), jnp.float32)
    (key_acc, value_acc), grad_query = lax.scan(backward_step, (empty_acc, empty_acc), jnp.arange(N_CTX, dtype=jnp.int32))
    grad_qk = (grad_query + key_acc).reshape(TOKENS, width).astype(jnp.bfloat16)
    grad_val = value_acc.reshape(TOKENS, width).astype(jnp.bfloat16)
    return (projected, grad_qk, grad_val, grad_weight)
```

```python
import functools
import math

import jax
import jax.numpy as jnp
from jax import lax
from jax.experimental import pallas as pl
from jax.experimental.pallas import tpu as pltpu
from jax.sharding import Mesh, PartitionSpec as P

HD = 64
NGLOB = 2
ROUNDS = 4
CTX = ("z", "x")
HEAD = ("y", "core")
NT = (((1,), (1,)), ((), ()))
TN = (((0,), (0,)), ((), ()))
NN = (((1,), (0,)), ((), ()))
F32 = jnp.float32
BF16 = jnp.bfloat16
MASKED = -1e30


def dot(a, b, dims):
    return lax.dot_general(a, b, dims, preferred_element_type=F32)


def attention_kernel(
    bias_ref, own_ref, p0, p1, p2, p3, p4, glob_ref, gout_ref, w_ref,
    partial_ref, sums_ref, r0, r1, r2, r3, r4, gquery_ref, gown_ref,
    score_ref, out_ref,
):
    length = own_ref.shape[0] // 2
    width = own_ref.shape[1]
    pieces = gout_ref.shape[0]
    nheads = width // HD
    scaling = 1.0 / math.sqrt(HD)
    base2 = scaling / math.log(2.0)
    keys = [r[:length] for r in (own_ref, p0, p1, p2, p3, p4)]
    vals = [r[length:] for r in (own_ref, p0, p1, p2, p3, p4)]
    for g in range(NGLOB):
        keys.append(glob_ref[g, :length])
        vals.append(glob_ref[g, length:])
    count = len(keys)
    query = own_ref[:length]
    lane = lax.broadcasted_iota(jnp.int32, (1, width), 1) // HD

    gatt = jnp.zeros((length, width), F32)
    for c in range(pieces):
        gatt = gatt + dot(gout_ref[c], w_ref[:, c * 128:(c + 1) * 128], NT)
    gatt_b = gatt.astype(BF16)

    inverse = []
    for h in range(nheads):
        query_h = jnp.where(lane == h, query, jnp.zeros_like(query))
        highest = jnp.full((length, 1), MASKED, F32)
        for b in range(count):
            s = dot(query_h, keys[b], NT) * base2 + bias_ref[b]
            score_ref[h, :, b * length:(b + 1) * length] = s
            highest = jnp.maximum(highest, jnp.max(s, axis=1, keepdims=True))
        total = jnp.zeros((length, 1), F32)
        for b in range(count):
            e = jnp.exp2(score_ref[h, :, b * length:(b + 1) * length] - highest)
            score_ref[h, :, b * length:(b + 1) * length] = e
            total = total + jnp.sum(e, axis=1, keepdims=True)
        inv = 1.0 / total
        inverse.append(inv)
        acc = jnp.zeros((length, width), F32)
        for b in range(count):
            e = score_ref[h, :, b * length:(b + 1) * length]
            acc = acc + dot((e * inv).astype(BF16), vals[b], NN)
        if h == 0:
            out_ref[...] = acc
        else:
            out_ref[...] = jnp.where(lane == h, acc, out_ref[...])

    attended = out_ref[...]
    attended_b = attended.astype(BF16)
    for c in range(pieces):
        partial_ref[c] = dot(attended_b, w_ref[:, c * 128:(c + 1) * 128], NN)
        part = dot(attended_b, gout_ref[c], TN).astype(BF16)
        n = width // 16
        sums_ref[c * n:(c + 1) * n, 0:16, :] = part.reshape(n, 16, 128)

    product = gatt_b.astype(F32) * attended
    query_t = query.astype(F32).T.astype(BF16)
    gatt_t = gatt_b.astype(F32).T.astype(BF16)
    outs = [gown_ref, r0, r1, r2, r3, r4]
    for h in range(nheads):
        gatt_h = jnp.where(lane == h, gatt_b, jnp.zeros_like(gatt_b))
        row_dot = jnp.sum(jnp.where(lane == h, product, 0.0), axis=1, keepdims=True)
        inv = inverse[h]
        qt = query_t[h * HD:(h + 1) * HD]
        gt = gatt_t[h * HD:(h + 1) * HD]
        acc = jnp.zeros((length, width), F32)
        for b in range(count - 1, -1, -1):
            weights = score_ref[h, :, b * length:(b + 1) * length] * inv
            gw = dot(gatt_h, vals[b], NT)
            gs = (weights * (gw - row_dot)).astype(BF16)
            acc = acc + dot(gs, keys[b], NN)
            gk = dot(qt, gs, NN) * scaling
            gv = dot(gt, weights.astype(BF16), NN)
            if b < count - NGLOB:
                o = outs[b]
                o[h * HD:(h + 1) * HD, :] = gk.astype(o.dtype)
                o[width + h * HD:width + (h + 1) * HD, :] = gv.astype(o.dtype)
            else:
                g = b - (count - NGLOB)
                n = HD // 16
                rows = width * 2 // 16
                for a in range(length // 128):
                    at = (g * (length // 128) + a) * rows
                    sub = gk[:, a * 128:(a + 1) * 128].astype(BF16)
                    sums_ref[at + h * n:at + (h + 1) * n, 16:32, :] = sub.reshape(n, 16, 128)
                    sub = gv[:, a * 128:(a + 1) * 128].astype(BF16)
                    at = at + width // 16
                    sums_ref[at + h * n:at + (h + 1) * n, 16:32, :] = sub.reshape(n, 16, 128)
        if h == 0:
            out_ref[...] = acc
        else:
            out_ref[...] = jnp.where(lane == h, acc, out_ref[...])
    gquery_ref[...] = out_ref[...] * scaling


def finish_kernel(
    mark_ref, b0, b1, b2, b3, b4, gown_ref, gquery_ref, total_ref, gqk_ref, gval_ref, gweight_ref
):
    length, width = gquery_ref.shape
    halves = length // 128
    rows = width * 2 // 16
    for a in range(halves):
        cols = slice(a * 128, (a + 1) * 128)
        acc = gown_ref[:, cols]
        for b in (b0, b1, b2, b3, b4):
            acc = acc + b[:, cols].astype(F32)
        for g in range(NGLOB):
            at = (g * halves + a) * rows
            term = total_ref[at:at + rows, 16:32, :].reshape(2 * width, 128).astype(F32)
            acc = acc + term * mark_ref[g]
        tokens = slice(a * 128, (a + 1) * 128)
        gqk_ref[tokens, :] = (gquery_ref[tokens, :] + acc[:width].T).astype(BF16)
        gval_ref[tokens, :] = acc[width:].T.astype(BF16)
    n = width // 16
    for c in range(gweight_ref.shape[1] // 128):
        piece = total_ref[c * n:(c + 1) * n, 0:16, :].reshape(width, 128)
        gweight_ref[:, c * 128:(c + 1) * 128] = piece.astype(F32)


def vmem(count):
    return [pl.BlockSpec(memory_space=pltpu.VMEM)] * count


def smem():
    return pl.BlockSpec(memory_space=pltpu.SMEM)


def local(qk_vectors, token_values, grad_output, out_weight, global_ids, pair_active):
    length, width = qk_vectors.shape
    devices = lax.axis_size(CTX)
    pieces = lax.axis_size(HEAD)
    position = lax.axis_index(CTX)
    joined = jnp.concatenate([qk_vectors, token_values], axis=0)

    step = 2 * length // devices
    slices = lax.all_to_all(joined.reshape(devices, step, width), CTX, 0, 0)
    routes = [[(i, i ^ 1) for i in range(devices)]]
    other = [i + 1 if i % 2 else i - 1 for i in range(devices)]
    routes.append([(i, j) for i, j in enumerate(other) if 0 <= j < devices])
    routes += [[(i, i ^ (1 << k)) for i in range(devices)] for k in range(1, ROUNDS)]
    received = [lax.ppermute(joined, CTX, route) for route in routes]

    picked = jnp.stack(
        [lax.dynamic_index_in_dim(slices, global_ids[g], keepdims=False) for g in range(NGLOB)]
    )
    spread = lax.all_to_all(
        jnp.broadcast_to(picked[None], (devices, NGLOB, step, width)), CTX, 0, 0
    )
    globals_all = jnp.swapaxes(spread, 0, 1).reshape(NGLOB, 2 * length, width)
    portion = lax.all_gather(grad_output, HEAD, axis=0)

    linked = []
    for k in range(ROUNDS):
        stride = 1 << k
        lowest = jnp.bitwise_and(position, devices - 1 - stride)
        slot = jnp.right_shift(lowest, k + 1) * stride + jnp.bitwise_and(lowest, stride - 1)
        linked.append(lax.dynamic_index_in_dim(pair_active[k], slot, keepdims=False) == 1)
    inside = jnp.logical_and(position > 0, position < devices - 1)
    bias = jnp.stack(
        [jnp.float32(0.0), jnp.where(linked[0], 1.0, 0.0)]
        + [jnp.where(m, 0.0, MASKED) for m in [inside] + linked[1:]]
        + [jnp.float32(0.0)] * NGLOB
    ).astype(F32)

    count = ROUNDS + 2 + NGLOB
    block = jax.ShapeDtypeStruct((2 * width, length), BF16)
    outputs = pl.pallas_call(
        attention_kernel,
        out_shape=(
            jax.ShapeDtypeStruct((pieces, length, 128), F32),
            jax.ShapeDtypeStruct((devices, 32, 128), BF16),
            block, block, block, block, block,
            jax.ShapeDtypeStruct((length, width), F32),
            jax.ShapeDtypeStruct((2 * width, length), F32),
        ),
        in_specs=[smem()] + vmem(9),
        out_specs=tuple(vmem(9)),
        scratch_shapes=[
            pltpu.VMEM((width // HD, length, count * length), F32),
            pltpu.VMEM((length, width), F32),
        ],
        compiler_params=pltpu.CompilerParams(vmem_limit_bytes=40 * 1024 * 1024),
        cost_estimate=pl.CostEstimate(
            flops=4_000_000_000, bytes_accessed=4_000_000, transcendentals=1_100_000
        ),
        name="attention",
    )(bias, joined, *received, globals_all, portion, out_weight)
    partial, sums, gquery, gown = outputs[0], outputs[1], outputs[7], outputs[8]
    returned = [
        lax.ppermute(o, CTX, [(j, i) for i, j in route])
        for o, route in zip(outputs[2:7], routes)
    ]
    projected = lax.psum_scatter(partial, HEAD, scatter_dimension=0, tiled=False).astype(BF16)

    shares = lax.all_to_all(sums, CTX, 0, 0)
    share = jnp.sum(shares.astype(F32), axis=0).astype(BF16)
    totals = lax.all_to_all(jnp.broadcast_to(share[None], shares.shape), CTX, 0, 0)

    marks = (global_ids == position).astype(F32)
    gqk, gval, gweight = pl.pallas_call(
        finish_kernel,
        out_shape=(
            jax.ShapeDtypeStruct((length, width), BF16),
            jax.ShapeDtypeStruct((length, width), BF16),
            jax.ShapeDtypeStruct((width, pieces * 128), F32),
        ),
        in_specs=[smem()] + vmem(8),
        out_specs=tuple(vmem(3)),
        compiler_params=pltpu.CompilerParams(vmem_limit_bytes=16 * 1024 * 1024),
        cost_estimate=pl.CostEstimate(
            flops=2_000_000, bytes_accessed=2_500_000, transcendentals=0
        ),
        name="finish",
    )(marks, *returned, gown, gquery, totals)
    return (projected, gqk, gval, gweight)


def solution(mesh):
    ctx, head = mesh.devices.shape
    cores = 2 if head % 2 == 0 else 1
    inner = Mesh(mesh.devices.reshape(ctx // 4, 4, head // cores, cores), CTX + HEAD)
    row = P(CTX, HEAD)
    return jax.shard_map(
        local,
        mesh=inner,
        in_specs=(row, row, row, P(HEAD, None), P(), P()),
        out_specs=(row, row, row, P(HEAD, None)),
        check_vma=False,
    )
```

```python
import functools
import math

import jax
import jax.numpy as jnp
from jax import lax
from jax.experimental import pallas as pl
from jax.experimental.pallas import tpu as pltpu
from jax.sharding import Mesh, PartitionSpec as P

HD = 64
NGLOB = 2
ROUNDS = 4
CTX = ("z", "x")
HEAD = ("y", "core")
NT = (((1,), (1,)), ((), ()))
TN = (((0,), (0,)), ((), ()))
NN = (((1,), (0,)), ((), ()))
F32 = jnp.float32
BF16 = jnp.bfloat16
MASKED = -1e30


def dot(a, b, dims):
    return lax.dot_general(a, b, dims, preferred_element_type=F32)


def block_bias(pos_ref, pair_ref):
    position = pos_ref[0]
    devices = 2 * pair_ref.shape[1]
    linked = []
    for k in range(ROUNDS):
        stride = 1 << k
        lowest = jnp.bitwise_and(position, devices - 1 - stride)
        slot = jnp.right_shift(lowest, k + 1) * stride + jnp.bitwise_and(lowest, stride - 1)
        linked.append(pair_ref[k, slot] == 1)
    inside = jnp.logical_and(position > 0, position < devices - 1)
    zero = jnp.float32(0.0)
    bias = [zero, jnp.where(linked[0], jnp.float32(1.0), zero)]
    bias += [jnp.where(m, zero, jnp.float32(MASKED)) for m in [inside] + linked[1:]]
    return bias + [zero] * NGLOB


def forward_kernel(
    pos_ref, pair_ref, own_ref, p0, p1, p2, p3, p4, glob_ref, gout_ref, w_ref,
    partial_ref, sums_ref, stats_ref, gatt_ref, gquery_ref,
    score_ref, out_ref,
):
    length = own_ref.shape[0] // 2
    width = own_ref.shape[1]
    pieces = gout_ref.shape[0]
    nheads = width // HD
    scaling = 1.0 / math.sqrt(HD)
    base2 = scaling / math.log(2.0)
    bias = block_bias(pos_ref, pair_ref)
    keys = [r[:length] for r in (own_ref, p0, p1, p2, p3, p4)]
    vals = [r[length:] for r in (own_ref, p0, p1, p2, p3, p4)]
    for g in range(NGLOB):
        keys.append(glob_ref[g, :length])
        vals.append(glob_ref[g, length:])
    count = len(keys)
    query = own_ref[:length]
    lane = lax.broadcasted_iota(jnp.int32, (1, width), 1)
    head = lane // HD

    gatt = jnp.zeros((length, width), F32)
    for c in range(pieces):
        gatt = gatt + dot(gout_ref[c], w_ref[:, c * 128:(c + 1) * 128], NT)
    gatt_b = gatt.astype(BF16)
    gatt_ref[...] = gatt_b

    inverse = []
    stats = jnp.zeros((length, width), F32)
    for h in range(nheads):
        query_h = jnp.where(head == h, query, jnp.zeros_like(query))
        highest = jnp.full((length, 1), MASKED, F32)
        for b in range(count):
            s = dot(query_h, keys[b], NT) * base2 + bias[b]
            score_ref[h, :, b * length:(b + 1) * length] = s
            highest = jnp.maximum(highest, jnp.max(s, axis=1, keepdims=True))
        total = jnp.zeros((length, 1), F32)
        for b in range(count):
            e = jnp.exp2(score_ref[h, :, b * length:(b + 1) * length] - highest)
            score_ref[h, :, b * length:(b + 1) * length] = e
            total = total + jnp.sum(e, axis=1, keepdims=True)
        inv = 1.0 / total
        inverse.append(inv)
        stats = jnp.where(lane == h, highest + jnp.log2(total), stats)
        acc = jnp.zeros((length, width), F32)
        for b in range(count):
            e = score_ref[h, :, b * length:(b + 1) * length]
            acc = acc + dot((e * inv).astype(BF16), vals[b], NN)
        if h == 0:
            out_ref[...] = acc
        else:
            out_ref[...] = jnp.where(head == h, acc, out_ref[...])

    attended = out_ref[...]
    attended_b = attended.astype(BF16)
    for c in range(pieces):
        partial_ref[c] = dot(attended_b, w_ref[:, c * 128:(c + 1) * 128], NN)
        part = dot(attended_b, gout_ref[c], TN).astype(BF16)
        n = width // 16
        at = c * n % sums_ref.shape[0]
        sums_ref[at:at + n, c * n // sums_ref.shape[0], 0:16, :] = part.reshape(n, 16, 128)

    product = gatt_b.astype(F32) * attended
    query_t = query.astype(F32).T.astype(BF16)
    gatt_t = gatt_b.astype(F32).T.astype(BF16)
    for h in range(nheads):
        gatt_h = jnp.where(head == h, gatt_b, jnp.zeros_like(gatt_b))
        row_dot = jnp.sum(jnp.where(head == h, product, 0.0), axis=1, keepdims=True)
        stats = jnp.where(lane == nheads + h, row_dot, stats)
        inv = inverse[h]
        qt = query_t[h * HD:(h + 1) * HD]
        gt = gatt_t[h * HD:(h + 1) * HD]
        acc = jnp.zeros((length, width), F32)
        for g in range(NGLOB):
            b = count - NGLOB + g
            weights = score_ref[h, :, b * length:(b + 1) * length] * inv
            gw = dot(gatt_h, vals[b], NT)
            gs = (weights * (gw - row_dot)).astype(BF16)
            acc = acc + dot(gs, keys[b], NN)
            gk = dot(qt, gs, NN) * scaling
            gv = dot(gt, weights.astype(BF16), NN)
            n = HD // 16
            for a in range(length // 128):
                x = g * (length // 128) + a
                for at, term in ((h * n, gk), (width // 16 + h * n, gv)):
                    sub = term[:, a * 128:(a + 1) * 128].astype(BF16)
                    sums_ref[at:at + n, x, 16:32, :] = sub.reshape(n, 16, 128)
        if h == 0:
            out_ref[...] = acc
        else:
            out_ref[...] = jnp.where(head == h, acc, out_ref[...])
    stats_ref[...] = stats
    gquery_ref[...] = out_ref[...]


def backward_kernel(
    pos_ref, pair_ref, own_ref, p0, p1, p2, p3, p4, stats_ref, gatt_ref, gglob_ref,
    r0, r1, r2, r3, r4, gquery_ref, gown_ref,
):
    length = own_ref.shape[0] // 2
    width = own_ref.shape[1]
    nheads = width // HD
    scaling = 1.0 / math.sqrt(HD)
    base2 = scaling / math.log(2.0)
    bias = block_bias(pos_ref, pair_ref)
    query = own_ref[:length]
    gatt_b = gatt_ref[...]
    head = lax.broadcasted_iota(jnp.int32, (1, width), 1) // HD
    query_t = query.astype(F32).T.astype(BF16)
    gatt_t = gatt_b.astype(F32).T.astype(BF16)
    blocks = (own_ref, p0, p1, p2, p3, p4)
    outs = (gown_ref, r0, r1, r2, r3, r4)
    result = gglob_ref[...]
    for h in range(nheads):
        query_h = jnp.where(head == h, query, jnp.zeros_like(query))
        gatt_h = jnp.where(head == h, gatt_b, jnp.zeros_like(gatt_b))
        log_total = stats_ref[:, h:h + 1]
        row_dot = stats_ref[:, nheads + h:nheads + h + 1]
        qt = query_t[h * HD:(h + 1) * HD]
        gt = gatt_t[h * HD:(h + 1) * HD]
        acc = jnp.zeros((length, width), F32)
        for b in (1, 2, 3, 4, 5, 0):
            keys = blocks[b][:length]
            s = dot(query_h, keys, NT) * base2 + (bias[b] - log_total)
            weights = jnp.exp2(s)
            gw = dot(gatt_h, blocks[b][length:], NT)
            gs = (weights * (gw - row_dot)).astype(BF16)
            acc = acc + dot(gs, keys, NN)
            gk = dot(qt, gs, NN) * scaling
            gv = dot(gt, weights.astype(BF16), NN)
            o = outs[b]
            o[h * HD:(h + 1) * HD, :] = gk.astype(o.dtype)
            o[width + h * HD:width + (h + 1) * HD, :] = gv.astype(o.dtype)
        result = result + jnp.where(head == h, acc, 0.0)
    gquery_ref[...] = result * scaling


def finish_kernel(
    pos_ref, ids_ref, b0, b1, b2, b3, b4, gown_ref, gquery_ref, total_ref,
    gqk_ref, gval_ref, gweight_ref,
):
    length, width = gquery_ref.shape
    halves = length // 128
    rows = width * 2 // 16
    for a in range(halves):
        cols = slice(a * 128, (a + 1) * 128)
        acc = gown_ref[:, cols]
        for b in (b0, b1, b2, b3, b4):
            acc = acc + b[:, cols].astype(F32)
        for g in range(NGLOB):
            at = (g * halves + a) * rows
            term = total_ref[at:at + rows, 16:32, :].reshape(2 * width, 128).astype(F32)
            acc = acc + jnp.where(ids_ref[g] == pos_ref[0], term, 0.0)
        tokens = slice(a * 128, (a + 1) * 128)
        gqk_ref[tokens, :] = (gquery_ref[tokens, :] + acc[:width].T).astype(BF16)
        gval_ref[tokens, :] = acc[width:].T.astype(BF16)
    n = width // 16
    for c in range(gweight_ref.shape[1] // 128):
        piece = total_ref[c * n:(c + 1) * n, 0:16, :].reshape(width, 128)
        gweight_ref[:, c * 128:(c + 1) * 128] = piece.astype(F32)


def vmem(count):
    return [pl.BlockSpec(memory_space=pltpu.VMEM)] * count


def smem():
    return pl.BlockSpec(memory_space=pltpu.SMEM)


def local(qk_vectors, token_values, grad_output, out_weight, global_ids, pair_active):
    length, width = qk_vectors.shape
    devices = lax.axis_size(CTX)
    pieces = lax.axis_size(HEAD)
    position = lax.axis_index(CTX)
    joined = jnp.concatenate([qk_vectors, token_values], axis=0)

    step = 2 * length // devices
    slices = lax.all_to_all(joined.reshape(devices, step, width), CTX, 0, 0)
    routes = [[(i, i ^ 1) for i in range(devices)]]
    other = [i + 1 if i % 2 else i - 1 for i in range(devices)]
    routes.append([(i, j) for i, j in enumerate(other) if 0 <= j < devices])
    routes += [[(i, i ^ (1 << k)) for i in range(devices)] for k in range(1, ROUNDS)]
    received = [lax.ppermute(joined, CTX, route) for route in routes]

    slices, *received = lax.optimization_barrier((slices, *received))
    picked = jnp.stack(
        [lax.dynamic_index_in_dim(slices, global_ids[g], keepdims=False) for g in range(NGLOB)]
    )
    spread = lax.all_to_all(
        jnp.broadcast_to(picked[None], (devices, NGLOB, step, width)), CTX, 0, 0
    )
    globals_all = jnp.swapaxes(spread, 0, 1).reshape(NGLOB, 2 * length, width)
    portion = lax.all_gather(grad_output, HEAD, axis=0)

    count = ROUNDS + 2 + NGLOB
    nheads = width // HD
    block = jax.ShapeDtypeStruct((2 * width, length), BF16)
    square = jax.ShapeDtypeStruct((length, width), F32)
    partial, sums, stats, gatt, gglob = pl.pallas_call(
        forward_kernel,
        out_shape=(
            jax.ShapeDtypeStruct((pieces, length, 128), F32),
            jax.ShapeDtypeStruct((lax.axis_size("z"), lax.axis_size("x"), 32, 128), BF16),
            square,
            jax.ShapeDtypeStruct((length, width), BF16),
            square,
        ),
        in_specs=[smem()] * 2 + vmem(9),
        out_specs=tuple(vmem(5)),
        scratch_shapes=[
            pltpu.VMEM((nheads, length, count * length), F32),
            pltpu.VMEM((length, width), F32),
        ],
        compiler_params=pltpu.CompilerParams(vmem_limit_bytes=40 * 1024 * 1024),
        cost_estimate=pl.CostEstimate(
            flops=3_000_000_000, bytes_accessed=4_000_000, transcendentals=1_100_000
        ),
        name="forward",
    )(position[None], pair_active, joined, *received, globals_all, portion, out_weight)

    shares = lax.all_to_all(sums.reshape(devices, 32, 128), CTX, 0, 0)
    projected = lax.psum_scatter(partial, HEAD, scatter_dimension=0, tiled=False).astype(BF16)
    *terms, gquery, gown = pl.pallas_call(
        backward_kernel,
        out_shape=(
            block, block, block, block, block,
            square,
            jax.ShapeDtypeStruct((2 * width, length), F32),
        ),
        in_specs=[smem()] * 2 + vmem(9),
        out_specs=tuple(vmem(7)),
        compiler_params=pltpu.CompilerParams(vmem_limit_bytes=24 * 1024 * 1024),
        cost_estimate=pl.CostEstimate(
            flops=3_000_000_000, bytes_accessed=4_000_000, transcendentals=800_000
        ),
        name="backward",
    )(position[None], pair_active, joined, *received, stats, gatt, gglob)
    returned = [lax.ppermute(t, CTX, route) for t, route in zip(terms, routes)]

    shares, *returned = lax.optimization_barrier((shares, *returned))
    share = jnp.sum(shares.astype(F32), axis=0).astype(BF16)
    column = lax.all_to_all(
        jnp.broadcast_to(share[None], (lax.axis_size("z"),) + share.shape), "z", 0, 0
    )
    totals = lax.all_to_all(
        jnp.broadcast_to(column[None], (lax.axis_size("x"),) + column.shape), "x", 0, 0
    ).reshape(shares.shape)

    gqk, gval, gweight = pl.pallas_call(
        finish_kernel,
        out_shape=(
            jax.ShapeDtypeStruct((length, width), BF16),
            jax.ShapeDtypeStruct((length, width), BF16),
            jax.ShapeDtypeStruct((width, pieces * 128), F32),
        ),
        in_specs=[smem()] * 2 + vmem(8),
        out_specs=tuple(vmem(3)),
        compiler_params=pltpu.CompilerParams(vmem_limit_bytes=16 * 1024 * 1024),
        cost_estimate=pl.CostEstimate(
            flops=2_000_000, bytes_accessed=2_500_000, transcendentals=0
        ),
        name="finish",
    )(position[None], global_ids, *returned, gown, gquery, totals)
    return (projected, gqk, gval, gweight)


def solution(mesh):
    ctx, head = mesh.devices.shape
    cores = 2 if head % 2 == 0 else 1
    inner = Mesh(mesh.devices.reshape(ctx // 4, 4, head // cores, cores), CTX + HEAD)
    row = P(CTX, HEAD)
    return jax.shard_map(
        local,
        mesh=inner,
        in_specs=(row, row, row, P(HEAD, None), P(), P()),
        out_specs=(row, row, row, P(HEAD, None)),
        check_vma=False,
    )
```

```python
import functools
import math

import jax
import jax.numpy as jnp
from jax import lax
from jax.experimental import pallas as pl
from jax.experimental.pallas import tpu as pltpu
from jax.sharding import Mesh, PartitionSpec as P

HD = 64
NGLOB = 2
ROUNDS = 4
CTX = ("z", "x")
HEAD = ("y", "core")
NT = (((1,), (1,)), ((), ()))
TN = (((0,), (0,)), ((), ()))
NN = (((1,), (0,)), ((), ()))
F32 = jnp.float32
BF16 = jnp.bfloat16
MASKED = -1e30


def dot(a, b, dims):
    return lax.dot_general(a, b, dims, preferred_element_type=F32)


def block_bias(pos_ref, pair_ref):
    position = pos_ref[0]
    devices = 2 * pair_ref.shape[1]
    linked = []
    for k in range(ROUNDS):
        stride = 1 << k
        lowest = jnp.bitwise_and(position, devices - 1 - stride)
        slot = jnp.right_shift(lowest, k + 1) * stride + jnp.bitwise_and(lowest, stride - 1)
        linked.append(pair_ref[k, slot] == 1)
    inside = jnp.logical_and(position > 0, position < devices - 1)
    zero = jnp.float32(0.0)
    bias = [zero, jnp.where(linked[0], jnp.float32(1.0), zero)]
    bias += [jnp.where(m, zero, jnp.float32(MASKED)) for m in [inside] + linked[1:]]
    return bias + [zero] * NGLOB


def forward_kernel(
    pos_ref, pair_ref, own_ref, p0, p1, p2, p3, p4, glob_ref, gout_ref, w_ref,
    partial_ref, sums_ref, stats_ref, gatt_ref, gquery_ref,
    score_ref, out_ref,
):
    length = own_ref.shape[0] // 2
    width = own_ref.shape[1]
    pieces = gout_ref.shape[0]
    nheads = width // HD
    scaling = 1.0 / math.sqrt(HD)
    base2 = scaling / math.log(2.0)
    bias = block_bias(pos_ref, pair_ref)
    keys = [r[:length] for r in (own_ref, p0, p1, p2, p3, p4)]
    vals = [r[length:] for r in (own_ref, p0, p1, p2, p3, p4)]
    for g in range(NGLOB):
        keys.append(glob_ref[g, :length])
        vals.append(glob_ref[g, length:])
    count = len(keys)
    query = own_ref[:length]
    lane = lax.broadcasted_iota(jnp.int32, (1, width), 1)
    head = lane // HD

    gatt = jnp.zeros((length, width), F32)
    for c in range(pieces):
        gatt = gatt + dot(gout_ref[c], w_ref[:, c * 128:(c + 1) * 128], NT)
    gatt_b = gatt.astype(BF16)
    gatt_ref[...] = gatt_b

    inverse = []
    stats = jnp.zeros((length, width), F32)
    for h in range(nheads):
        query_h = jnp.where(head == h, query, jnp.zeros_like(query))
        highest = jnp.full((length, 1), MASKED, F32)
        for b in range(count):
            s = dot(query_h, keys[b], NT) * base2 + bias[b]
            score_ref[h, :, b * length:(b + 1) * length] = s
            highest = jnp.maximum(highest, jnp.max(s, axis=1, keepdims=True))
        total = jnp.zeros((length, 1), F32)
        for b in range(count):
            e = jnp.exp2(score_ref[h, :, b * length:(b + 1) * length] - highest)
            score_ref[h, :, b * length:(b + 1) * length] = e
            total = total + jnp.sum(e, axis=1, keepdims=True)
        inv = 1.0 / total
        inverse.append(inv)
        stats = jnp.where(lane == h, highest + jnp.log2(total), stats)
        acc = jnp.zeros((length, width), F32)
        for b in range(count):
            e = score_ref[h, :, b * length:(b + 1) * length]
            acc = acc + dot((e * inv).astype(BF16), vals[b], NN)
        if h == 0:
            out_ref[...] = acc
        else:
            out_ref[...] = jnp.where(head == h, acc, out_ref[...])

    attended = out_ref[...]
    attended_b = attended.astype(BF16)
    for c in range(pieces):
        partial_ref[c] = dot(attended_b, w_ref[:, c * 128:(c + 1) * 128], NN)
        part = dot(attended_b, gout_ref[c], TN).astype(BF16)
        n = width // 16
        sums_ref[c * n:(c + 1) * n, 0:16, :] = part.reshape(n, 16, 128)

    product = gatt_b.astype(F32) * attended
    query_t = query.astype(F32).T.astype(BF16)
    gatt_t = gatt_b.astype(F32).T.astype(BF16)
    for h in range(nheads):
        gatt_h = jnp.where(head == h, gatt_b, jnp.zeros_like(gatt_b))
        row_dot = jnp.sum(jnp.where(head == h, product, 0.0), axis=1, keepdims=True)
        stats = jnp.where(lane == nheads + h, row_dot, stats)
        inv = inverse[h]
        qt = query_t[h * HD:(h + 1) * HD]
        gt = gatt_t[h * HD:(h + 1) * HD]
        acc = jnp.zeros((length, width), F32)
        for g in range(NGLOB):
            b = count - NGLOB + g
            weights = score_ref[h, :, b * length:(b + 1) * length] * inv
            gw = dot(gatt_h, vals[b], NT)
            gs = (weights * (gw - row_dot)).astype(BF16)
            acc = acc + dot(gs, keys[b], NN)
            gk = dot(qt, gs, NN) * scaling
            gv = dot(gt, weights.astype(BF16), NN)
            n = HD // 16
            for a in range(length // 128):
                start = (g * (length // 128) + a) * 2 * width // 16
                for at, term in ((start + h * n, gk), (start + width // 16 + h * n, gv)):
                    sub = term[:, a * 128:(a + 1) * 128].astype(BF16)
                    sums_ref[at:at + n, 16:32, :] = sub.reshape(n, 16, 128)
        if h == 0:
            out_ref[...] = acc
        else:
            out_ref[...] = jnp.where(head == h, acc, out_ref[...])
    stats_ref[...] = stats
    gquery_ref[...] = out_ref[...]


def backward_kernel(
    pos_ref, pair_ref, own_ref, p0, p1, p2, p3, p4, stats_ref, gatt_ref, gglob_ref,
    r0, r1, r2, r3, r4, gquery_ref, gown_ref,
):
    length = own_ref.shape[0] // 2
    width = own_ref.shape[1]
    nheads = width // HD
    scaling = 1.0 / math.sqrt(HD)
    base2 = scaling / math.log(2.0)
    bias = block_bias(pos_ref, pair_ref)
    query = own_ref[:length]
    gatt_b = gatt_ref[...]
    head = lax.broadcasted_iota(jnp.int32, (1, width), 1) // HD
    query_t = query.astype(F32).T.astype(BF16)
    gatt_t = gatt_b.astype(F32).T.astype(BF16)
    blocks = (own_ref, p0, p1, p2, p3, p4)
    outs = (gown_ref, r0, r1, r2, r3, r4)
    result = gglob_ref[...]
    for h in range(nheads):
        query_h = jnp.where(head == h, query, jnp.zeros_like(query))
        gatt_h = jnp.where(head == h, gatt_b, jnp.zeros_like(gatt_b))
        log_total = stats_ref[:, h:h + 1]
        row_dot = stats_ref[:, nheads + h:nheads + h + 1]
        qt = query_t[h * HD:(h + 1) * HD]
        gt = gatt_t[h * HD:(h + 1) * HD]
        acc = jnp.zeros((length, width), F32)
        for b in (1, 2, 3, 4, 5, 0):
            keys = blocks[b][:length]
            s = dot(query_h, keys, NT) * base2 + (bias[b] - log_total)
            weights = jnp.exp2(s)
            gw = dot(gatt_h, blocks[b][length:], NT)
            gs = (weights * (gw - row_dot)).astype(BF16)
            acc = acc + dot(gs, keys, NN)
            gk = dot(qt, gs, NN) * scaling
            gv = dot(gt, weights.astype(BF16), NN)
            o = outs[b]
            o[h * HD:(h + 1) * HD, :] = gk.astype(o.dtype)
            o[width + h * HD:width + (h + 1) * HD, :] = gv.astype(o.dtype)
        result = result + jnp.where(head == h, acc, 0.0)
    gquery_ref[...] = result * scaling


def finish_kernel(
    pos_ref, ids_ref, b0, b1, b2, b3, b4, gown_ref, gquery_ref, total_ref,
    gqk_ref, gval_ref, gweight_ref,
):
    length, width = gquery_ref.shape
    halves = length // 128
    rows = width * 2 // 16
    for a in range(halves):
        cols = slice(a * 128, (a + 1) * 128)
        acc = gown_ref[:, cols]
        for b in (b0, b1, b2, b3, b4):
            acc = acc + b[:, cols].astype(F32)
        for g in range(NGLOB):
            at = (g * halves + a) * rows
            term = total_ref[at:at + rows, 16:32, :].reshape(2 * width, 128).astype(F32)
            acc = acc + jnp.where(ids_ref[g] == pos_ref[0], term, 0.0)
        tokens = slice(a * 128, (a + 1) * 128)
        gqk_ref[tokens, :] = (gquery_ref[tokens, :] + acc[:width].T).astype(BF16)
        gval_ref[tokens, :] = acc[width:].T.astype(BF16)
    n = width // 16
    for c in range(gweight_ref.shape[1] // 128):
        piece = total_ref[c * n:(c + 1) * n, 0:16, :].reshape(width, 128)
        gweight_ref[:, c * 128:(c + 1) * 128] = piece.astype(F32)


def pack_kernel(qk_ref, val_ref, joined_ref, chunks_ref):
    length = qk_ref.shape[0]
    for n, ref in enumerate((qk_ref, val_ref)):
        rows = ref[...]
        joined_ref[n * length:(n + 1) * length, :] = rows
        pieces = rows.reshape(chunks_ref.shape[0], 16, rows.shape[1])
        for g in range(NGLOB):
            chunks_ref[:, g * 2 + n] = pieces


def pick_kernel(pos_ref, ids_ref, slices_ref, out_ref):
    chosen = slices_ref[ids_ref[pos_ref[0] % 4 // 2]]
    for z in range(out_ref.shape[0]):
        out_ref[z] = chosen


def vmem(count):
    return [pl.BlockSpec(memory_space=pltpu.VMEM)] * count


def smem():
    return pl.BlockSpec(memory_space=pltpu.SMEM)


def local(qk_vectors, token_values, grad_output, out_weight, global_ids, pair_active):
    length, width = qk_vectors.shape
    devices = lax.axis_size(CTX)
    pieces = lax.axis_size(HEAD)
    position = lax.axis_index(CTX)
    joined = jnp.concatenate([qk_vectors, token_values], axis=0)

    zs, xs = lax.axis_size("z"), lax.axis_size("x")
    joined, chunks = pl.pallas_call(
        pack_kernel,
        out_shape=(
            jax.ShapeDtypeStruct((2 * length, width), BF16),
            jax.ShapeDtypeStruct((zs, xs, 16, width), BF16),
        ),
        in_specs=vmem(2),
        out_specs=tuple(vmem(2)),
        name="pack",
    )(qk_vectors, token_values)

    slices = lax.all_to_all(chunks.reshape(devices, 16, width), CTX, 0, 0)
    routes = [[(i, i ^ 1) for i in range(devices)]]
    other = [i + 1 if i % 2 else i - 1 for i in range(devices)]
    routes.append([(i, j) for i, j in enumerate(other) if 0 <= j < devices])
    routes += [[(i, i ^ (1 << k)) for i in range(devices)] for k in range(1, ROUNDS)]
    received = [None] * len(routes)
    for n in (4, 3, 2, 1):
        received[n] = lax.ppermute(joined, CTX, routes[n])
    slices, *received[1:] = lax.optimization_barrier((slices, *received[1:]))
    picked = pl.pallas_call(
        pick_kernel,
        out_shape=jax.ShapeDtypeStruct((zs, 16, width), BF16),
        in_specs=[smem()] * 2 + vmem(1),
        out_specs=vmem(1)[0],
        name="pick",
    )(position[None], global_ids, slices)
    picked, cotangent = lax.optimization_barrier((picked, grad_output))
    column = lax.all_to_all(picked, "z", 0, 0)
    portion = lax.all_gather(cotangent, HEAD, axis=0)
    column, portion, joined_late = lax.optimization_barrier((column, portion, joined))
    received[0] = lax.ppermute(joined_late, CTX, routes[0])
    globals_all = lax.all_to_all(
        jnp.broadcast_to(column[None], (xs,) + column.shape), "x", 0, 0
    ).reshape(NGLOB, 2 * length, width)

    count = ROUNDS + 2 + NGLOB
    nheads = width // HD
    block = jax.ShapeDtypeStruct((2 * width, length), BF16)
    square = jax.ShapeDtypeStruct((length, width), F32)
    partial, sums, stats, gatt, gglob = pl.pallas_call(
        forward_kernel,
        out_shape=(
            jax.ShapeDtypeStruct((pieces, length, 128), F32),
            jax.ShapeDtypeStruct((devices, 32, 128), BF16),
            square,
            jax.ShapeDtypeStruct((length, width), BF16),
            square,
        ),
        in_specs=[smem()] * 2 + vmem(9),
        out_specs=tuple(vmem(5)),
        scratch_shapes=[
            pltpu.VMEM((nheads, length, count * length), F32),
            pltpu.VMEM((length, width), F32),
        ],
        compiler_params=pltpu.CompilerParams(vmem_limit_bytes=40 * 1024 * 1024),
        cost_estimate=pl.CostEstimate(
            flops=3_000_000_000, bytes_accessed=4_000_000, transcendentals=1_100_000
        ),
        name="forward",
    )(position[None], pair_active, joined, *received, globals_all, portion, out_weight)

    row = lax.all_to_all(sums.reshape(xs, zs, 32, 128), "x", 0, 0)
    projected = lax.psum_scatter(partial, HEAD, scatter_dimension=0, tiled=False).astype(BF16)
    *terms, gquery, gown = pl.pallas_call(
        backward_kernel,
        out_shape=(
            block, block, block, block, block,
            square,
            jax.ShapeDtypeStruct((2 * width, length), F32),
        ),
        in_specs=[smem()] * 2 + vmem(9),
        out_specs=tuple(vmem(7)),
        compiler_params=pltpu.CompilerParams(vmem_limit_bytes=24 * 1024 * 1024),
        cost_estimate=pl.CostEstimate(
            flops=3_000_000_000, bytes_accessed=4_000_000, transcendentals=800_000
        ),
        name="backward",
    )(position[None], pair_active, joined, *received, stats, gatt, gglob)
    row, *terms = lax.optimization_barrier((row, *terms))
    returned = [lax.ppermute(t, CTX, route) for t, route in zip(terms, routes)]

    row = jnp.sum(row.astype(F32), axis=0).astype(BF16)
    shares = lax.all_to_all(row, "z", 0, 0)
    shares, returned[0], returned[2] = lax.optimization_barrier((shares, returned[0], returned[2]))
    share = jnp.sum(shares.astype(F32), axis=0).astype(BF16)
    column = lax.all_to_all(jnp.broadcast_to(share[None], (zs,) + share.shape), "z", 0, 0)
    column, returned[1], returned[3] = lax.optimization_barrier((column, returned[1], returned[3]))
    totals = lax.all_to_all(
        jnp.broadcast_to(column[None], (xs,) + column.shape), "x", 0, 0
    ).reshape(devices, 32, 128)

    gqk, gval, gweight = pl.pallas_call(
        finish_kernel,
        out_shape=(
            jax.ShapeDtypeStruct((length, width), BF16),
            jax.ShapeDtypeStruct((length, width), BF16),
            jax.ShapeDtypeStruct((width, pieces * 128), F32),
        ),
        in_specs=[smem()] * 2 + vmem(8),
        out_specs=tuple(vmem(3)),
        compiler_params=pltpu.CompilerParams(vmem_limit_bytes=16 * 1024 * 1024),
        cost_estimate=pl.CostEstimate(
            flops=2_000_000, bytes_accessed=2_500_000, transcendentals=0
        ),
        name="finish",
    )(position[None], global_ids, *returned, gown, gquery, totals)
    return (projected, gqk, gval, gweight)


def solution(mesh):
    ctx, head = mesh.devices.shape
    cores = 2 if head % 2 == 0 else 1
    inner = Mesh(mesh.devices.reshape(ctx // 4, 4, head // cores, cores), CTX + HEAD)
    row = P(CTX, HEAD)
    return jax.shard_map(
        local,
        mesh=inner,
        in_specs=(row, row, row, P(HEAD, None), P(), P()),
        out_specs=(row, row, row, P(HEAD, None)),
        check_vma=False,
    )
```

```python
import functools
import math

import jax
import jax.numpy as jnp
from jax import lax
from jax.experimental import pallas as pl
from jax.experimental.pallas import tpu as pltpu
from jax.sharding import Mesh, PartitionSpec as P

HD = 64
NGLOB = 2
ROUNDS = 4
CTX = ("z", "x")
HEAD = ("y", "core")
NT = (((1,), (1,)), ((), ()))
TN = (((0,), (0,)), ((), ()))
NN = (((1,), (0,)), ((), ()))
F32 = jnp.float32
BF16 = jnp.bfloat16
MASKED = -1e30


def dot(a, b, dims):
    return lax.dot_general(a, b, dims, preferred_element_type=F32)


def block_bias(pos_ref, pair_ref):
    position = pos_ref[0]
    devices = 2 * pair_ref.shape[1]
    linked = []
    for k in range(ROUNDS):
        stride = 1 << k
        lowest = jnp.bitwise_and(position, devices - 1 - stride)
        slot = jnp.right_shift(lowest, k + 1) * stride + jnp.bitwise_and(lowest, stride - 1)
        linked.append(pair_ref[k, slot] == 1)
    inside = jnp.logical_and(position > 0, position < devices - 1)
    zero = jnp.float32(0.0)
    bias = [zero, jnp.where(linked[0], jnp.float32(1.0), zero)]
    bias += [jnp.where(m, zero, jnp.float32(MASKED)) for m in [inside] + linked[1:]]
    return bias + [zero] * NGLOB


def cotangent_kernel(gout_ref, w_ref, out_ref, gatt_ref):
    pieces, length, width = gout_ref.shape
    gatt = jnp.zeros((length, width), F32)
    for c in range(pieces):
        part = gout_ref[c].astype(BF16)
        out_ref[c] = part
        gatt = gatt + dot(part, w_ref[:, c * width:(c + 1) * width], NT)
    gatt_ref[...] = gatt.astype(BF16)


def forward_kernel(
    pos_ref, pair_ref, own_ref, p0, p1, p2, p3, p4, glob_ref, gout_ref, gatt_ref,
    att_ref, sums_ref, stats_ref, gquery_ref,
    score_ref, out_ref,
):
    length = own_ref.shape[0] // 2
    width = own_ref.shape[1]
    pieces = gout_ref.shape[0]
    nheads = width // HD
    scaling = 1.0 / math.sqrt(HD)
    base2 = scaling / math.log(2.0)
    bias = block_bias(pos_ref, pair_ref)
    keys = [r[:length] for r in (own_ref, p0, p1, p2, p3, p4)]
    vals = [r[length:] for r in (own_ref, p0, p1, p2, p3, p4)]
    half = glob_ref.shape[0] // 2
    for g in range(NGLOB):
        keys.append(jnp.concatenate([glob_ref[x, g] for x in range(half)], axis=0))
        vals.append(jnp.concatenate([glob_ref[half + x, g] for x in range(half)], axis=0))
    count = len(keys)
    query = own_ref[:length]
    lane = lax.broadcasted_iota(jnp.int32, (1, width), 1)
    head = lane // HD
    gatt_b = gatt_ref[...]

    inverse = []
    stats = jnp.zeros((length, width), F32)
    for h in range(nheads):
        query_h = jnp.where(head == h, query, jnp.zeros_like(query))
        highest = jnp.full((length, 1), MASKED, F32)
        for b in range(count):
            s = dot(query_h, keys[b], NT) * base2 + bias[b]
            score_ref[h, :, b * length:(b + 1) * length] = s
            highest = jnp.maximum(highest, jnp.max(s, axis=1, keepdims=True))
        total = jnp.zeros((length, 1), F32)
        for b in range(count):
            e = jnp.exp2(score_ref[h, :, b * length:(b + 1) * length] - highest)
            score_ref[h, :, b * length:(b + 1) * length] = e
            total = total + jnp.sum(e, axis=1, keepdims=True)
        inv = 1.0 / total
        inverse.append(inv)
        stats = jnp.where(lane == h, highest + jnp.log2(total), stats)
        acc = jnp.zeros((length, width), F32)
        for b in range(count):
            e = score_ref[h, :, b * length:(b + 1) * length]
            acc = acc + dot((e * inv).astype(BF16), vals[b], NN)
        if h == 0:
            out_ref[...] = acc
        else:
            out_ref[...] = jnp.where(head == h, acc, out_ref[...])

    attended = out_ref[...]
    att_ref[...] = attended
    attended_b = attended.astype(BF16)
    for c in range(pieces):
        part = dot(attended_b, gout_ref[c], TN).astype(BF16)
        n = width // 16
        at = c * n % sums_ref.shape[0]
        sums_ref[at:at + n, c * n // sums_ref.shape[0], 0:16, :] = part.reshape(n, 16, 128)

    product = gatt_b.astype(F32) * attended
    query_t = query.astype(F32).T.astype(BF16)
    gatt_t = gatt_b.astype(F32).T.astype(BF16)
    for h in range(nheads):
        gatt_h = jnp.where(head == h, gatt_b, jnp.zeros_like(gatt_b))
        row_dot = jnp.sum(jnp.where(head == h, product, 0.0), axis=1, keepdims=True)
        stats = jnp.where(lane == nheads + h, row_dot, stats)
        inv = inverse[h]
        qt = query_t[h * HD:(h + 1) * HD]
        gt = gatt_t[h * HD:(h + 1) * HD]
        acc = jnp.zeros((length, width), F32)
        for g in range(NGLOB):
            b = count - NGLOB + g
            weights = score_ref[h, :, b * length:(b + 1) * length] * inv
            gw = dot(gatt_h, vals[b], NT)
            gs = (weights * (gw - row_dot)).astype(BF16)
            acc = acc + dot(gs, keys[b], NN)
            gk = dot(qt, gs, NN) * scaling
            gv = dot(gt, weights.astype(BF16), NN)
            n = HD // 16
            for a in range(length // 128):
                x = g * (length // 128) + a
                for at, term in ((h * n, gk), (width // 16 + h * n, gv)):
                    sub = term[:, a * 128:(a + 1) * 128].astype(BF16)
                    sums_ref[at:at + n, x, 16:32, :] = sub.reshape(n, 16, 128)
        if h == 0:
            out_ref[...] = acc
        else:
            out_ref[...] = jnp.where(head == h, acc, out_ref[...])
    stats_ref[...] = stats
    gquery_ref[...] = out_ref[...]


def backward_kernel(
    pos_ref, pair_ref, own_ref, p0, p1, p2, p3, p4, stats_ref, gatt_ref, gglob_ref,
    r0, r1, r2, r3, r4, gquery_ref, gown_ref,
):
    length = own_ref.shape[0] // 2
    width = own_ref.shape[1]
    nheads = width // HD
    scaling = 1.0 / math.sqrt(HD)
    base2 = scaling / math.log(2.0)
    bias = block_bias(pos_ref, pair_ref)
    query = own_ref[:length]
    gatt_b = gatt_ref[...]
    head = lax.broadcasted_iota(jnp.int32, (1, width), 1) // HD
    query_t = query.astype(F32).T.astype(BF16)
    gatt_t = gatt_b.astype(F32).T.astype(BF16)
    blocks = (own_ref, p0, p1, p2, p3, p4)
    outs = (gown_ref, r0, r1, r2, r3, r4)
    result = gglob_ref[...]
    for h in range(nheads):
        query_h = jnp.where(head == h, query, jnp.zeros_like(query))
        gatt_h = jnp.where(head == h, gatt_b, jnp.zeros_like(gatt_b))
        log_total = stats_ref[:, h:h + 1]
        row_dot = stats_ref[:, nheads + h:nheads + h + 1]
        qt = query_t[h * HD:(h + 1) * HD]
        gt = gatt_t[h * HD:(h + 1) * HD]
        acc = jnp.zeros((length, width), F32)
        for b in (1, 2, 3, 4, 5, 0):
            keys = blocks[b][:length]
            s = dot(query_h, keys, NT) * base2 + (bias[b] - log_total)
            weights = jnp.exp2(s)
            gw = dot(gatt_h, blocks[b][length:], NT)
            gs = (weights * (gw - row_dot)).astype(BF16)
            acc = acc + dot(gs, keys, NN)
            gk = dot(qt, gs, NN) * scaling
            gv = dot(gt, weights.astype(BF16), NN)
            o = outs[b]
            o[h * HD:(h + 1) * HD, :] = gk.astype(o.dtype)
            o[width + h * HD:width + (h + 1) * HD, :] = gv.astype(o.dtype)
        result = result + jnp.where(head == h, acc, 0.0)
    gquery_ref[...] = result * scaling


def project_kernel(att_ref, w_ref, projected_ref):
    projected = jnp.zeros(projected_ref.shape, F32)
    for c in range(att_ref.shape[0]):
        projected = projected + dot(att_ref[c].astype(BF16), w_ref[c], NN)
    projected_ref[...] = projected.astype(BF16)


def finish_kernel(
    pos_ref, ids_ref, b0, b1, b2, b3, b4, gown_ref, gquery_ref, total_ref,
    gqk_ref, gval_ref, gweight_ref,
):
    length, width = gquery_ref.shape
    halves = length // 128
    rows = width * 2 // 16
    for a in range(halves):
        cols = slice(a * 128, (a + 1) * 128)
        acc = gown_ref[:, cols]
        for b in (b0, b1, b2, b3, b4):
            acc = acc + b[:, cols].astype(F32)
        for g in range(NGLOB):
            at = (g * halves + a) * rows
            term = total_ref[at:at + rows, 16:32, :].reshape(2 * width, 128).astype(F32)
            acc = acc + jnp.where(ids_ref[g] == pos_ref[0], term, 0.0)
        tokens = slice(a * 128, (a + 1) * 128)
        gqk_ref[tokens, :] = (gquery_ref[tokens, :] + acc[:width].T).astype(BF16)
        gval_ref[tokens, :] = acc[width:].T.astype(BF16)
    n = width // 16
    for c in range(gweight_ref.shape[1] // 128):
        piece = total_ref[c * n:(c + 1) * n, 0:16, :].reshape(width, 128)
        gweight_ref[:, c * 128:(c + 1) * 128] = piece.astype(F32)


def pack_kernel(qk_ref, val_ref, gout_ref, joined_ref, chunks_ref, wide_ref):
    length, width = qk_ref.shape
    zs, xs, step, _ = chunks_ref.shape
    joined_ref[:length] = qk_ref[...]
    joined_ref[length:] = val_ref[...]
    half = xs // 2
    for x in range(xs):
        ref = (qk_ref, val_ref)[x // half]
        rows = ref[x % half * zs * step:(x % half + 1) * zs * step, :]
        chunks_ref[:, x] = rows.reshape(zs, step, width)
    wide_ref[...] = gout_ref[...].astype(F32)


def pick_kernel(ids_ref, slices_ref, out_ref):
    step = slices_ref.shape[1]
    for g in range(NGLOB):
        chosen = slices_ref[ids_ref[g]]
        for z in range(out_ref.shape[0]):
            out_ref[z, g * step:(g + 1) * step] = chosen


def vmem(count):
    return [pl.BlockSpec(memory_space=pltpu.VMEM)] * count


def smem():
    return pl.BlockSpec(memory_space=pltpu.SMEM)


def local(qk_vectors, token_values, grad_output, out_weight, global_ids, pair_active):
    length, width = qk_vectors.shape
    devices = lax.axis_size(CTX)
    pieces = lax.axis_size(HEAD)
    position = lax.axis_index(CTX)
    joined = jnp.concatenate([qk_vectors, token_values], axis=0)

    zs, xs = lax.axis_size("z"), lax.axis_size("x")
    step = 2 * length // devices
    joined, chunks, wide = pl.pallas_call(
        pack_kernel,
        out_shape=(
            jax.ShapeDtypeStruct((2 * length, width), BF16),
            jax.ShapeDtypeStruct((zs, xs, step, width), BF16),
            jax.ShapeDtypeStruct((length, width), F32),
        ),
        in_specs=vmem(3),
        out_specs=tuple(vmem(3)),
        name="pack",
    )(qk_vectors, token_values, grad_output)

    slices = lax.all_to_all(chunks.reshape(devices, step, width), CTX, 0, 0)
    portion = lax.all_gather(wide, HEAD, axis=0)
    weight_all = lax.all_gather(out_weight, HEAD, axis=0)
    routes = [[(i, i ^ 1) for i in range(devices)]]
    other = [i + 1 if i % 2 else i - 1 for i in range(devices)]
    routes.append([(i, j) for i, j in enumerate(other) if 0 <= j < devices])
    routes += [[(i, i ^ (1 << k)) for i in range(devices)] for k in range(1, ROUNDS)]
    received = [None] * len(routes)
    for n in (4, 3, 2, 1):
        received[n] = lax.ppermute(joined, CTX, routes[n])
    slices, *received[1:] = lax.optimization_barrier((slices, *received[1:]))
    picked = pl.pallas_call(
        pick_kernel,
        out_shape=jax.ShapeDtypeStruct((zs, NGLOB * step, width), BF16),
        in_specs=[smem()] + vmem(1),
        out_specs=vmem(1)[0],
        name="pick",
    )(global_ids, slices)
    picked, joined_late, portion = lax.optimization_barrier((picked, joined, portion))
    column = lax.all_to_all(picked, "z", 0, 0)
    received[0] = lax.ppermute(joined_late, CTX, routes[0])
    portion_b, gatt = pl.pallas_call(
        cotangent_kernel,
        out_shape=(
            jax.ShapeDtypeStruct((pieces, length, width), BF16),
            jax.ShapeDtypeStruct((length, width), BF16),
        ),
        in_specs=vmem(2),
        out_specs=tuple(vmem(2)),
        compiler_params=pltpu.CompilerParams(vmem_limit_bytes=16 * 1024 * 1024),
        cost_estimate=pl.CostEstimate(
            flops=600_000_000, bytes_accessed=2_000_000, transcendentals=0
        ),
        name="cotangent",
    )(portion, out_weight)
    column, portion_b, gatt = lax.optimization_barrier((column, portion_b, gatt))
    column = jnp.swapaxes(column.reshape(zs, NGLOB, step, width), 0, 1)
    column = column.reshape(NGLOB, zs * step, width)
    globals_all = lax.all_to_all(
        jnp.broadcast_to(column[None], (xs,) + column.shape), "x", 0, 0
    )
    count = ROUNDS + 2 + NGLOB
    nheads = width // HD
    block = jax.ShapeDtypeStruct((2 * width, length), BF16)
    square = jax.ShapeDtypeStruct((length, width), F32)
    attended, sums, stats, gglob = pl.pallas_call(
        forward_kernel,
        out_shape=(
            square,
            jax.ShapeDtypeStruct((zs, xs, 32, 128), BF16),
            square,
            square,
        ),
        in_specs=[smem()] * 2 + vmem(9),
        out_specs=tuple(vmem(4)),
        scratch_shapes=[
            pltpu.VMEM((nheads, length, count * length), F32),
            pltpu.VMEM((length, width), F32),
        ],
        compiler_params=pltpu.CompilerParams(vmem_limit_bytes=40 * 1024 * 1024),
        cost_estimate=pl.CostEstimate(
            flops=3_000_000_000, bytes_accessed=4_000_000, transcendentals=1_100_000
        ),
        name="forward",
    )(position[None], pair_active, joined, *received, globals_all, portion_b, gatt)

    shares = lax.all_to_all(sums.reshape(devices, 32, 128), CTX, 0, 0)
    attended_all = lax.all_gather(attended, HEAD, axis=0)
    *terms, gquery, gown = pl.pallas_call(
        backward_kernel,
        out_shape=(
            block, block, block, block, block,
            square,
            jax.ShapeDtypeStruct((2 * width, length), F32),
        ),
        in_specs=[smem()] * 2 + vmem(9),
        out_specs=tuple(vmem(7)),
        compiler_params=pltpu.CompilerParams(vmem_limit_bytes=24 * 1024 * 1024),
        cost_estimate=pl.CostEstimate(
            flops=3_000_000_000, bytes_accessed=4_000_000, transcendentals=800_000
        ),
        name="backward",
    )(position[None], pair_active, joined, *received, stats, gatt, gglob)
    returned = [lax.ppermute(t, CTX, route) for t, route in zip(terms, routes)]
    shares, *returned = lax.optimization_barrier((shares, *returned))
    share = jnp.sum(shares.astype(F32), axis=0).astype(BF16)
    column = lax.all_to_all(jnp.broadcast_to(share[None], (zs,) + share.shape), "z", 0, 0)
    weight_cols = lax.dynamic_slice_in_dim(
        weight_all, lax.axis_index(HEAD) * width, width, axis=2
    )
    totals = lax.all_to_all(
        jnp.broadcast_to(column[None], (xs,) + column.shape), "x", 0, 0
    ).reshape(devices, 32, 128)

    projected = pl.pallas_call(
        project_kernel,
        out_shape=jax.ShapeDtypeStruct((length, width), BF16),
        in_specs=vmem(2),
        out_specs=vmem(1)[0],
        cost_estimate=pl.CostEstimate(
            flops=70_000_000, bytes_accessed=1_500_000, transcendentals=0
        ),
        name="project",
    )(attended_all, weight_cols)
    gqk, gval, gweight = pl.pallas_call(
        finish_kernel,
        out_shape=(
            jax.ShapeDtypeStruct((length, width), BF16),
            jax.ShapeDtypeStruct((length, width), BF16),
            jax.ShapeDtypeStruct((width, pieces * 128), F32),
        ),
        in_specs=[smem()] * 2 + vmem(8),
        out_specs=tuple(vmem(3)),
        compiler_params=pltpu.CompilerParams(vmem_limit_bytes=16 * 1024 * 1024),
        cost_estimate=pl.CostEstimate(
            flops=2_000_000, bytes_accessed=2_500_000, transcendentals=0
        ),
        name="finish",
    )(position[None], global_ids, *returned, gown, gquery, totals)
    return (projected, gqk, gval, gweight)


def solution(mesh):
    ctx, head = mesh.devices.shape
    cores = 2 if head % 2 == 0 else 1
    inner = Mesh(mesh.devices.reshape(ctx // 4, 4, head // cores, cores), CTX + HEAD)
    row = P(CTX, HEAD)
    return jax.shard_map(
        local,
        mesh=inner,
        in_specs=(row, row, row, P(HEAD, None), P(), P()),
        out_specs=(row, row, row, P(HEAD, None)),
        check_vma=False,
    )
```

```python
import functools
import math

import jax
import jax.numpy as jnp
from jax import lax
from jax.experimental import pallas as pl
from jax.experimental.pallas import tpu as pltpu
from jax.sharding import Mesh, PartitionSpec as P

HD = 64
NGLOB = 2
ROUNDS = 4
CTX = ("hi", "lo")
HEAD = "head"
PATCH = 16
NT = (((1,), (1,)), ((), ()))
TN = (((0,), (0,)), ((), ()))
NN = (((1,), (0,)), ((), ()))
F32 = jnp.float32
BF16 = jnp.bfloat16
MASKED = -1e30


def dot(a, b, dims):
    return lax.dot_general(a, b, dims, preferred_element_type=F32)


def block_bias(pos_ref, pair_ref):
    position = pos_ref[0]
    devices = 2 * pair_ref.shape[1]
    linked = []
    for k in range(ROUNDS):
        stride = 1 << k
        lowest = jnp.bitwise_and(position, devices - 1 - stride)
        slot = jnp.right_shift(lowest, k + 1) * stride + jnp.bitwise_and(lowest, stride - 1)
        linked.append(pair_ref[k, slot] == 1)
    inside = jnp.logical_and(position > 0, position < devices - 1)
    zero = jnp.float32(0.0)
    bias = [zero, jnp.where(linked[0], jnp.float32(1.0), zero)]
    bias += [jnp.where(m, zero, jnp.float32(MASKED)) for m in [inside] + linked[1:]]
    return bias + [zero] * NGLOB


def cotangent_kernel(head_ref, all_ref, w_ref, out_ref, gatt_ref, cols_ref):
    pieces, length, width = out_ref.shape
    blocks = length // 128
    gatt = jnp.zeros((length, width), F32)
    for c in range(pieces):
        part = all_ref[c, 0:blocks].reshape(length, width)
        out_ref[c] = part
        gatt = gatt + dot(part, w_ref[:, c * width:(c + 1) * width], NT)
        cols_ref[c] = all_ref[c, blocks + head_ref[0]]
    gatt_ref[...] = gatt.astype(BF16)


def forward_kernel(
    pos_ref, pair_ref, own_ref, p0, p1, p2, p3, p4, glob_ref, gout_ref, gatt_ref,
    att_ref, sums_ref, stats_ref, gquery_ref,
    score_ref, out_ref,
):
    length = own_ref.shape[0] // 2
    width = own_ref.shape[1]
    pieces = gout_ref.shape[0]
    nheads = width // HD
    scaling = 1.0 / math.sqrt(HD)
    base2 = scaling / math.log(2.0)
    bias = block_bias(pos_ref, pair_ref)
    keys = [r[:length] for r in (own_ref, p0, p1, p2, p3, p4)]
    vals = [r[length:] for r in (own_ref, p0, p1, p2, p3, p4)]
    half = glob_ref.shape[0] // 2
    for g in range(NGLOB):
        keys.append(jnp.concatenate([glob_ref[p, g] for p in range(half)], axis=0))
        vals.append(jnp.concatenate([glob_ref[half + p, g] for p in range(half)], axis=0))
    count = len(keys)
    query = own_ref[:length]
    lane = lax.broadcasted_iota(jnp.int32, (1, width), 1)
    head = lane // HD
    gatt_b = gatt_ref[...]

    inverse = []
    stats = jnp.zeros((length, width), F32)
    for h in range(nheads):
        query_h = jnp.where(head == h, query, jnp.zeros_like(query))
        highest = jnp.full((length, 1), MASKED, F32)
        for b in range(count):
            s = dot(query_h, keys[b], NT) * base2 + bias[b]
            score_ref[h, :, b * length:(b + 1) * length] = s
            highest = jnp.maximum(highest, jnp.max(s, axis=1, keepdims=True))
        total = jnp.zeros((length, 1), F32)
        for b in range(count):
            e = jnp.exp2(score_ref[h, :, b * length:(b + 1) * length] - highest)
            score_ref[h, :, b * length:(b + 1) * length] = e
            total = total + jnp.sum(e, axis=1, keepdims=True)
        inv = 1.0 / total
        inverse.append(inv)
        stats = jnp.where(lane == h, highest + jnp.log2(total), stats)
        acc = jnp.zeros((length, width), F32)
        for b in range(count):
            e = score_ref[h, :, b * length:(b + 1) * length]
            acc = acc + dot((e * inv).astype(BF16), vals[b], NN)
        if h == 0:
            out_ref[...] = acc
        else:
            out_ref[...] = jnp.where(head == h, acc, out_ref[...])

    attended = out_ref[...]
    att_ref[...] = attended
    attended_b = attended.astype(BF16)
    for c in range(pieces):
        part = dot(attended_b, gout_ref[c], TN).astype(BF16)
        n = width // HD
        sums_ref[c * n:(c + 1) * n, 0:HD, :] = part.reshape(n, HD, 128)

    product = gatt_b.astype(F32) * attended
    query_t = query.astype(F32).T.astype(BF16)
    gatt_t = gatt_b.astype(F32).T.astype(BF16)
    for h in range(nheads):
        gatt_h = jnp.where(head == h, gatt_b, jnp.zeros_like(gatt_b))
        row_dot = jnp.sum(jnp.where(head == h, product, 0.0), axis=1, keepdims=True)
        stats = jnp.where(lane == nheads + h, row_dot, stats)
        inv = inverse[h]
        qt = query_t[h * HD:(h + 1) * HD]
        gt = gatt_t[h * HD:(h + 1) * HD]
        acc = jnp.zeros((length, width), F32)
        for g in range(NGLOB):
            b = count - NGLOB + g
            weights = score_ref[h, :, b * length:(b + 1) * length] * inv
            gw = dot(gatt_h, vals[b], NT)
            gs = (weights * (gw - row_dot)).astype(BF16)
            acc = acc + dot(gs, keys[b], NN)
            gk = dot(qt, gs, NN) * scaling
            gv = dot(gt, weights.astype(BF16), NN)
            for a in range(length // 128):
                at = (g * (length // 128) + a) * 2 * nheads + h
                cols = slice(a * 128, (a + 1) * 128)
                sums_ref[at, HD:2 * HD, :] = gk[:, cols].astype(BF16)
                sums_ref[at + nheads, HD:2 * HD, :] = gv[:, cols].astype(BF16)
        if h == 0:
            out_ref[...] = acc
        else:
            out_ref[...] = jnp.where(head == h, acc, out_ref[...])
    stats_ref[...] = stats
    gquery_ref[...] = out_ref[...]


def backward_kernel(
    pos_ref, pair_ref, own_ref, p0, p1, p2, p3, p4, stats_ref, gatt_ref, gglob_ref,
    r0, r1, r2, r3, r4, gquery_ref, gown_ref,
):
    length = own_ref.shape[0] // 2
    width = own_ref.shape[1]
    nheads = width // HD
    scaling = 1.0 / math.sqrt(HD)
    base2 = scaling / math.log(2.0)
    bias = block_bias(pos_ref, pair_ref)
    query = own_ref[:length]
    gatt_b = gatt_ref[...]
    head = lax.broadcasted_iota(jnp.int32, (1, width), 1) // HD
    query_t = query.astype(F32).T.astype(BF16)
    gatt_t = gatt_b.astype(F32).T.astype(BF16)
    blocks = (own_ref, p0, p1, p2, p3, p4)
    outs = (gown_ref, r0, r1, r2, r3, r4)
    result = gglob_ref[...]
    for h in range(nheads):
        query_h = jnp.where(head == h, query, jnp.zeros_like(query))
        gatt_h = jnp.where(head == h, gatt_b, jnp.zeros_like(gatt_b))
        log_total = stats_ref[:, h:h + 1]
        row_dot = stats_ref[:, nheads + h:nheads + h + 1]
        qt = query_t[h * HD:(h + 1) * HD]
        gt = gatt_t[h * HD:(h + 1) * HD]
        acc = jnp.zeros((length, width), F32)
        for b in (1, 2, 3, 4, 5, 0):
            keys = blocks[b][:length]
            s = dot(query_h, keys, NT) * base2 + (bias[b] - log_total)
            weights = jnp.exp2(s)
            gw = dot(gatt_h, blocks[b][length:], NT)
            gs = (weights * (gw - row_dot)).astype(BF16)
            acc = acc + dot(gs, keys, NN)
            gk = dot(qt, gs, NN) * scaling
            gv = dot(gt, weights.astype(BF16), NN)
            o = outs[b]
            o[h * HD:(h + 1) * HD, :] = gk.astype(o.dtype)
            o[width + h * HD:width + (h + 1) * HD, :] = gv.astype(o.dtype)
        result = result + jnp.where(head == h, acc, 0.0)
    gquery_ref[...] = result * scaling


def project_kernel(att_ref, w_ref, projected_ref):
    projected = jnp.zeros(projected_ref.shape, F32)
    for c in range(att_ref.shape[0]):
        projected = projected + dot(att_ref[c].astype(BF16), w_ref[c], NN)
    projected_ref[...] = projected.astype(BF16)


def finish_kernel(
    pos_ref, ids_ref, b0, b1, b2, b3, b4, gown_ref, gquery_ref, total_ref,
    gqk_ref, gval_ref, gweight_ref,
):
    length, width = gquery_ref.shape
    halves = length // 128
    rows = width * 2 // HD
    for a in range(halves):
        cols = slice(a * 128, (a + 1) * 128)
        acc = gown_ref[:, cols]
        for b in (b0, b1, b2, b3, b4):
            acc = acc + b[:, cols].astype(F32)
        for g in range(NGLOB):
            at = (g * halves + a) * rows
            term = total_ref[at:at + rows, HD:2 * HD, :].reshape(2 * width, 128).astype(F32)
            acc = acc + jnp.where(ids_ref[g] == pos_ref[0], term, 0.0)
        tokens = slice(a * 128, (a + 1) * 128)
        gqk_ref[tokens, :] = (gquery_ref[tokens, :] + acc[:width].T).astype(BF16)
        gval_ref[tokens, :] = acc[width:].T.astype(BF16)
    n = width // HD
    for c in range(gweight_ref.shape[1] // 128):
        piece = total_ref[c * n:(c + 1) * n, 0:HD, :].reshape(width, 128)
        gweight_ref[:, c * 128:(c + 1) * 128] = piece.astype(F32)


def pack_kernel(qk_ref, val_ref, gout_ref, w_ref, joined_ref, share_ref):
    length, width = qk_ref.shape
    blocks = length // 128
    joined_ref[:length] = qk_ref[...]
    joined_ref[length:] = val_ref[...]
    share_ref[0:blocks] = gout_ref[...].reshape(blocks, 128, width)
    for c in range(w_ref.shape[1] // 128):
        share_ref[blocks + c] = w_ref[:, c * 128:(c + 1) * 128]


def pick_kernel(ids_ref, slices_ref, out_ref):
    for g in range(NGLOB):
        chosen = slices_ref[lax.rem(ids_ref[g], PATCH)]
        for n in range(out_ref.shape[0]):
            out_ref[n, g] = chosen


def spread_kernel(ids_ref, slices_ref, out_ref):
    for g in range(NGLOB):
        chosen = slices_ref[lax.div(ids_ref[g], PATCH), g]
        for n in range(out_ref.shape[0]):
            out_ref[n, g] = chosen


def vmem(count):
    return [pl.BlockSpec(memory_space=pltpu.VMEM)] * count


def smem():
    return pl.BlockSpec(memory_space=pltpu.SMEM)


def local(qk_vectors, token_values, grad_output, out_weight, global_ids, pair_active):
    length, width = qk_vectors.shape
    devices = lax.axis_size(CTX)
    pieces = lax.axis_size(HEAD)
    position = lax.axis_index(CTX)
    joined = jnp.concatenate([qk_vectors, token_values], axis=0)

    his, los = lax.axis_size("hi"), lax.axis_size("lo")
    step = 2 * length // los
    joined, share = pl.pallas_call(
        pack_kernel,
        out_shape=(
            jax.ShapeDtypeStruct((2 * length, width), BF16),
            jax.ShapeDtypeStruct((length // 128 + pieces, 128, width), BF16),
        ),
        in_specs=vmem(4),
        out_specs=tuple(vmem(2)),
        name="pack",
    )(qk_vectors, token_values, grad_output, out_weight)

    slices = lax.all_to_all(joined.reshape(los, step, width), "lo", 0, 0)
    portion = lax.all_gather(share, HEAD, axis=0)
    routes = [[(i, i ^ 1) for i in range(devices)]]
    other = [i + 1 if i % 2 else i - 1 for i in range(devices)]
    routes.append([(i, j) for i, j in enumerate(other) if 0 <= j < devices])
    routes += [[(i, i ^ (1 << k)) for i in range(devices)] for k in range(1, ROUNDS)]
    received = [None] * len(routes)
    for n in (0, 2):
        received[n] = lax.ppermute(joined, CTX, routes[n])
    slices, received[0], received[2] = lax.optimization_barrier((slices, received[0], received[2]))
    picked = pl.pallas_call(
        pick_kernel,
        out_shape=jax.ShapeDtypeStruct((his, NGLOB, step, width), BF16),
        in_specs=[smem()] + vmem(1),
        out_specs=vmem(1)[0],
        name="pick",
    )(global_ids, slices)
    picked, joined_late = lax.optimization_barrier((picked, joined))
    column = lax.all_to_all(picked, "hi", 0, 0)
    for n in (4, 3):
        received[n] = lax.ppermute(joined_late, CTX, routes[n])
    column, received[3], received[4] = lax.optimization_barrier((column, received[3], received[4]))
    chosen = pl.pallas_call(
        spread_kernel,
        out_shape=jax.ShapeDtypeStruct((los, NGLOB, step, width), BF16),
        in_specs=[smem()] + vmem(1),
        out_specs=vmem(1)[0],
        name="spread",
    )(global_ids, column)
    chosen, joined_late, portion = lax.optimization_barrier((chosen, joined, portion))
    globals_all = lax.all_to_all(chosen, "lo", 0, 0)
    received[1] = lax.ppermute(joined_late, CTX, routes[1])
    portion_b, gatt, weight_cols = pl.pallas_call(
        cotangent_kernel,
        out_shape=(
            jax.ShapeDtypeStruct((pieces, length, width), BF16),
            jax.ShapeDtypeStruct((length, width), BF16),
            jax.ShapeDtypeStruct((pieces, width, 128), BF16),
        ),
        in_specs=[smem()] + vmem(2),
        out_specs=tuple(vmem(3)),
        compiler_params=pltpu.CompilerParams(vmem_limit_bytes=16 * 1024 * 1024),
        cost_estimate=pl.CostEstimate(
            flops=600_000_000, bytes_accessed=4_000_000, transcendentals=0
        ),
        name="cotangent",
    )(lax.axis_index(HEAD)[None], portion, out_weight)

    count = ROUNDS + 2 + NGLOB
    nheads = width // HD
    block = jax.ShapeDtypeStruct((2 * width, length), BF16)
    square = jax.ShapeDtypeStruct((length, width), F32)
    attended, sums, stats, gglob = pl.pallas_call(
        forward_kernel,
        out_shape=(
            square,
            jax.ShapeDtypeStruct((los, 2 * HD, 128), BF16),
            square,
            square,
        ),
        in_specs=[smem()] * 2 + vmem(9),
        out_specs=tuple(vmem(4)),
        scratch_shapes=[
            pltpu.VMEM((nheads, length, count * length), F32),
            pltpu.VMEM((length, width), F32),
        ],
        compiler_params=pltpu.CompilerParams(vmem_limit_bytes=40 * 1024 * 1024),
        cost_estimate=pl.CostEstimate(
            flops=3_000_000_000, bytes_accessed=4_000_000, transcendentals=1_100_000
        ),
        name="forward",
    )(position[None], pair_active, joined, *received, globals_all, portion_b, gatt)

    shares = lax.all_to_all(sums, "lo", 0, 0)
    attended_all = lax.all_gather(attended, HEAD, axis=0)
    *terms, gquery, gown = pl.pallas_call(
        backward_kernel,
        out_shape=(
            block, block, block, block, block,
            square,
            jax.ShapeDtypeStruct((2 * width, length), F32),
        ),
        in_specs=[smem()] * 2 + vmem(9),
        out_specs=tuple(vmem(7)),
        compiler_params=pltpu.CompilerParams(vmem_limit_bytes=24 * 1024 * 1024),
        cost_estimate=pl.CostEstimate(
            flops=3_000_000_000, bytes_accessed=4_000_000, transcendentals=800_000
        ),
        name="backward",
    )(position[None], pair_active, joined, *received, stats, gatt, gglob)
    shares, *terms = lax.optimization_barrier((shares, *terms))
    share = jnp.sum(shares.astype(F32), axis=0).astype(BF16)
    column = lax.all_to_all(jnp.broadcast_to(share[None], (his,) + share.shape), "hi", 0, 0)
    returned = [lax.ppermute(t, CTX, route) for t, route in zip(terms, routes)]
    column, attended_all, *returned[:3] = lax.optimization_barrier(
        (column, attended_all, *returned[:3])
    )
    share = jnp.sum(column.astype(F32), axis=0).astype(BF16)
    totals = lax.all_to_all(jnp.broadcast_to(share[None], (los,) + share.shape), "lo", 0, 0)

    projected = pl.pallas_call(
        project_kernel,
        out_shape=jax.ShapeDtypeStruct((length, width), BF16),
        in_specs=vmem(2),
        out_specs=vmem(1)[0],
        cost_estimate=pl.CostEstimate(
            flops=70_000_000, bytes_accessed=1_500_000, transcendentals=0
        ),
        name="project",
    )(attended_all, weight_cols)
    gqk, gval, gweight = pl.pallas_call(
        finish_kernel,
        out_shape=(
            jax.ShapeDtypeStruct((length, width), BF16),
            jax.ShapeDtypeStruct((length, width), BF16),
            jax.ShapeDtypeStruct((width, pieces * 128), F32),
        ),
        in_specs=[smem()] * 2 + vmem(8),
        out_specs=tuple(vmem(3)),
        compiler_params=pltpu.CompilerParams(vmem_limit_bytes=16 * 1024 * 1024),
        cost_estimate=pl.CostEstimate(
            flops=2_000_000, bytes_accessed=2_500_000, transcendentals=0
        ),
        name="finish",
    )(position[None], global_ids, *returned, gown, gquery, totals)
    return (projected, gqk, gval, gweight)


def solution(mesh):
    ctx, head = mesh.devices.shape
    inner = Mesh(mesh.devices.reshape(ctx // PATCH, PATCH, head), CTX + (HEAD,))
    row = P(CTX, HEAD)
    return jax.shard_map(
        local,
        mesh=inner,
        in_specs=(row, row, row, P(HEAD, None), P(), P()),
        out_specs=(row, row, row, P(HEAD, None)),
        check_vma=False,
    )
```

```python
import functools
import math

import jax
import jax.numpy as jnp
from jax import lax
from jax.experimental import pallas as pl
from jax.experimental.pallas import tpu as pltpu
from jax.sharding import Mesh, PartitionSpec as P

HD = 64
NGLOB = 2
ROUNDS = 4
CTX = ("hi", "lo")
HEAD = "head"
PATCH = 16
NT = (((1,), (1,)), ((), ()))
TN = (((0,), (0,)), ((), ()))
NN = (((1,), (0,)), ((), ()))
F32 = jnp.float32
BF16 = jnp.bfloat16
MASKED = -1e30


def dot(a, b, dims):
    return lax.dot_general(a, b, dims, preferred_element_type=F32)


def block_bias(pos_ref, pair_ref):
    position = pos_ref[0]
    devices = 2 * pair_ref.shape[1]
    linked = []
    for k in range(ROUNDS):
        stride = 1 << k
        lowest = jnp.bitwise_and(position, devices - 1 - stride)
        slot = jnp.right_shift(lowest, k + 1) * stride + jnp.bitwise_and(lowest, stride - 1)
        linked.append(pair_ref[k, slot] == 1)
    inside = jnp.logical_and(position > 0, position < devices - 1)
    zero = jnp.float32(0.0)
    bias = [zero, jnp.where(linked[0], jnp.float32(1.0), zero)]
    bias += [jnp.where(m, zero, jnp.float32(MASKED)) for m in [inside] + linked[1:]]
    return bias + [zero] * NGLOB


def cotangent_kernel(head_ref, all_ref, w_ref, out_ref, gatt_ref, cols_ref):
    pieces, length, width = out_ref.shape
    blocks = length // 128
    gatt = jnp.zeros((length, width), F32)
    for c in range(pieces):
        part = all_ref[c, 0:blocks].reshape(length, width)
        out_ref[c] = part
        gatt = gatt + dot(part, w_ref[:, c * width:(c + 1) * width], NT)
        cols_ref[c] = all_ref[c, blocks + head_ref[0]]
    gatt_ref[...] = gatt.astype(BF16)


def forward_kernel(
    pos_ref, pair_ref, own_ref, p0, p1, p2, p3, p4, glob_ref, gout_ref, gatt_ref,
    att_ref, sums_ref, stats_ref, gquery_ref,
    score_ref, out_ref,
):
    length = own_ref.shape[0] // 2
    width = own_ref.shape[1]
    pieces = gout_ref.shape[0]
    nheads = width // HD
    scaling = 1.0 / math.sqrt(HD)
    base2 = scaling / math.log(2.0)
    bias = block_bias(pos_ref, pair_ref)
    keys = [r[:length] for r in (own_ref, p0, p1, p2, p3, p4)]
    vals = [r[length:] for r in (own_ref, p0, p1, p2, p3, p4)]
    half = glob_ref.shape[0] // 2
    for g in range(NGLOB):
        keys.append(jnp.concatenate([glob_ref[p, g] for p in range(half)], axis=0))
        vals.append(jnp.concatenate([glob_ref[half + p, g] for p in range(half)], axis=0))
    count = len(keys)
    query = own_ref[:length]
    lane = lax.broadcasted_iota(jnp.int32, (1, width), 1)
    head = lane // HD
    gatt_b = gatt_ref[...]

    inverse = []
    stats = jnp.zeros((length, width), F32)
    for h in range(nheads):
        query_h = jnp.where(head == h, query, jnp.zeros_like(query))
        highest = jnp.full((length, 1), MASKED, F32)
        for b in range(count):
            s = dot(query_h, keys[b], NT) * base2 + bias[b]
            score_ref[h, :, b * length:(b + 1) * length] = s
            highest = jnp.maximum(highest, jnp.max(s, axis=1, keepdims=True))
        total = jnp.zeros((length, 1), F32)
        for b in range(count):
            e = jnp.exp2(score_ref[h, :, b * length:(b + 1) * length] - highest)
            score_ref[h, :, b * length:(b + 1) * length] = e
            total = total + jnp.sum(e, axis=1, keepdims=True)
        inv = 1.0 / total
        inverse.append(inv)
        stats = jnp.where(lane == h, highest + jnp.log2(total), stats)
        acc = jnp.zeros((length, width), F32)
        for b in range(count):
            e = score_ref[h, :, b * length:(b + 1) * length]
            acc = acc + dot((e * inv).astype(BF16), vals[b], NN)
        if h == 0:
            out_ref[...] = acc
        else:
            out_ref[...] = jnp.where(head == h, acc, out_ref[...])

    attended = out_ref[...]
    att_ref[...] = attended
    attended_b = attended.astype(BF16)
    for c in range(pieces):
        part = dot(attended_b, gout_ref[c], TN).astype(BF16)
        n = width // HD
        sums_ref[c * n:(c + 1) * n, 0:HD, :] = part.reshape(n, HD, 128)

    product = gatt_b.astype(F32) * attended
    query_t = query.astype(F32).T.astype(BF16)
    gatt_t = gatt_b.astype(F32).T.astype(BF16)
    for h in range(nheads):
        gatt_h = jnp.where(head == h, gatt_b, jnp.zeros_like(gatt_b))
        row_dot = jnp.sum(jnp.where(head == h, product, 0.0), axis=1, keepdims=True)
        stats = jnp.where(lane == nheads + h, row_dot, stats)
        inv = inverse[h]
        qt = query_t[h * HD:(h + 1) * HD]
        gt = gatt_t[h * HD:(h + 1) * HD]
        acc = jnp.zeros((length, width), F32)
        for g in range(NGLOB):
            b = count - NGLOB + g
            weights = score_ref[h, :, b * length:(b + 1) * length] * inv
            gw = dot(gatt_h, vals[b], NT)
            gs = (weights * (gw - row_dot)).astype(BF16)
            acc = acc + dot(gs, keys[b], NN)
            gk = dot(qt, gs, NN) * scaling
            gv = dot(gt, weights.astype(BF16), NN)
            for a in range(length // 128):
                at = (g * (length // 128) + a) * 2 * nheads + h
                cols = slice(a * 128, (a + 1) * 128)
                sums_ref[at, HD:2 * HD, :] = gk[:, cols].astype(BF16)
                sums_ref[at + nheads, HD:2 * HD, :] = gv[:, cols].astype(BF16)
        if h == 0:
            out_ref[...] = acc
        else:
            out_ref[...] = jnp.where(head == h, acc, out_ref[...])
    stats_ref[...] = stats
    gquery_ref[...] = out_ref[...]


def backward_kernel(
    pos_ref, pair_ref, own_ref, p0, p1, p2, p3, p4, stats_ref, gatt_ref, gglob_ref,
    r0, r1, r2, r3, r4, gquery_ref, gown_ref,
):
    length = own_ref.shape[0] // 2
    width = own_ref.shape[1]
    nheads = width // HD
    scaling = 1.0 / math.sqrt(HD)
    base2 = scaling / math.log(2.0)
    bias = block_bias(pos_ref, pair_ref)
    query = own_ref[:length]
    gatt_b = gatt_ref[...]
    head = lax.broadcasted_iota(jnp.int32, (1, width), 1) // HD
    query_t = query.astype(F32).T.astype(BF16)
    gatt_t = gatt_b.astype(F32).T.astype(BF16)
    blocks = (own_ref, p0, p1, p2, p3, p4)
    outs = (gown_ref, r0, r1, r2, r3, r4)
    result = gglob_ref[...]
    for h in range(nheads):
        query_h = jnp.where(head == h, query, jnp.zeros_like(query))
        gatt_h = jnp.where(head == h, gatt_b, jnp.zeros_like(gatt_b))
        log_total = stats_ref[:, h:h + 1]
        row_dot = stats_ref[:, nheads + h:nheads + h + 1]
        qt = query_t[h * HD:(h + 1) * HD]
        gt = gatt_t[h * HD:(h + 1) * HD]
        acc = jnp.zeros((length, width), F32)
        for b in (1, 2, 3, 4, 5, 0):
            keys = blocks[b][:length]
            s = dot(query_h, keys, NT) * base2 + (bias[b] - log_total)
            weights = jnp.exp2(s)
            gw = dot(gatt_h, blocks[b][length:], NT)
            gs = (weights * (gw - row_dot)).astype(BF16)
            acc = acc + dot(gs, keys, NN)
            gk = dot(qt, gs, NN) * scaling
            gv = dot(gt, weights.astype(BF16), NN)
            o = outs[b]
            o[h * HD:(h + 1) * HD, :] = gk.astype(o.dtype)
            o[width + h * HD:width + (h + 1) * HD, :] = gv.astype(o.dtype)
        result = result + jnp.where(head == h, acc, 0.0)
    gquery_ref[...] = result * scaling


def project_kernel(att_ref, w_ref, projected_ref):
    projected = jnp.zeros(projected_ref.shape, F32)
    for c in range(att_ref.shape[0]):
        projected = projected + dot(att_ref[c].astype(BF16), w_ref[c], NN)
    projected_ref[...] = projected.astype(BF16)


def finish_kernel(
    pos_ref, ids_ref, b0, b1, b2, b3, b4, gown_ref, gquery_ref, total_ref,
    gqk_ref, gval_ref, gweight_ref,
):
    length, width = gquery_ref.shape
    halves = length // 128
    rows = width * 2 // HD
    for a in range(halves):
        cols = slice(a * 128, (a + 1) * 128)
        acc = gown_ref[:, cols]
        for b in (b0, b1, b2, b3, b4):
            acc = acc + b[:, cols].astype(F32)
        for g in range(NGLOB):
            at = (g * halves + a) * rows
            term = total_ref[at:at + rows, HD:2 * HD, :].reshape(2 * width, 128).astype(F32)
            acc = acc + jnp.where(ids_ref[g] == pos_ref[0], term, 0.0)
        tokens = slice(a * 128, (a + 1) * 128)
        gqk_ref[tokens, :] = (gquery_ref[tokens, :] + acc[:width].T).astype(BF16)
        gval_ref[tokens, :] = acc[width:].T.astype(BF16)
    n = width // HD
    for c in range(gweight_ref.shape[1] // 128):
        piece = total_ref[c * n:(c + 1) * n, 0:HD, :].reshape(width, 128)
        gweight_ref[:, c * 128:(c + 1) * 128] = piece.astype(F32)


def pack_kernel(qk_ref, val_ref, gout_ref, w_ref, joined_ref, share_ref):
    length, width = qk_ref.shape
    blocks = length // 128
    joined_ref[:length] = qk_ref[...]
    joined_ref[length:] = val_ref[...]
    share_ref[0:blocks] = gout_ref[...].reshape(blocks, 128, width)
    for c in range(w_ref.shape[1] // 128):
        share_ref[blocks + c] = w_ref[:, c * 128:(c + 1) * 128]


def copy_all(copies):
    for copy in copies:
        copy.start()
    for copy in copies:
        copy.wait()


def pick_kernel(ids_ref, slices_ref, out_ref, sems):
    count = out_ref.shape[0]
    copies = []
    for g in range(NGLOB):
        chosen = slices_ref.at[lax.rem(ids_ref[g], PATCH)]
        for n in range(count):
            sem = sems.at[g * count + n]
            copies.append(pltpu.make_async_copy(chosen, out_ref.at[n, g], sem))
    copy_all(copies)


def spread_kernel(ids_ref, slices_ref, out_ref, sems):
    count = out_ref.shape[0]
    copies = []
    for g in range(NGLOB):
        chosen = slices_ref.at[lax.div(ids_ref[g], PATCH), g]
        for n in range(count):
            sem = sems.at[g * count + n]
            copies.append(pltpu.make_async_copy(chosen, out_ref.at[n, g], sem))
    copy_all(copies)


def anywhere():
    return pl.BlockSpec(memory_space=pl.ANY)


def limit(mebibytes):
    return pltpu.CompilerParams(vmem_limit_bytes=mebibytes * 1024 * 1024)


def vmem(count):
    return [pl.BlockSpec(memory_space=pltpu.VMEM)] * count


def smem():
    return pl.BlockSpec(memory_space=pltpu.SMEM)


def local(qk_vectors, token_values, grad_output, out_weight, global_ids, pair_active):
    length, width = qk_vectors.shape
    devices = lax.axis_size(CTX)
    pieces = lax.axis_size(HEAD)
    position = lax.axis_index(CTX)
    joined = jnp.concatenate([qk_vectors, token_values], axis=0)

    his, los = lax.axis_size("hi"), lax.axis_size("lo")
    step = 2 * length // los
    joined, share = pl.pallas_call(
        pack_kernel,
        out_shape=(
            jax.ShapeDtypeStruct((2 * length, width), BF16),
            jax.ShapeDtypeStruct((length // 128 + pieces, 128, width), BF16),
        ),
        in_specs=vmem(4),
        out_specs=tuple(vmem(2)),
        name="pack",
    )(qk_vectors, token_values, grad_output, out_weight)

    slices = lax.all_to_all(joined.reshape(los, step, width), "lo", 0, 0)
    portion = lax.all_gather(share, HEAD, axis=0)
    routes = [[(i, i ^ 1) for i in range(devices)]]
    other = [i + 1 if i % 2 else i - 1 for i in range(devices)]
    routes.append([(i, j) for i, j in enumerate(other) if 0 <= j < devices])
    routes += [[(i, i ^ (1 << k)) for i in range(devices)] for k in range(1, ROUNDS)]
    received = [None] * len(routes)
    for n in (0, 2):
        received[n] = lax.ppermute(joined, CTX, routes[n])
    slices, received[0] = lax.optimization_barrier((slices, received[0]))
    picked = pl.pallas_call(
        pick_kernel,
        out_shape=jax.ShapeDtypeStruct((his, NGLOB, step, width), BF16),
        in_specs=[smem(), anywhere()],
        out_specs=anywhere(),
        scratch_shapes=[pltpu.SemaphoreType.DMA((NGLOB * his,))],
        compiler_params=limit(1),
        name="pick",
    )(global_ids, slices)
    picked, joined_late, received[2] = lax.optimization_barrier((picked, joined, received[2]))
    column = lax.all_to_all(picked, "hi", 0, 0)
    for n in (4, 3):
        received[n] = lax.ppermute(joined_late, CTX, routes[n])
    portion_b, gatt, weight_cols = pl.pallas_call(
        cotangent_kernel,
        out_shape=(
            jax.ShapeDtypeStruct((pieces, length, width), BF16),
            jax.ShapeDtypeStruct((length, width), BF16),
            jax.ShapeDtypeStruct((pieces, width, 128), BF16),
        ),
        in_specs=[smem()] + vmem(2),
        out_specs=tuple(vmem(3)),
        compiler_params=limit(8),
        cost_estimate=pl.CostEstimate(
            flops=600_000_000, bytes_accessed=4_000_000, transcendentals=0
        ),
        name="cotangent",
    )(lax.axis_index(HEAD)[None], portion, out_weight)
    column, received[4], portion_b, gatt, weight_cols = lax.optimization_barrier(
        (column, received[4], portion_b, gatt, weight_cols)
    )
    chosen = pl.pallas_call(
        spread_kernel,
        out_shape=jax.ShapeDtypeStruct((los, NGLOB, step, width), BF16),
        in_specs=[smem(), anywhere()],
        out_specs=anywhere(),
        scratch_shapes=[pltpu.SemaphoreType.DMA((NGLOB * los,))],
        compiler_params=limit(1),
        name="spread",
    )(global_ids, column)
    chosen, joined_late, received[3] = lax.optimization_barrier((chosen, joined, received[3]))
    globals_all = lax.all_to_all(chosen, "lo", 0, 0)
    received[1] = lax.ppermute(joined_late, CTX, routes[1])
    count = ROUNDS + 2 + NGLOB
    nheads = width // HD
    block = jax.ShapeDtypeStruct((2 * width, length), BF16)
    square = jax.ShapeDtypeStruct((length, width), F32)
    attended, sums, stats, gglob = pl.pallas_call(
        forward_kernel,
        out_shape=(
            square,
            jax.ShapeDtypeStruct((los, 2 * HD, 128), BF16),
            square,
            square,
        ),
        in_specs=[smem()] * 2 + vmem(9),
        out_specs=tuple(vmem(4)),
        scratch_shapes=[
            pltpu.VMEM((nheads, length, count * length), F32),
            pltpu.VMEM((length, width), F32),
        ],
        compiler_params=limit(20),
        cost_estimate=pl.CostEstimate(
            flops=3_000_000_000, bytes_accessed=4_000_000, transcendentals=1_100_000
        ),
        name="forward",
    )(position[None], pair_active, joined, *received, globals_all, portion_b, gatt)

    shares = lax.all_to_all(sums, "lo", 0, 0)
    attended_all = lax.all_gather(attended, HEAD, axis=0)
    *terms, gquery, gown = pl.pallas_call(
        backward_kernel,
        out_shape=(
            block, block, block, block, block,
            square,
            jax.ShapeDtypeStruct((2 * width, length), F32),
        ),
        in_specs=[smem()] * 2 + vmem(9),
        out_specs=tuple(vmem(7)),
        compiler_params=limit(10),
        cost_estimate=pl.CostEstimate(
            flops=3_000_000_000, bytes_accessed=4_000_000, transcendentals=800_000
        ),
        name="backward",
    )(position[None], pair_active, joined, *received, stats, gatt, gglob)
    returned = [None] * len(routes)
    returned[0] = lax.ppermute(terms[0], CTX, routes[0])
    shares, *terms = lax.optimization_barrier((shares, *terms))
    share = jnp.sum(shares.astype(F32), axis=0).astype(BF16)
    share, returned[0] = lax.optimization_barrier((share, returned[0]))
    column = lax.all_to_all(jnp.broadcast_to(share[None], (his,) + share.shape), "hi", 0, 0)
    for n in (4, 2, 3, 1):
        returned[n] = lax.ppermute(terms[n], CTX, routes[n])
    column, returned[2], returned[4] = lax.optimization_barrier((column, returned[2], returned[4]))
    share = jnp.sum(column.astype(F32), axis=0).astype(BF16)
    share, attended_all = lax.optimization_barrier((share, attended_all))
    totals = lax.all_to_all(jnp.broadcast_to(share[None], (los,) + share.shape), "lo", 0, 0)

    projected = pl.pallas_call(
        project_kernel,
        out_shape=jax.ShapeDtypeStruct((length, width), BF16),
        in_specs=vmem(2),
        out_specs=vmem(1)[0],
        compiler_params=limit(4),
        cost_estimate=pl.CostEstimate(
            flops=70_000_000, bytes_accessed=1_500_000, transcendentals=0
        ),
        name="project",
    )(attended_all, weight_cols)
    gqk, gval, gweight = pl.pallas_call(
        finish_kernel,
        out_shape=(
            jax.ShapeDtypeStruct((length, width), BF16),
            jax.ShapeDtypeStruct((length, width), BF16),
            jax.ShapeDtypeStruct((width, pieces * 128), F32),
        ),
        in_specs=[smem()] * 2 + vmem(8),
        out_specs=tuple(vmem(3)),
        compiler_params=limit(6),
        cost_estimate=pl.CostEstimate(
            flops=2_000_000, bytes_accessed=2_500_000, transcendentals=0
        ),
        name="finish",
    )(position[None], global_ids, *returned, gown, gquery, totals)
    return (projected, gqk, gval, gweight)


def solution(mesh):
    ctx, head = mesh.devices.shape
    inner = Mesh(mesh.devices.reshape(ctx // PATCH, PATCH, head), CTX + (HEAD,))
    row = P(CTX, HEAD)
    return jax.shard_map(
        local,
        mesh=inner,
        in_specs=(row, row, row, P(HEAD, None), P(), P()),
        out_specs=(row, row, row, P(HEAD, None)),
        check_vma=False,
    )
```

```python
import functools
import math

import jax
import jax.numpy as jnp
from jax import lax
from jax.experimental import pallas as pl
from jax.experimental.pallas import tpu as pltpu
from jax.sharding import Mesh, PartitionSpec as P

HD = 64
NGLOB = 2
ROUNDS = 4
CTX = ("hi", "lo")
HEAD = "head"
PATCH = 16
NT = (((1,), (1,)), ((), ()))
TN = (((0,), (0,)), ((), ()))
NN = (((1,), (0,)), ((), ()))
F32 = jnp.float32
BF16 = jnp.bfloat16
MASKED = -1e30


def dot(a, b, dims):
    return lax.dot_general(a, b, dims, preferred_element_type=F32)


def block_bias(pos_ref, pair_ref):
    position = pos_ref[0]
    devices = 2 * pair_ref.shape[1]
    linked = []
    for k in range(ROUNDS):
        stride = 1 << k
        lowest = jnp.bitwise_and(position, devices - 1 - stride)
        slot = jnp.right_shift(lowest, k + 1) * stride + jnp.bitwise_and(lowest, stride - 1)
        linked.append(pair_ref[k, slot] == 1)
    inside = jnp.logical_and(position > 0, position < devices - 1)
    zero = jnp.float32(0.0)
    bias = [zero, jnp.where(linked[0], jnp.float32(1.0), zero)]
    bias += [jnp.where(m, zero, jnp.float32(MASKED)) for m in [inside] + linked[1:]]
    return bias + [zero] * NGLOB


def cotangent_kernel(head_ref, all_ref, w_ref, out_ref, gatt_ref, cols_ref):
    pieces, length, width = out_ref.shape
    blocks = length // 128
    gatt = jnp.zeros((length, width), F32)
    for c in range(pieces):
        part = all_ref[c, 0:blocks].reshape(length, width)
        out_ref[c] = part
        gatt = gatt + dot(part, w_ref[:, c * width:(c + 1) * width], NT)
        cols_ref[c] = all_ref[c, blocks + head_ref[0]]
    gatt_ref[...] = gatt.astype(BF16)


def near_kernel(
    pos_ref, pair_ref, own_ref, p0, p2, p3, p4, stats_ref, sum_ref, score_ref,
):
    length = own_ref.shape[0] // 2
    width = own_ref.shape[1]
    nheads = width // HD
    base2 = 1.0 / math.sqrt(HD) / math.log(2.0)
    bias = block_bias(pos_ref, pair_ref)
    blocks = ((own_ref, bias[0]), (p0, bias[1]), (p2, bias[3]), (p3, bias[4]), (p4, bias[5]))
    query = own_ref[:length]
    lane = lax.broadcasted_iota(jnp.int32, (1, width), 1)
    head = lane // HD
    stats = jnp.zeros((length, width), F32)
    for h in range(nheads):
        query_h = jnp.where(head == h, query, jnp.zeros_like(query))
        highest = jnp.full((length, 1), MASKED, F32)
        for b, (ref, shift) in enumerate(blocks):
            s = dot(query_h, ref[:length], NT) * base2 + shift
            score_ref[:, b * length:(b + 1) * length] = s
            highest = jnp.maximum(highest, jnp.max(s, axis=1, keepdims=True))
        total = jnp.zeros((length, 1), F32)
        acc = jnp.zeros((length, width), F32)
        for b, (ref, _) in enumerate(blocks):
            e = jnp.exp2(score_ref[:, b * length:(b + 1) * length] - highest)
            total = total + jnp.sum(e, axis=1, keepdims=True)
            acc = acc + dot(e.astype(BF16), ref[length:], NN)
        stats = jnp.where(lane == h, highest, stats)
        stats = jnp.where(lane == nheads + h, total, stats)
        if h == 0:
            sum_ref[...] = acc
        else:
            sum_ref[...] = jnp.where(head == h, acc, sum_ref[...])
    stats_ref[...] = stats


def forward_kernel(
    pos_ref, pair_ref, own_ref, p1, near_ref, sum_ref, glob_ref, gout_ref, gatt_ref,
    att_ref, sums_ref, stats_ref, gquery_ref,
    score_ref, out_ref,
):
    length = own_ref.shape[0] // 2
    width = own_ref.shape[1]
    pieces = gout_ref.shape[0]
    nheads = width // HD
    scaling = 1.0 / math.sqrt(HD)
    base2 = scaling / math.log(2.0)
    bias = block_bias(pos_ref, pair_ref)
    bias = [bias[2]] + bias[-NGLOB:]
    keys = [p1[:length]]
    vals = [p1[length:]]
    half = glob_ref.shape[0] // 2
    for g in range(NGLOB):
        keys.append(jnp.concatenate([glob_ref[p, g] for p in range(half)], axis=0))
        vals.append(jnp.concatenate([glob_ref[half + p, g] for p in range(half)], axis=0))
    count = len(keys)
    query = own_ref[:length]
    lane = lax.broadcasted_iota(jnp.int32, (1, width), 1)
    head = lane // HD
    gatt_b = gatt_ref[...]

    inverse = []
    stats = jnp.zeros((length, width), F32)
    for h in range(nheads):
        query_h = jnp.where(head == h, query, jnp.zeros_like(query))
        near = near_ref[:, h:h + 1]
        highest = near
        for b in range(count):
            s = dot(query_h, keys[b], NT) * base2 + bias[b]
            score_ref[h, :, b * length:(b + 1) * length] = s
            highest = jnp.maximum(highest, jnp.max(s, axis=1, keepdims=True))
        factor = jnp.exp2(near - highest)
        total = near_ref[:, nheads + h:nheads + h + 1] * factor
        acc = sum_ref[...] * factor
        for b in range(count):
            e = jnp.exp2(score_ref[h, :, b * length:(b + 1) * length] - highest)
            score_ref[h, :, b * length:(b + 1) * length] = e
            total = total + jnp.sum(e, axis=1, keepdims=True)
            acc = acc + dot(e.astype(BF16), vals[b], NN)
        inv = 1.0 / total
        inverse.append(inv)
        stats = jnp.where(lane == h, highest + jnp.log2(total), stats)
        if h == 0:
            out_ref[...] = acc * inv
        else:
            out_ref[...] = jnp.where(head == h, acc * inv, out_ref[...])

    attended = out_ref[...]
    att_ref[...] = attended
    attended_b = attended.astype(BF16)
    for c in range(pieces):
        part = dot(attended_b, gout_ref[c], TN).astype(BF16)
        n = width // HD
        sums_ref[c * n:(c + 1) * n, 0:HD, :] = part.reshape(n, HD, 128)

    product = gatt_b.astype(F32) * attended
    query_t = query.astype(F32).T.astype(BF16)
    gatt_t = gatt_b.astype(F32).T.astype(BF16)
    for h in range(nheads):
        gatt_h = jnp.where(head == h, gatt_b, jnp.zeros_like(gatt_b))
        row_dot = jnp.sum(jnp.where(head == h, product, 0.0), axis=1, keepdims=True)
        stats = jnp.where(lane == nheads + h, row_dot, stats)
        inv = inverse[h]
        qt = query_t[h * HD:(h + 1) * HD]
        gt = gatt_t[h * HD:(h + 1) * HD]
        acc = jnp.zeros((length, width), F32)
        for g in range(NGLOB):
            b = count - NGLOB + g
            weights = score_ref[h, :, b * length:(b + 1) * length] * inv
            gw = dot(gatt_h, vals[b], NT)
            gs = (weights * (gw - row_dot)).astype(BF16)
            acc = acc + dot(gs, keys[b], NN)
            gk = dot(qt, gs, NN) * scaling
            gv = dot(gt, weights.astype(BF16), NN)
            for a in range(length // 128):
                at = (g * (length // 128) + a) * 2 * nheads + h
                cols = slice(a * 128, (a + 1) * 128)
                sums_ref[at, HD:2 * HD, :] = gk[:, cols].astype(BF16)
                sums_ref[at + nheads, HD:2 * HD, :] = gv[:, cols].astype(BF16)
        if h == 0:
            out_ref[...] = acc
        else:
            out_ref[...] = jnp.where(head == h, acc, out_ref[...])
    stats_ref[...] = stats
    gquery_ref[...] = out_ref[...]


def backward_kernel(
    pos_ref, pair_ref, own_ref, p0, p1, p2, p3, p4, stats_ref, gatt_ref, gglob_ref,
    r0, r1, r2, r3, r4, gquery_ref, gown_ref,
):
    length = own_ref.shape[0] // 2
    width = own_ref.shape[1]
    nheads = width // HD
    scaling = 1.0 / math.sqrt(HD)
    base2 = scaling / math.log(2.0)
    bias = block_bias(pos_ref, pair_ref)
    query = own_ref[:length]
    gatt_b = gatt_ref[...]
    head = lax.broadcasted_iota(jnp.int32, (1, width), 1) // HD
    query_t = query.astype(F32).T.astype(BF16)
    gatt_t = gatt_b.astype(F32).T.astype(BF16)
    blocks = (own_ref, p0, p1, p2, p3, p4)
    outs = (gown_ref, r0, r1, r2, r3, r4)
    result = gglob_ref[...]
    for h in range(nheads):
        query_h = jnp.where(head == h, query, jnp.zeros_like(query))
        gatt_h = jnp.where(head == h, gatt_b, jnp.zeros_like(gatt_b))
        log_total = stats_ref[:, h:h + 1]
        row_dot = stats_ref[:, nheads + h:nheads + h + 1]
        qt = query_t[h * HD:(h + 1) * HD]
        gt = gatt_t[h * HD:(h + 1) * HD]
        acc = jnp.zeros((length, width), F32)
        for b in (1, 2, 3, 4, 5, 0):
            keys = blocks[b][:length]
            s = dot(query_h, keys, NT) * base2 + (bias[b] - log_total)
            weights = jnp.exp2(s)
            gw = dot(gatt_h, blocks[b][length:], NT)
            gs = (weights * (gw - row_dot)).astype(BF16)
            acc = acc + dot(gs, keys, NN)
            gk = dot(qt, gs, NN) * scaling
            gv = dot(gt, weights.astype(BF16), NN)
            o = outs[b]
            o[h * HD:(h + 1) * HD, :] = gk.astype(o.dtype)
            o[width + h * HD:width + (h + 1) * HD, :] = gv.astype(o.dtype)
        result = result + jnp.where(head == h, acc, 0.0)
    gquery_ref[...] = result * scaling


def project_kernel(att_ref, w_ref, projected_ref):
    projected = jnp.zeros(projected_ref.shape, F32)
    for c in range(att_ref.shape[0]):
        projected = projected + dot(att_ref[c].astype(BF16), w_ref[c], NN)
    projected_ref[...] = projected.astype(BF16)


def finish_kernel(
    pos_ref, ids_ref, b0, b1, b2, b3, b4, gown_ref, gquery_ref, total_ref,
    gqk_ref, gval_ref, gweight_ref,
):
    length, width = gquery_ref.shape
    halves = length // 128
    rows = width * 2 // HD
    for a in range(halves):
        cols = slice(a * 128, (a + 1) * 128)
        acc = gown_ref[:, cols]
        for b in (b0, b1, b2, b3, b4):
            acc = acc + b[:, cols].astype(F32)
        for g in range(NGLOB):
            at = (g * halves + a) * rows
            term = total_ref[at:at + rows, HD:2 * HD, :].reshape(2 * width, 128).astype(F32)
            acc = acc + jnp.where(ids_ref[g] == pos_ref[0], term, 0.0)
        tokens = slice(a * 128, (a + 1) * 128)
        gqk_ref[tokens, :] = (gquery_ref[tokens, :] + acc[:width].T).astype(BF16)
        gval_ref[tokens, :] = acc[width:].T.astype(BF16)
    n = width // HD
    for c in range(gweight_ref.shape[1] // 128):
        piece = total_ref[c * n:(c + 1) * n, 0:HD, :].reshape(width, 128)
        gweight_ref[:, c * 128:(c + 1) * 128] = piece.astype(F32)


def copy_all(copies):
    for copy in copies:
        copy.start()
    for copy in copies:
        copy.wait()


def pack_kernel(qk_ref, val_ref, gout_ref, w_ref, joined_ref, share_ref, sems):
    length = qk_ref.shape[0]
    blocks = length // 128
    pairs = [
        (qk_ref, joined_ref.at[pl.ds(0, length)]),
        (val_ref, joined_ref.at[pl.ds(length, length)]),
    ]
    for b in range(blocks):
        pairs.append((gout_ref.at[pl.ds(b * 128, 128)], share_ref.at[b]))
    for c in range(w_ref.shape[1] // 128):
        pairs.append((w_ref.at[:, pl.ds(c * 128, 128)], share_ref.at[blocks + c]))
    copy_all([pltpu.make_async_copy(a, b, sems.at[n]) for n, (a, b) in enumerate(pairs)])


def pick_kernel(ids_ref, slices_ref, out_ref, sems):
    count = out_ref.shape[0]
    copies = []
    for g in range(NGLOB):
        chosen = slices_ref.at[lax.rem(ids_ref[g], PATCH)]
        for n in range(count):
            sem = sems.at[g * count + n]
            copies.append(pltpu.make_async_copy(chosen, out_ref.at[n, g], sem))
    copy_all(copies)


def spread_kernel(ids_ref, slices_ref, out_ref, sems):
    count = out_ref.shape[0]
    copies = []
    for g in range(NGLOB):
        chosen = slices_ref.at[lax.div(ids_ref[g], PATCH), g]
        for n in range(count):
            sem = sems.at[g * count + n]
            copies.append(pltpu.make_async_copy(chosen, out_ref.at[n, g], sem))
    copy_all(copies)


def anywhere():
    return pl.BlockSpec(memory_space=pl.ANY)


def limit(mebibytes):
    return pltpu.CompilerParams(vmem_limit_bytes=mebibytes * 1024 * 1024)


def vmem(count):
    return [pl.BlockSpec(memory_space=pltpu.VMEM)] * count


def smem():
    return pl.BlockSpec(memory_space=pltpu.SMEM)


def local(qk_vectors, token_values, grad_output, out_weight, global_ids, pair_active):
    length, width = qk_vectors.shape
    devices = lax.axis_size(CTX)
    pieces = lax.axis_size(HEAD)
    position = lax.axis_index(CTX)
    joined = jnp.concatenate([qk_vectors, token_values], axis=0)

    his, los = lax.axis_size("hi"), lax.axis_size("lo")
    step = 2 * length // los
    joined, share = pl.pallas_call(
        pack_kernel,
        out_shape=(
            jax.ShapeDtypeStruct((2 * length, width), BF16),
            jax.ShapeDtypeStruct((length // 128 + pieces, 128, width), BF16),
        ),
        in_specs=[anywhere()] * 4,
        out_specs=(anywhere(), anywhere()),
        scratch_shapes=[pltpu.SemaphoreType.DMA((2 + length // 128 + pieces,))],
        name="pack",
    )(qk_vectors, token_values, grad_output, out_weight)

    slices = lax.all_to_all(joined.reshape(los, step, width), "lo", 0, 0)
    portion = lax.all_gather(share, HEAD, axis=0)
    routes = [[(i, i ^ 1) for i in range(devices)]]
    other = [i + 1 if i % 2 else i - 1 for i in range(devices)]
    routes.append([(i, j) for i, j in enumerate(other) if 0 <= j < devices])
    routes += [[(i, i ^ (1 << k)) for i in range(devices)] for k in range(1, ROUNDS)]
    received = [None] * len(routes)
    for n in (0, 2):
        received[n] = lax.ppermute(joined, CTX, routes[n])
    slices, received[0] = lax.optimization_barrier((slices, received[0]))
    picked = pl.pallas_call(
        pick_kernel,
        out_shape=jax.ShapeDtypeStruct((his, NGLOB, step, width), BF16),
        in_specs=[smem(), anywhere()],
        out_specs=anywhere(),
        scratch_shapes=[pltpu.SemaphoreType.DMA((NGLOB * his,))],
        compiler_params=limit(1),
        name="pick",
    )(global_ids, slices)
    picked, joined_late, received[2] = lax.optimization_barrier((picked, joined, received[2]))
    column = lax.all_to_all(picked, "hi", 0, 0)
    for n in (4, 3):
        received[n] = lax.ppermute(joined_late, CTX, routes[n])
    portion_b, gatt, weight_cols = pl.pallas_call(
        cotangent_kernel,
        out_shape=(
            jax.ShapeDtypeStruct((pieces, length, width), BF16),
            jax.ShapeDtypeStruct((length, width), BF16),
            jax.ShapeDtypeStruct((pieces, width, 128), BF16),
        ),
        in_specs=[smem()] + vmem(2),
        out_specs=tuple(vmem(3)),
        compiler_params=limit(8),
        cost_estimate=pl.CostEstimate(
            flops=600_000_000, bytes_accessed=4_000_000, transcendentals=0
        ),
        name="cotangent",
    )(lax.axis_index(HEAD)[None], portion, out_weight)
    column, received[4], portion_b, gatt, weight_cols = lax.optimization_barrier(
        (column, received[4], portion_b, gatt, weight_cols)
    )
    chosen = pl.pallas_call(
        spread_kernel,
        out_shape=jax.ShapeDtypeStruct((los, NGLOB, step, width), BF16),
        in_specs=[smem(), anywhere()],
        out_specs=anywhere(),
        scratch_shapes=[pltpu.SemaphoreType.DMA((NGLOB * los,))],
        compiler_params=limit(1),
        name="spread",
    )(global_ids, column)
    chosen, joined_late, received[3] = lax.optimization_barrier((chosen, joined, received[3]))
    globals_all = lax.all_to_all(chosen, "lo", 0, 0)
    received[1] = lax.ppermute(joined_late, CTX, routes[1])
    nheads = width // HD
    block = jax.ShapeDtypeStruct((2 * width, length), BF16)
    square = jax.ShapeDtypeStruct((length, width), F32)
    near_stats, near_sum = pl.pallas_call(
        near_kernel,
        out_shape=(square, square),
        in_specs=[smem()] * 2 + vmem(5),
        out_specs=tuple(vmem(2)),
        scratch_shapes=[pltpu.VMEM((length, 5 * length), F32)],
        compiler_params=limit(12),
        cost_estimate=pl.CostEstimate(
            flops=1_000_000_000, bytes_accessed=1_000_000, transcendentals=650_000
        ),
        name="near",
    )(position[None], pair_active, joined, received[0], *received[2:])
    globals_all, near_stats, near_sum = lax.optimization_barrier(
        (globals_all, near_stats, near_sum)
    )
    attended, sums, stats, gglob = pl.pallas_call(
        forward_kernel,
        out_shape=(
            square,
            jax.ShapeDtypeStruct((los, 2 * HD, 128), BF16),
            square,
            square,
        ),
        in_specs=[smem()] * 2 + vmem(7),
        out_specs=tuple(vmem(4)),
        scratch_shapes=[
            pltpu.VMEM((nheads, length, (1 + NGLOB) * length), F32),
            pltpu.VMEM((length, width), F32),
        ],
        compiler_params=limit(20),
        cost_estimate=pl.CostEstimate(
            flops=3_000_000_000, bytes_accessed=4_000_000, transcendentals=1_100_000
        ),
        name="forward",
    )(
        position[None], pair_active, joined, received[1], near_stats, near_sum,
        globals_all, portion_b, gatt,
    )

    shares = lax.all_to_all(sums, "lo", 0, 0)
    attended_all = lax.all_gather(attended, HEAD, axis=0)
    *terms, gquery, gown = pl.pallas_call(
        backward_kernel,
        out_shape=(
            block, block, block, block, block,
            square,
            jax.ShapeDtypeStruct((2 * width, length), F32),
        ),
        in_specs=[smem()] * 2 + vmem(9),
        out_specs=tuple(vmem(7)),
        compiler_params=limit(10),
        cost_estimate=pl.CostEstimate(
            flops=3_000_000_000, bytes_accessed=4_000_000, transcendentals=800_000
        ),
        name="backward",
    )(position[None], pair_active, joined, *received, stats, gatt, gglob)
    returned = [None] * len(routes)
    returned[0] = lax.ppermute(terms[0], CTX, routes[0])
    shares, *terms = lax.optimization_barrier((shares, *terms))
    share = jnp.sum(shares.astype(F32), axis=0).astype(BF16)
    share, returned[0] = lax.optimization_barrier((share, returned[0]))
    column = lax.all_to_all(jnp.broadcast_to(share[None], (his,) + share.shape), "hi", 0, 0)
    for n in (4, 2, 3, 1):
        returned[n] = lax.ppermute(terms[n], CTX, routes[n])
    column, returned[4], returned[2] = lax.optimization_barrier((column, returned[4], returned[2]))
    share = jnp.sum(column.astype(F32), axis=0).astype(BF16)
    share, attended_all = lax.optimization_barrier((share, attended_all))
    totals = lax.all_to_all(jnp.broadcast_to(share[None], (los,) + share.shape), "lo", 0, 0)

    projected = pl.pallas_call(
        project_kernel,
        out_shape=jax.ShapeDtypeStruct((length, width), BF16),
        in_specs=vmem(2),
        out_specs=vmem(1)[0],
        compiler_params=limit(4),
        cost_estimate=pl.CostEstimate(
            flops=70_000_000, bytes_accessed=1_500_000, transcendentals=0
        ),
        name="project",
    )(attended_all, weight_cols)
    gqk, gval, gweight = pl.pallas_call(
        finish_kernel,
        out_shape=(
            jax.ShapeDtypeStruct((length, width), BF16),
            jax.ShapeDtypeStruct((length, width), BF16),
            jax.ShapeDtypeStruct((width, pieces * 128), F32),
        ),
        in_specs=[smem()] * 2 + vmem(8),
        out_specs=tuple(vmem(3)),
        compiler_params=limit(6),
        cost_estimate=pl.CostEstimate(
            flops=2_000_000, bytes_accessed=2_500_000, transcendentals=0
        ),
        name="finish",
    )(position[None], global_ids, *returned, gown, gquery, totals)
    return (projected, gqk, gval, gweight)


def solution(mesh):
    ctx, head = mesh.devices.shape
    inner = Mesh(mesh.devices.reshape(ctx // PATCH, PATCH, head), CTX + (HEAD,))
    row = P(CTX, HEAD)
    return jax.shard_map(
        local,
        mesh=inner,
        in_specs=(row, row, row, P(HEAD, None), P(), P()),
        out_specs=(row, row, row, P(HEAD, None)),
        check_vma=False,
    )
```

```python
import functools
import math

import jax
import jax.numpy as jnp
from jax import lax
from jax.experimental import pallas as pl
from jax.experimental.pallas import tpu as pltpu
from jax.sharding import Mesh, PartitionSpec as P

HD = 64
NGLOB = 2
ROUNDS = 4
CTX = ("hi", "lo")
HEAD = "head"
PATCH = 16
NT = (((1,), (1,)), ((), ()))
NN = (((1,), (0,)), ((), ()))
F32 = jnp.float32
BF16 = jnp.bfloat16
MASKED = -1e30


def dot(a, b, dims):
    return lax.dot_general(a, b, dims, preferred_element_type=F32)


def block_bias(pos_ref, pair_ref):
    position = pos_ref[0]
    devices = 2 * pair_ref.shape[1]
    linked = []
    for k in range(ROUNDS):
        stride = 1 << k
        lowest = jnp.bitwise_and(position, devices - 1 - stride)
        slot = jnp.right_shift(lowest, k + 1) * stride + jnp.bitwise_and(lowest, stride - 1)
        linked.append(pair_ref[k, slot] == 1)
    inside = jnp.logical_and(position > 0, position < devices - 1)
    zero = jnp.float32(0.0)
    bias = [zero, jnp.where(linked[0], jnp.float32(1.0), zero)]
    bias += [jnp.where(m, zero, jnp.float32(MASKED)) for m in [inside] + linked[1:]]
    return bias + [zero] * NGLOB


def cotangent_kernel(head_ref, all_ref, w_ref, out_ref, gatt_ref, cols_ref):
    pieces, length, width = out_ref.shape
    blocks = length // 128
    gatt = jnp.zeros((length, width), F32)
    for c in range(pieces):
        part = all_ref[c, 0:blocks].reshape(length, width)
        out_ref[c] = part
        gatt = gatt + dot(part, w_ref[:, c * width:(c + 1) * width], NT)
        cols_ref[c] = all_ref[c, blocks + head_ref[0]]
    gatt_ref[...] = gatt.astype(BF16)


def near_kernel(
    pos_ref, pair_ref, own_ref, p0, p2, p3, p4, stats_ref, sum_ref, score_ref,
):
    length = own_ref.shape[0] // 2
    width = own_ref.shape[1]
    nheads = width // HD
    base2 = 1.0 / math.sqrt(HD) / math.log(2.0)
    bias = block_bias(pos_ref, pair_ref)
    blocks = ((own_ref, bias[0]), (p0, bias[1]), (p2, bias[3]), (p3, bias[4]), (p4, bias[5]))
    query = own_ref[:length]
    lane = lax.broadcasted_iota(jnp.int32, (1, width), 1)
    head = lane // HD
    stats = jnp.zeros((length, width), F32)
    for h in range(nheads):
        query_h = jnp.where(head == h, query, jnp.zeros_like(query))
        highest = jnp.full((length, 1), MASKED, F32)
        for b, (ref, shift) in enumerate(blocks):
            s = dot(query_h, ref[:length], NT) * base2 + shift
            score_ref[:, b * length:(b + 1) * length] = s
            highest = jnp.maximum(highest, jnp.max(s, axis=1, keepdims=True))
        total = jnp.zeros((length, 1), F32)
        acc = jnp.zeros((length, width), F32)
        for b, (ref, _) in enumerate(blocks):
            e = jnp.exp2(score_ref[:, b * length:(b + 1) * length] - highest)
            total = total + jnp.sum(e, axis=1, keepdims=True)
            acc = acc + dot(e.astype(BF16), ref[length:], NN)
        stats = jnp.where(lane == h, highest, stats)
        stats = jnp.where(lane == nheads + h, total, stats)
        if h == 0:
            sum_ref[...] = acc
        else:
            sum_ref[...] = jnp.where(head == h, acc, sum_ref[...])
    stats_ref[...] = stats


def forward_kernel(
    pos_ref, pair_ref, own_ref, p1, near_ref, sum_ref, glob_ref, gout_ref, gatt_ref,
    att_ref, sums_ref, stats_ref, gquery_ref,
    score_ref, out_ref,
):
    length = own_ref.shape[0] // 2
    width = own_ref.shape[1]
    pieces = gout_ref.shape[0]
    nheads = width // HD
    scaling = 1.0 / math.sqrt(HD)
    base2 = scaling / math.log(2.0)
    bias = block_bias(pos_ref, pair_ref)
    bias = [bias[2]] + bias[-NGLOB:]
    keys = [p1[:length]]
    vals = [p1[length:]]
    half = glob_ref.shape[0] // 2
    for g in range(NGLOB):
        keys.append(jnp.concatenate([glob_ref[p, g] for p in range(half)], axis=0))
        vals.append(jnp.concatenate([glob_ref[half + p, g] for p in range(half)], axis=0))
    count = len(keys)
    query = own_ref[:length]
    lane = lax.broadcasted_iota(jnp.int32, (1, width), 1)
    head = lane // HD
    gatt_b = gatt_ref[...]

    inverse = []
    stats = jnp.zeros((length, width), F32)
    for h in range(nheads):
        query_h = jnp.where(head == h, query, jnp.zeros_like(query))
        near = near_ref[:, h:h + 1]
        highest = near
        for b in range(count):
            s = dot(query_h, keys[b], NT) * base2 + bias[b]
            score_ref[h, :, b * length:(b + 1) * length] = s
            highest = jnp.maximum(highest, jnp.max(s, axis=1, keepdims=True))
        factor = jnp.exp2(near - highest)
        total = near_ref[:, nheads + h:nheads + h + 1] * factor
        acc = sum_ref[...] * factor
        for b in range(count):
            e = jnp.exp2(score_ref[h, :, b * length:(b + 1) * length] - highest)
            score_ref[h, :, b * length:(b + 1) * length] = e
            total = total + jnp.sum(e, axis=1, keepdims=True)
            acc = acc + dot(e.astype(BF16), vals[b], NN)
        inv = 1.0 / total
        inverse.append(inv)
        stats = jnp.where(lane == h, highest + jnp.log2(total), stats)
        if h == 0:
            out_ref[...] = acc * inv
        else:
            out_ref[...] = jnp.where(head == h, acc * inv, out_ref[...])

    attended = out_ref[...]
    att_ref[...] = attended
    attended_t = attended.T.astype(BF16)
    for c in range(pieces):
        part = dot(attended_t, gout_ref[c], NN).astype(BF16)
        n = width // HD
        sums_ref[c * n:(c + 1) * n, 0:HD, :] = part.reshape(n, HD, 128)

    product = gatt_b.astype(F32) * attended
    query_t = query.astype(F32).T.astype(BF16)
    gatt_t = gatt_b.astype(F32).T.astype(BF16)
    for h in range(nheads):
        gatt_h = jnp.where(head == h, gatt_b, jnp.zeros_like(gatt_b))
        row_dot = jnp.sum(jnp.where(head == h, product, 0.0), axis=1, keepdims=True)
        stats = jnp.where(lane == nheads + h, row_dot, stats)
        inv = inverse[h]
        qt = query_t[h * HD:(h + 1) * HD]
        gt = gatt_t[h * HD:(h + 1) * HD]
        acc = jnp.zeros((length, width), F32)
        for g in range(NGLOB):
            b = count - NGLOB + g
            weights = score_ref[h, :, b * length:(b + 1) * length] * inv
            gw = dot(gatt_h, vals[b], NT)
            gs = (weights * (gw - row_dot)).astype(BF16)
            acc = acc + dot(gs, keys[b], NN)
            gk = dot(qt, gs, NN) * scaling
            gv = dot(gt, weights.astype(BF16), NN)
            for a in range(length // 128):
                at = (g * (length // 128) + a) * 2 * nheads + h
                cols = slice(a * 128, (a + 1) * 128)
                sums_ref[at, HD:2 * HD, :] = gk[:, cols].astype(BF16)
                sums_ref[at + nheads, HD:2 * HD, :] = gv[:, cols].astype(BF16)
        if h == 0:
            out_ref[...] = acc
        else:
            out_ref[...] = jnp.where(head == h, acc, out_ref[...])
    stats_ref[...] = stats
    gquery_ref[...] = out_ref[...]


def backward_kernel(
    pos_ref, pair_ref, own_ref, p0, p1, p2, p3, p4, stats_ref, gatt_ref, gglob_ref,
    r0, r1, r2, r3, r4, gquery_ref, gown_ref,
):
    length = own_ref.shape[0] // 2
    width = own_ref.shape[1]
    nheads = width // HD
    scaling = 1.0 / math.sqrt(HD)
    base2 = scaling / math.log(2.0)
    bias = block_bias(pos_ref, pair_ref)
    query = own_ref[:length]
    gatt_b = gatt_ref[...]
    head = lax.broadcasted_iota(jnp.int32, (1, width), 1) // HD
    query_t = query.astype(F32).T.astype(BF16)
    gatt_t = gatt_b.astype(F32).T.astype(BF16)
    blocks = (own_ref, p0, p1, p2, p3, p4)
    outs = (gown_ref, r0, r1, r2, r3, r4)
    result = gglob_ref[...]
    for h in range(nheads):
        query_h = jnp.where(head == h, query, jnp.zeros_like(query))
        gatt_h = jnp.where(head == h, gatt_b, jnp.zeros_like(gatt_b))
        log_total = stats_ref[:, h:h + 1]
        row_dot = stats_ref[:, nheads + h:nheads + h + 1]
        qt = query_t[h * HD:(h + 1) * HD]
        gt = gatt_t[h * HD:(h + 1) * HD]
        acc = jnp.zeros((length, width), F32)
        for b in (1, 2, 3, 4, 5, 0):
            keys = blocks[b][:length]
            s = dot(query_h, keys, NT) * base2 + (bias[b] - log_total)
            weights = jnp.exp2(s)
            gw = dot(gatt_h, blocks[b][length:], NT)
            gs = (weights * (gw - row_dot)).astype(BF16)
            acc = acc + dot(gs, keys, NN)
            gk = dot(qt, gs, NN) * scaling
            gv = dot(gt, weights.astype(BF16), NN)
            o = outs[b]
            o[h * HD:(h + 1) * HD, :] = gk.astype(o.dtype)
            o[width + h * HD:width + (h + 1) * HD, :] = gv.astype(o.dtype)
        result = result + jnp.where(head == h, acc, 0.0)
    gquery_ref[...] = result * scaling


def project_kernel(att_ref, w_ref, projected_ref):
    projected = jnp.zeros(projected_ref.shape, F32)
    for c in range(att_ref.shape[0]):
        projected = projected + dot(att_ref[c].astype(BF16), w_ref[c], NN)
    projected_ref[...] = projected.astype(BF16)


def finish_kernel(
    pos_ref, ids_ref, b0, b1, b2, b3, b4, gown_ref, gquery_ref, total_ref,
    gqk_ref, gval_ref, gweight_ref,
):
    length, width = gquery_ref.shape
    halves = length // 128
    rows = width * 2 // HD
    for a in range(halves):
        cols = slice(a * 128, (a + 1) * 128)
        acc = gown_ref[:, cols]
        for b in (b0, b1, b2, b3, b4):
            acc = acc + b[:, cols].astype(F32)
        for g in range(NGLOB):
            at = (g * halves + a) * rows
            term = total_ref[at:at + rows, HD:2 * HD, :].reshape(2 * width, 128).astype(F32)
            acc = acc + jnp.where(ids_ref[g] == pos_ref[0], term, 0.0)
        tokens = slice(a * 128, (a + 1) * 128)
        gqk_ref[tokens, :] = (gquery_ref[tokens, :] + acc[:width].T).astype(BF16)
        gval_ref[tokens, :] = acc[width:].T.astype(BF16)
    n = width // HD
    for c in range(gweight_ref.shape[1] // 128):
        piece = total_ref[c * n:(c + 1) * n, 0:HD, :].reshape(width, 128)
        gweight_ref[:, c * 128:(c + 1) * 128] = piece.astype(F32)


def copy_all(copies):
    for copy in copies:
        copy.start()
    for copy in copies:
        copy.wait()


def pack_kernel(qk_ref, val_ref, gout_ref, w_ref, joined_ref, share_ref):
    length, width = qk_ref.shape
    blocks = length // 128
    joined_ref[:length] = qk_ref[...]
    joined_ref[length:] = val_ref[...]
    share_ref[0:blocks] = gout_ref[...].reshape(blocks, 128, width)
    for c in range(w_ref.shape[1] // 128):
        share_ref[blocks + c] = w_ref[:, c * 128:(c + 1) * 128]


def pick_kernel(ids_ref, slices_ref, out_ref, sems):
    count = out_ref.shape[0]
    copies = []
    for g in range(NGLOB):
        chosen = slices_ref.at[lax.rem(ids_ref[g], PATCH)]
        for n in range(count):
            sem = sems.at[g * count + n]
            copies.append(pltpu.make_async_copy(chosen, out_ref.at[n, g], sem))
    copy_all(copies)


def spread_kernel(ids_ref, slices_ref, out_ref, sems):
    count = out_ref.shape[0]
    copies = []
    for g in range(NGLOB):
        chosen = slices_ref.at[lax.div(ids_ref[g], PATCH), g]
        for n in range(count):
            sem = sems.at[g * count + n]
            copies.append(pltpu.make_async_copy(chosen, out_ref.at[n, g], sem))
    copy_all(copies)


def anywhere():
    return pl.BlockSpec(memory_space=pl.ANY)


def limit(mebibytes):
    return pltpu.CompilerParams(vmem_limit_bytes=mebibytes * 1024 * 1024)


def vmem(count):
    return [pl.BlockSpec(memory_space=pltpu.VMEM)] * count


def smem():
    return pl.BlockSpec(memory_space=pltpu.SMEM)


def local(qk_vectors, token_values, grad_output, out_weight, global_ids, pair_active):
    length, width = qk_vectors.shape
    devices = lax.axis_size(CTX)
    pieces = lax.axis_size(HEAD)
    position = lax.axis_index(CTX)
    joined = jnp.concatenate([qk_vectors, token_values], axis=0)

    his, los = lax.axis_size("hi"), lax.axis_size("lo")
    step = 2 * length // los
    joined, share = pl.pallas_call(
        pack_kernel,
        out_shape=(
            jax.ShapeDtypeStruct((2 * length, width), BF16),
            jax.ShapeDtypeStruct((length // 128 + pieces, 128, width), BF16),
        ),
        in_specs=vmem(4),
        out_specs=tuple(vmem(2)),
        name="pack",
    )(qk_vectors, token_values, grad_output, out_weight)

    slices = lax.all_to_all(joined.reshape(los, step, width), "lo", 0, 0)
    portion = lax.all_gather(share, HEAD, axis=0)
    routes = [[(i, i ^ 1) for i in range(devices)]]
    other = [i + 1 if i % 2 else i - 1 for i in range(devices)]
    routes.append([(i, j) for i, j in enumerate(other) if 0 <= j < devices])
    routes += [[(i, i ^ (1 << k)) for i in range(devices)] for k in range(1, ROUNDS)]
    received = [None] * len(routes)
    for n in (4, 0):
        received[n] = lax.ppermute(joined, CTX, routes[n])
    picked = pl.pallas_call(
        pick_kernel,
        out_shape=jax.ShapeDtypeStruct((his, NGLOB, step, width), BF16),
        in_specs=[smem(), anywhere()],
        out_specs=anywhere(),
        scratch_shapes=[pltpu.SemaphoreType.DMA((NGLOB * his,))],
        compiler_params=limit(1),
        name="pick",
    )(global_ids, slices)
    picked, joined_late, received[4], received[0] = lax.optimization_barrier(
        (picked, joined, received[4], received[0])
    )
    column = lax.all_to_all(picked, "hi", 0, 0)
    for n in (3, 2):
        received[n] = lax.ppermute(joined_late, CTX, routes[n])
    portion_b, gatt, weight_cols = pl.pallas_call(
        cotangent_kernel,
        out_shape=(
            jax.ShapeDtypeStruct((pieces, length, width), BF16),
            jax.ShapeDtypeStruct((length, width), BF16),
            jax.ShapeDtypeStruct((pieces, width, 128), BF16),
        ),
        in_specs=[smem()] + vmem(2),
        out_specs=tuple(vmem(3)),
        compiler_params=limit(8),
        cost_estimate=pl.CostEstimate(
            flops=600_000_000, bytes_accessed=4_000_000, transcendentals=0
        ),
        name="cotangent",
    )(lax.axis_index(HEAD)[None], portion, out_weight)
    column, portion_b, gatt, weight_cols = lax.optimization_barrier(
        (column, portion_b, gatt, weight_cols)
    )
    chosen = pl.pallas_call(
        spread_kernel,
        out_shape=jax.ShapeDtypeStruct((los, NGLOB, step, width), BF16),
        in_specs=[smem(), anywhere()],
        out_specs=anywhere(),
        scratch_shapes=[pltpu.SemaphoreType.DMA((NGLOB * los,))],
        compiler_params=limit(1),
        name="spread",
    )(global_ids, column)
    chosen, joined_late, received[3], received[2] = lax.optimization_barrier(
        (chosen, joined, received[3], received[2])
    )
    globals_all = lax.all_to_all(chosen, "lo", 0, 0)
    received[1] = lax.ppermute(joined_late, CTX, routes[1])
    nheads = width // HD
    block = jax.ShapeDtypeStruct((2 * width, length), BF16)
    square = jax.ShapeDtypeStruct((length, width), F32)
    near_stats, near_sum = pl.pallas_call(
        near_kernel,
        out_shape=(square, square),
        in_specs=[smem()] * 2 + vmem(5),
        out_specs=tuple(vmem(2)),
        scratch_shapes=[pltpu.VMEM((length, 5 * length), F32)],
        compiler_params=limit(12),
        cost_estimate=pl.CostEstimate(
            flops=1_000_000_000, bytes_accessed=1_000_000, transcendentals=650_000
        ),
        name="near",
    )(position[None], pair_active, joined, received[0], *received[2:])
    globals_all, near_stats, near_sum = lax.optimization_barrier(
        (globals_all, near_stats, near_sum)
    )
    attended, sums, stats, gglob = pl.pallas_call(
        forward_kernel,
        out_shape=(
            square,
            jax.ShapeDtypeStruct((los, 2 * HD, 128), BF16),
            square,
            square,
        ),
        in_specs=[smem()] * 2 + vmem(7),
        out_specs=tuple(vmem(4)),
        scratch_shapes=[
            pltpu.VMEM((nheads, length, (1 + NGLOB) * length), F32),
            pltpu.VMEM((length, width), F32),
        ],
        compiler_params=limit(20),
        cost_estimate=pl.CostEstimate(
            flops=3_000_000_000, bytes_accessed=4_000_000, transcendentals=1_100_000
        ),
        name="forward",
    )(
        position[None], pair_active, joined, received[1], near_stats, near_sum,
        globals_all, portion_b, gatt,
    )

    shares = lax.all_to_all(sums, "lo", 0, 0)
    attended_all = lax.all_gather(attended, HEAD, axis=0)
    *terms, gquery, gown = pl.pallas_call(
        backward_kernel,
        out_shape=(
            block, block, block, block, block,
            square,
            jax.ShapeDtypeStruct((2 * width, length), F32),
        ),
        in_specs=[smem()] * 2 + vmem(9),
        out_specs=tuple(vmem(7)),
        compiler_params=limit(10),
        cost_estimate=pl.CostEstimate(
            flops=1_000_000, bytes_accessed=10_000, transcendentals=0
        ),
        name="backward",
    )(position[None], pair_active, joined, *received, stats, gatt, gglob)
    returned = [None] * len(routes)
    returned[0] = lax.ppermute(terms[0], CTX, routes[0])
    shares, *terms = lax.optimization_barrier((shares, *terms))
    share = jnp.sum(shares.astype(F32), axis=0).astype(BF16)
    share, returned[0] = lax.optimization_barrier((share, returned[0]))
    column = lax.all_to_all(jnp.broadcast_to(share[None], (his,) + share.shape), "hi", 0, 0)
    for n in (4, 2, 3, 1):
        returned[n] = lax.ppermute(terms[n], CTX, routes[n])
    share = jnp.sum(column.astype(F32), axis=0).astype(BF16)
    share, returned[4], returned[2], attended_all = lax.optimization_barrier(
        (share, returned[4], returned[2], attended_all)
    )
    totals = lax.all_to_all(jnp.broadcast_to(share[None], (los,) + share.shape), "lo", 0, 0)

    projected = pl.pallas_call(
        project_kernel,
        out_shape=jax.ShapeDtypeStruct((length, width), BF16),
        in_specs=vmem(2),
        out_specs=vmem(1)[0],
        compiler_params=limit(4),
        cost_estimate=pl.CostEstimate(
            flops=70_000_000, bytes_accessed=1_500_000, transcendentals=0
        ),
        name="project",
    )(attended_all, weight_cols)
    totals, returned[3], returned[1] = lax.optimization_barrier(
        (totals, returned[3], returned[1])
    )
    gqk, gval, gweight = pl.pallas_call(
        finish_kernel,
        out_shape=(
            jax.ShapeDtypeStruct((length, width), BF16),
            jax.ShapeDtypeStruct((length, width), BF16),
            jax.ShapeDtypeStruct((width, pieces * 128), F32),
        ),
        in_specs=[smem()] * 2 + vmem(8),
        out_specs=tuple(vmem(3)),
        compiler_params=limit(6),
        cost_estimate=pl.CostEstimate(
            flops=2_000_000, bytes_accessed=2_500_000, transcendentals=0
        ),
        name="finish",
    )(position[None], global_ids, *returned, gown, gquery, totals)
    return (projected, gqk, gval, gweight)


def solution(mesh):
    ctx, head = mesh.devices.shape
    inner = Mesh(mesh.devices.reshape(ctx // PATCH, PATCH, head), CTX + (HEAD,))
    row = P(CTX, HEAD)
    return jax.shard_map(
        local,
        mesh=inner,
        in_specs=(row, row, row, P(HEAD, None), P(), P()),
        out_specs=(row, row, row, P(HEAD, None)),
        check_vma=False,
    )
```

```python
import functools
import math

import jax
import jax.numpy as jnp
from jax import lax
from jax.experimental import pallas as pl
from jax.experimental.pallas import tpu as pltpu
from jax.sharding import Mesh, PartitionSpec as P

HD = 64
NGLOB = 2
ROUNDS = 4
CTX = ("hi", "lo")
HEAD = "head"
PATCH = 16
NT = (((1,), (1,)), ((), ()))
NN = (((1,), (0,)), ((), ()))
TN = (((0,), (0,)), ((), ()))
F32 = jnp.float32
BF16 = jnp.bfloat16
MASKED = -1e30


def dot(a, b, dims):
    return lax.dot_general(a, b, dims, preferred_element_type=F32)


def block_bias(pos_ref, pair_ref):
    position = pos_ref[0]
    devices = 2 * pair_ref.shape[1]
    linked = []
    for k in range(ROUNDS):
        stride = 1 << k
        lowest = jnp.bitwise_and(position, devices - 1 - stride)
        slot = jnp.right_shift(lowest, k + 1) * stride + jnp.bitwise_and(lowest, stride - 1)
        linked.append(pair_ref[k, slot] == 1)
    inside = jnp.logical_and(position > 0, position < devices - 1)
    zero = jnp.float32(0.0)
    bias = [zero, jnp.where(linked[0], jnp.float32(1.0), zero)]
    bias += [jnp.where(m, zero, jnp.float32(MASKED)) for m in [inside] + linked[1:]]
    return bias + [zero] * NGLOB


def cotangent_kernel(head_ref, all_ref, w_hbm, out_ref, gatt_ref, cols_ref, w_ref, sems):
    pieces, length, width = out_ref.shape
    blocks = length // 128
    copies = [pltpu.make_async_copy(w_hbm, w_ref, sems.at[0])]
    for c in range(pieces):
        for b in range(blocks):
            copies.append(pltpu.make_async_copy(
                all_ref.at[c, b], out_ref.at[c, pl.ds(b * 128, 128)], sems.at[len(copies)]
            ))
    late = len(copies)
    for c in range(pieces):
        copies.append(pltpu.make_async_copy(
            all_ref.at[c, blocks + head_ref[0]], cols_ref.at[c], sems.at[len(copies)]
        ))
    for copy in copies:
        copy.start()
    for copy in copies[:late]:
        copy.wait()
    gatt = jnp.zeros((length, width), F32)
    for c in range(pieces):
        gatt = gatt + dot(out_ref[c], w_ref[:, c * width:(c + 1) * width], NT)
    gatt_ref[...] = gatt.astype(BF16)
    for copy in copies[late:]:
        copy.wait()


def near_kernel(
    pos_ref, pair_ref, own_ref, p0, p2, p3, p4, gatt_ref,
    stats_ref, sum_ref, turned_ref, score_ref,
):
    length = own_ref.shape[0] // 2
    width = own_ref.shape[1]
    nheads = width // HD
    base2 = 1.0 / math.sqrt(HD) / math.log(2.0)
    bias = block_bias(pos_ref, pair_ref)
    turned_ref[:width] = own_ref[:length].astype(F32).T.astype(BF16)
    turned_ref[width:] = gatt_ref[...].astype(F32).T.astype(BF16)
    blocks = ((own_ref, bias[0]), (p0, bias[1]), (p2, bias[3]), (p3, bias[4]), (p4, bias[5]))
    query = own_ref[:length]
    lane = lax.broadcasted_iota(jnp.int32, (1, width), 1)
    head = lane // HD
    stats = jnp.zeros((length, width), F32)
    for h in range(nheads):
        query_h = jnp.where(head == h, query, jnp.zeros_like(query))
        highest = jnp.full((length, 1), MASKED, F32)
        for b, (ref, shift) in enumerate(blocks):
            s = dot(query_h, ref[:length], NT) * base2 + shift
            score_ref[:, b * length:(b + 1) * length] = s
            highest = jnp.maximum(highest, jnp.max(s, axis=1, keepdims=True))
        total = jnp.zeros((length, 1), F32)
        acc = jnp.zeros((length, width), F32)
        for b, (ref, _) in enumerate(blocks):
            e = jnp.exp2(score_ref[:, b * length:(b + 1) * length] - highest)
            total = total + jnp.sum(e, axis=1, keepdims=True)
            acc = acc + dot(e.astype(BF16), ref[length:], NN)
        stats = jnp.where(lane == h, highest, stats)
        stats = jnp.where(lane == nheads + h, total, stats)
        if h == 0:
            sum_ref[...] = acc
        else:
            sum_ref[...] = jnp.where(head == h, acc, sum_ref[...])
    stats_ref[...] = stats


def forward_kernel(
    pos_ref, pair_ref, own_ref, p1, near_ref, sum_ref, turned_ref, glob_ref, gout_ref, gatt_ref,
    att_ref, sums_ref, stats_ref, gquery_ref,
    score_ref, out_ref,
):
    length = own_ref.shape[0] // 2
    width = own_ref.shape[1]
    pieces = gout_ref.shape[0]
    nheads = width // HD
    scaling = 1.0 / math.sqrt(HD)
    base2 = scaling / math.log(2.0)
    bias = block_bias(pos_ref, pair_ref)
    bias = [bias[2]] + bias[-NGLOB:]
    keys = [p1[:length]]
    vals = [p1[length:]]
    half = glob_ref.shape[0] // 2
    for g in range(NGLOB):
        keys.append(jnp.concatenate([glob_ref[p, g] for p in range(half)], axis=0))
        vals.append(jnp.concatenate([glob_ref[half + p, g] for p in range(half)], axis=0))
    count = len(keys)
    query = own_ref[:length]
    lane = lax.broadcasted_iota(jnp.int32, (1, width), 1)
    head = lane // HD
    gatt_b = gatt_ref[...]

    inverse = []
    stats = jnp.zeros((length, width), F32)
    for h in range(nheads):
        query_h = jnp.where(head == h, query, jnp.zeros_like(query))
        near = near_ref[:, h:h + 1]
        highest = near
        for b in range(count):
            s = dot(query_h, keys[b], NT) * base2 + bias[b]
            score_ref[h, :, b * length:(b + 1) * length] = s
            highest = jnp.maximum(highest, jnp.max(s, axis=1, keepdims=True))
        factor = jnp.exp2(near - highest)
        total = near_ref[:, nheads + h:nheads + h + 1] * factor
        acc = sum_ref[...] * factor
        for b in range(count):
            e = jnp.exp2(score_ref[h, :, b * length:(b + 1) * length] - highest)
            score_ref[h, :, b * length:(b + 1) * length] = e
            total = total + jnp.sum(e, axis=1, keepdims=True)
            acc = acc + dot(e.astype(BF16), vals[b], NN)
        inv = 1.0 / total
        inverse.append(inv)
        stats = jnp.where(lane == h, highest + jnp.log2(total), stats)
        if h == 0:
            out_ref[...] = acc * inv
        else:
            out_ref[...] = jnp.where(head == h, acc * inv, out_ref[...])

    attended = out_ref[...]
    att_ref[...] = attended
    attended_b = attended.astype(BF16)
    for c in range(pieces):
        part = dot(attended_b, gout_ref[c], TN).astype(BF16)
        n = width // HD
        sums_ref[c * n:(c + 1) * n, 0:HD, :] = part.reshape(n, HD, 128)

    product = gatt_b.astype(F32) * attended
    query_t = turned_ref[:width]
    gatt_t = turned_ref[width:]
    for h in range(nheads):
        gatt_h = jnp.where(head == h, gatt_b, jnp.zeros_like(gatt_b))
        row_dot = jnp.sum(jnp.where(head == h, product, 0.0), axis=1, keepdims=True)
        stats = jnp.where(lane == nheads + h, row_dot, stats)
        inv = inverse[h]
        qt = query_t[h * HD:(h + 1) * HD]
        gt = gatt_t[h * HD:(h + 1) * HD]
        acc = jnp.zeros((length, width), F32)
        for g in range(NGLOB):
            b = count - NGLOB + g
            weights = score_ref[h, :, b * length:(b + 1) * length] * inv
            gw = dot(gatt_h, vals[b], NT)
            gs = (weights * (gw - row_dot)).astype(BF16)
            acc = acc + dot(gs, keys[b], NN)
            gk = dot(qt, gs, NN) * scaling
            gv = dot(gt, weights.astype(BF16), NN)
            for a in range(length // 128):
                at = (g * (length // 128) + a) * 2 * nheads + h
                cols = slice(a * 128, (a + 1) * 128)
                sums_ref[at, HD:2 * HD, :] = gk[:, cols].astype(BF16)
                sums_ref[at + nheads, HD:2 * HD, :] = gv[:, cols].astype(BF16)
        if h == 0:
            out_ref[...] = acc
        else:
            out_ref[...] = jnp.where(head == h, acc, out_ref[...])
    stats_ref[...] = stats
    gquery_ref[...] = out_ref[...]


def backward_kernel(
    pos_ref, pair_ref, own_ref, p0, p1, p2, p3, p4, stats_ref, turned_ref, gatt_ref, gglob_ref,
    r0, r1, r2, r3, r4, gquery_ref, gown_ref,
):
    length = own_ref.shape[0] // 2
    width = own_ref.shape[1]
    nheads = width // HD
    scaling = 1.0 / math.sqrt(HD)
    base2 = scaling / math.log(2.0)
    bias = block_bias(pos_ref, pair_ref)
    query = own_ref[:length]
    gatt_b = gatt_ref[...]
    head = lax.broadcasted_iota(jnp.int32, (1, width), 1) // HD
    query_t = turned_ref[:width]
    gatt_t = turned_ref[width:]
    blocks = (own_ref, p0, p1, p2, p3, p4)
    outs = (gown_ref, r0, r1, r2, r3, r4)
    result = gglob_ref[...]
    for h in range(nheads):
        query_h = jnp.where(head == h, query, jnp.zeros_like(query))
        gatt_h = jnp.where(head == h, gatt_b, jnp.zeros_like(gatt_b))
        log_total = stats_ref[:, h:h + 1]
        row_dot = stats_ref[:, nheads + h:nheads + h + 1]
        qt = query_t[h * HD:(h + 1) * HD]
        gt = gatt_t[h * HD:(h + 1) * HD]
        acc = jnp.zeros((length, width), F32)
        for b in (1, 2, 3, 4, 5, 0):
            keys = blocks[b][:length]
            s = dot(query_h, keys, NT) * base2 + (bias[b] - log_total)
            weights = jnp.exp2(s)
            gw = dot(gatt_h, blocks[b][length:], NT)
            gs = (weights * (gw - row_dot)).astype(BF16)
            acc = acc + dot(gs, keys, NN)
            gk = dot(qt, gs, NN) * scaling
            gv = dot(gt, weights.astype(BF16), NN)
            o = outs[b]
            o[h * HD:(h + 1) * HD, :] = gk.astype(o.dtype)
            o[width + h * HD:width + (h + 1) * HD, :] = gv.astype(o.dtype)
        result = result + jnp.where(head == h, acc, 0.0)
    gquery_ref[...] = result * scaling


def project_kernel(att_ref, w_ref, projected_ref):
    projected = jnp.zeros(projected_ref.shape, F32)
    for c in range(att_ref.shape[0]):
        projected = projected + dot(att_ref[c].astype(BF16), w_ref[c], NN)
    projected_ref[...] = projected.astype(BF16)


def finish_kernel(
    pos_ref, ids_ref, b0, b1, b2, b3, b4, gown_ref, gquery_ref, total_ref,
    gqk_ref, gval_ref, gweight_ref,
):
    length, width = gquery_ref.shape
    halves = length // 128
    rows = width * 2 // HD
    for a in range(halves):
        cols = slice(a * 128, (a + 1) * 128)
        acc = gown_ref[:, cols]
        for b in (b0, b1, b2, b3, b4):
            acc = acc + b[:, cols].astype(F32)
        for g in range(NGLOB):
            at = (g * halves + a) * rows
            term = total_ref[at:at + rows, HD:2 * HD, :].reshape(2 * width, 128).astype(F32)
            acc = acc + jnp.where(ids_ref[g] == pos_ref[0], term, 0.0)
        tokens = slice(a * 128, (a + 1) * 128)
        gqk_ref[tokens, :] = (gquery_ref[tokens, :] + acc[:width].T).astype(BF16)
        gval_ref[tokens, :] = acc[width:].T.astype(BF16)
    n = width // HD
    for c in range(gweight_ref.shape[1] // 128):
        piece = total_ref[c * n:(c + 1) * n, 0:HD, :].reshape(width, 128)
        gweight_ref[:, c * 128:(c + 1) * 128] = piece.astype(F32)


def copy_all(copies):
    for copy in copies:
        copy.start()
    for copy in copies:
        copy.wait()


def pack_kernel(qk_ref, val_ref, gout_ref, w_ref, joined_ref, share_ref):
    length, width = qk_ref.shape
    blocks = length // 128
    joined_ref[:length] = qk_ref[...]
    joined_ref[length:] = val_ref[...]
    share_ref[0:blocks] = gout_ref[...].reshape(blocks, 128, width)
    for c in range(w_ref.shape[1] // 128):
        share_ref[blocks + c] = w_ref[:, c * 128:(c + 1) * 128]


def pick_kernel(ids_ref, slices_ref, out_ref, sems):
    count = out_ref.shape[0]
    copies = []
    for g in range(NGLOB):
        chosen = slices_ref.at[lax.rem(ids_ref[g], PATCH)]
        for n in range(count):
            sem = sems.at[g * count + n]
            copies.append(pltpu.make_async_copy(chosen, out_ref.at[n, g], sem))
    copy_all(copies)


def spread_kernel(ids_ref, slices_ref, out_ref, sems):
    count = out_ref.shape[0]
    copies = []
    for g in range(NGLOB):
        chosen = slices_ref.at[lax.div(ids_ref[g], PATCH), g]
        for n in range(count):
            sem = sems.at[g * count + n]
            copies.append(pltpu.make_async_copy(chosen, out_ref.at[n, g], sem))
    copy_all(copies)


def hbm():
    return pl.BlockSpec(memory_space=pltpu.HBM)


def anywhere():
    return pl.BlockSpec(memory_space=pl.ANY)


def limit(mebibytes):
    return pltpu.CompilerParams(vmem_limit_bytes=mebibytes * 1024 * 1024)


def vmem(count):
    return [pl.BlockSpec(memory_space=pltpu.VMEM)] * count


def smem():
    return pl.BlockSpec(memory_space=pltpu.SMEM)


def local(qk_vectors, token_values, grad_output, out_weight, global_ids, pair_active):
    length, width = qk_vectors.shape
    devices = lax.axis_size(CTX)
    pieces = lax.axis_size(HEAD)
    position = lax.axis_index(CTX)
    joined = jnp.concatenate([qk_vectors, token_values], axis=0)

    his, los = lax.axis_size("hi"), lax.axis_size("lo")
    step = 2 * length // los
    joined, share = pl.pallas_call(
        pack_kernel,
        out_shape=(
            jax.ShapeDtypeStruct((2 * length, width), BF16),
            jax.ShapeDtypeStruct((length // 128 + pieces, 128, width), BF16),
        ),
        in_specs=vmem(4),
        out_specs=tuple(vmem(2)),
        name="pack",
    )(qk_vectors, token_values, grad_output, out_weight)

    slices = lax.all_to_all(joined.reshape(los, step, width), "lo", 0, 0)
    portion = lax.all_gather(share, HEAD, axis=0)
    routes = [[(i, i ^ 1) for i in range(devices)]]
    other = [i + 1 if i % 2 else i - 1 for i in range(devices)]
    routes.append([(i, j) for i, j in enumerate(other) if 0 <= j < devices])
    routes += [[(i, i ^ (1 << k)) for i in range(devices)] for k in range(1, ROUNDS)]
    received = [None] * len(routes)
    for n in (4, 0):
        received[n] = lax.ppermute(joined, CTX, routes[n])
    picked = pl.pallas_call(
        pick_kernel,
        out_shape=jax.ShapeDtypeStruct((his, NGLOB, step, width), BF16),
        in_specs=[smem(), anywhere()],
        out_specs=anywhere(),
        scratch_shapes=[pltpu.SemaphoreType.DMA((NGLOB * his,))],
        compiler_params=limit(1),
        name="pick",
    )(global_ids, slices)
    picked, joined_late, received[4], received[0] = lax.optimization_barrier(
        (picked, joined, received[4], received[0])
    )
    column = lax.all_to_all(picked, "hi", 0, 0)
    for n in (3, 2):
        received[n] = lax.ppermute(joined_late, CTX, routes[n])
    portion_b, gatt, weight_cols = pl.pallas_call(
        cotangent_kernel,
        out_shape=(
            jax.ShapeDtypeStruct((pieces, length, width), BF16),
            jax.ShapeDtypeStruct((length, width), BF16),
            jax.ShapeDtypeStruct((pieces, width, 128), BF16),
        ),
        in_specs=[smem(), hbm(), hbm()],
        out_specs=tuple(vmem(3)),
        scratch_shapes=[
            pltpu.VMEM((width, pieces * width), BF16),
            pltpu.SemaphoreType.DMA((1 + pieces * (length // 128 + 1),)),
        ],
        compiler_params=limit(58),
        cost_estimate=pl.CostEstimate(
            flops=600_000_000, bytes_accessed=4_000_000, transcendentals=0
        ),
        name="cotangent",
    )(lax.axis_index(HEAD)[None], portion, out_weight)
    column, portion_b, gatt, weight_cols = lax.optimization_barrier(
        (column, portion_b, gatt, weight_cols)
    )
    chosen = pl.pallas_call(
        spread_kernel,
        out_shape=jax.ShapeDtypeStruct((los, NGLOB, step, width), BF16),
        in_specs=[smem(), anywhere()],
        out_specs=anywhere(),
        scratch_shapes=[pltpu.SemaphoreType.DMA((NGLOB * los,))],
        compiler_params=limit(1),
        name="spread",
    )(global_ids, column)
    chosen, joined_late, received[3], received[2] = lax.optimization_barrier(
        (chosen, joined, received[3], received[2])
    )
    globals_all = lax.all_to_all(chosen, "lo", 0, 0)
    received[1] = lax.ppermute(joined_late, CTX, routes[1])
    nheads = width // HD
    block = jax.ShapeDtypeStruct((2 * width, length), BF16)
    square = jax.ShapeDtypeStruct((length, width), F32)
    near_stats, near_sum, turned = pl.pallas_call(
        near_kernel,
        out_shape=(square, square, block),
        in_specs=[smem()] * 2 + vmem(6),
        out_specs=tuple(vmem(3)),
        scratch_shapes=[pltpu.VMEM((length, 5 * length), F32)],
        compiler_params=limit(12),
        cost_estimate=pl.CostEstimate(
            flops=1_000_000_000, bytes_accessed=1_000_000, transcendentals=650_000
        ),
        name="near",
    )(position[None], pair_active, joined, received[0], *received[2:], gatt)
    globals_all, near_stats, near_sum, turned = lax.optimization_barrier(
        (globals_all, near_stats, near_sum, turned)
    )
    attended, sums, stats, gglob = pl.pallas_call(
        forward_kernel,
        out_shape=(
            square,
            jax.ShapeDtypeStruct((los, 2 * HD, 128), BF16),
            square,
            square,
        ),
        in_specs=[smem()] * 2 + vmem(8),
        out_specs=tuple(vmem(4)),
        scratch_shapes=[
            pltpu.VMEM((nheads, length, (1 + NGLOB) * length), F32),
            pltpu.VMEM((length, width), F32),
        ],
        compiler_params=limit(20),
        cost_estimate=pl.CostEstimate(
            flops=3_000_000_000, bytes_accessed=4_000_000, transcendentals=1_100_000
        ),
        name="forward",
    )(
        position[None], pair_active, joined, received[1], near_stats, near_sum, turned,
        globals_all, portion_b, gatt,
    )

    shares = lax.all_to_all(sums, "lo", 0, 0)
    attended_all = lax.all_gather(attended, HEAD, axis=0)
    *terms, gquery, gown = pl.pallas_call(
        backward_kernel,
        out_shape=(
            block, block, block, block, block,
            square,
            jax.ShapeDtypeStruct((2 * width, length), F32),
        ),
        in_specs=[smem()] * 2 + vmem(10),
        out_specs=tuple(vmem(7)),
        compiler_params=limit(10),
        cost_estimate=pl.CostEstimate(
            flops=1_000_000, bytes_accessed=10_000, transcendentals=0
        ),
        name="backward",
    )(position[None], pair_active, joined, *received, stats, turned, gatt, gglob)
    returned = [None] * len(routes)
    for n in (1, 0):
        returned[n] = lax.ppermute(terms[n], CTX, routes[n])
    shares, *terms = lax.optimization_barrier((shares, *terms))
    share = jnp.sum(shares.astype(F32), axis=0).astype(BF16)
    share, returned[1], returned[0] = lax.optimization_barrier((share, returned[1], returned[0]))
    column = lax.all_to_all(jnp.broadcast_to(share[None], (his,) + share.shape), "hi", 0, 0)
    for n in (4, 2, 3):
        returned[n] = lax.ppermute(terms[n], CTX, routes[n])
    share = jnp.sum(column.astype(F32), axis=0).astype(BF16)
    share, returned[4], returned[2], attended_all = lax.optimization_barrier(
        (share, returned[4], returned[2], attended_all)
    )
    totals = lax.all_to_all(jnp.broadcast_to(share[None], (los,) + share.shape), "lo", 0, 0)

    projected = pl.pallas_call(
        project_kernel,
        out_shape=jax.ShapeDtypeStruct((length, width), BF16),
        in_specs=vmem(2),
        out_specs=vmem(1)[0],
        compiler_params=limit(4),
        cost_estimate=pl.CostEstimate(
            flops=70_000_000, bytes_accessed=1_500_000, transcendentals=0
        ),
        name="project",
    )(attended_all, weight_cols)
    gqk, gval, gweight = pl.pallas_call(
        finish_kernel,
        out_shape=(
            jax.ShapeDtypeStruct((length, width), BF16),
            jax.ShapeDtypeStruct((length, width), BF16),
            jax.ShapeDtypeStruct((width, pieces * 128), F32),
        ),
        in_specs=[smem()] * 2 + vmem(8),
        out_specs=tuple(vmem(3)),
        compiler_params=limit(6),
        cost_estimate=pl.CostEstimate(
            flops=2_000_000, bytes_accessed=2_500_000, transcendentals=0
        ),
        name="finish",
    )(position[None], global_ids, *returned, gown, gquery, totals)
    return (projected, gqk, gval, gweight)


def solution(mesh):
    ctx, head = mesh.devices.shape
    inner = Mesh(mesh.devices.reshape(ctx // PATCH, PATCH, head), CTX + (HEAD,))
    row = P(CTX, HEAD)
    return jax.shard_map(
        local,
        mesh=inner,
        in_specs=(row, row, row, P(HEAD, None), P(), P()),
        out_specs=(row, row, row, P(HEAD, None)),
        check_vma=False,
    )
```

```python
import functools
import math

import jax
import jax.numpy as jnp
from jax import lax
from jax.experimental import pallas as pl
from jax.experimental.pallas import tpu as pltpu
from jax.sharding import Mesh, PartitionSpec as P

HD = 64
NGLOB = 2
ROUNDS = 4
CTX = ("hi", "lo")
HEAD = "head"
PATCH = 16
NT = (((1,), (1,)), ((), ()))
NN = (((1,), (0,)), ((), ()))
TN = (((0,), (0,)), ((), ()))
F32 = jnp.float32
BF16 = jnp.bfloat16
MASKED = -1e30


def dot(a, b, dims):
    return lax.dot_general(a, b, dims, preferred_element_type=F32)


def block_bias(pos_ref, pair_ref):
    position = pos_ref[0]
    devices = 2 * pair_ref.shape[1]
    linked = []
    for k in range(ROUNDS):
        stride = 1 << k
        lowest = jnp.bitwise_and(position, devices - 1 - stride)
        slot = jnp.right_shift(lowest, k + 1) * stride + jnp.bitwise_and(lowest, stride - 1)
        linked.append(pair_ref[k, slot] == 1)
    inside = jnp.logical_and(position > 0, position < devices - 1)
    zero = jnp.float32(0.0)
    bias = [zero, jnp.where(linked[0], jnp.float32(1.0), zero)]
    bias += [jnp.where(m, zero, jnp.float32(MASKED)) for m in [inside] + linked[1:]]
    return bias + [zero] * NGLOB


def cotangent_kernel(
    head_ref, all_ref, w_hbm, out_ref, gatt_ref, gattt_ref, cols_ref, w_ref, sems
):
    pieces, length, width = out_ref.shape
    blocks = length // 128
    copies = [pltpu.make_async_copy(w_hbm, w_ref, sems.at[0])]
    for c in range(pieces):
        for b in range(blocks):
            copies.append(pltpu.make_async_copy(
                all_ref.at[c, b], out_ref.at[c, pl.ds(b * 128, 128)], sems.at[len(copies)]
            ))
    late = len(copies)
    for c in range(pieces):
        copies.append(pltpu.make_async_copy(
            all_ref.at[c, blocks + head_ref[0]], cols_ref.at[c], sems.at[len(copies)]
        ))
    for copy in copies:
        copy.start()
    for copy in copies[:late]:
        copy.wait()
    gatt = jnp.zeros((length, width), F32)
    for c in range(pieces):
        gatt = gatt + dot(out_ref[c], w_ref[:, c * width:(c + 1) * width], NT)
    gatt_ref[...] = gatt.astype(BF16)
    gattt_ref[...] = gatt.T.astype(BF16)
    for copy in copies[late:]:
        copy.wait()


def near_kernel(
    pos_ref, pair_ref, own_ref, p0, p2, p3, p4, stats_ref, sum_ref, turned_ref, score_ref,
):
    length = own_ref.shape[0] // 2
    width = own_ref.shape[1]
    nheads = width // HD
    base2 = 1.0 / math.sqrt(HD) / math.log(2.0)
    bias = block_bias(pos_ref, pair_ref)
    turned_ref[...] = own_ref[:length].astype(F32).T.astype(BF16)
    blocks = ((own_ref, bias[0]), (p0, bias[1]), (p2, bias[3]), (p3, bias[4]), (p4, bias[5]))
    query = own_ref[:length]
    lane = lax.broadcasted_iota(jnp.int32, (1, width), 1)
    head = lane // HD
    stats = jnp.zeros((length, width), F32)
    for h in range(nheads):
        query_h = jnp.where(head == h, query, jnp.zeros_like(query))
        highest = jnp.full((length, 1), MASKED, F32)
        for b, (ref, shift) in enumerate(blocks):
            s = dot(query_h, ref[:length], NT) * base2 + shift
            score_ref[:, b * length:(b + 1) * length] = s
            highest = jnp.maximum(highest, jnp.max(s, axis=1, keepdims=True))
        total = jnp.zeros((length, 1), F32)
        acc = jnp.zeros((length, width), F32)
        for b, (ref, _) in enumerate(blocks):
            e = jnp.exp2(score_ref[:, b * length:(b + 1) * length] - highest)
            total = total + jnp.sum(e, axis=1, keepdims=True)
            acc = acc + dot(e.astype(BF16), ref[length:], NN)
        stats = jnp.where(lane == h, highest, stats)
        stats = jnp.where(lane == nheads + h, total, stats)
        if h == 0:
            sum_ref[...] = acc
        else:
            sum_ref[...] = jnp.where(head == h, acc, sum_ref[...])
    stats_ref[...] = stats


def forward_kernel(
    pos_ref, pair_ref, own_ref, p1, near_ref, sum_ref, turned_ref, gattt_ref, glob_ref, gout_ref,
    gatt_ref,
    att_ref, sums_ref, stats_ref, gquery_ref,
    score_ref, out_ref,
):
    length = own_ref.shape[0] // 2
    width = own_ref.shape[1]
    pieces = gout_ref.shape[0]
    nheads = width // HD
    scaling = 1.0 / math.sqrt(HD)
    base2 = scaling / math.log(2.0)
    bias = block_bias(pos_ref, pair_ref)
    bias = [bias[2]] + bias[-NGLOB:]
    keys = [p1[:length]]
    vals = [p1[length:]]
    half = glob_ref.shape[0] // 2
    for g in range(NGLOB):
        keys.append(jnp.concatenate([glob_ref[p, g] for p in range(half)], axis=0))
        vals.append(jnp.concatenate([glob_ref[half + p, g] for p in range(half)], axis=0))
    count = len(keys)
    query = own_ref[:length]
    lane = lax.broadcasted_iota(jnp.int32, (1, width), 1)
    head = lane // HD
    gatt_b = gatt_ref[...]

    inverse = []
    stats = jnp.zeros((length, width), F32)
    for h in range(nheads):
        query_h = jnp.where(head == h, query, jnp.zeros_like(query))
        near = near_ref[:, h:h + 1]
        highest = near
        for b in range(count):
            s = dot(query_h, keys[b], NT) * base2 + bias[b]
            score_ref[h, :, b * length:(b + 1) * length] = s
            highest = jnp.maximum(highest, jnp.max(s, axis=1, keepdims=True))
        factor = jnp.exp2(near - highest)
        total = near_ref[:, nheads + h:nheads + h + 1] * factor
        acc = sum_ref[...] * factor
        for b in range(count):
            e = jnp.exp2(score_ref[h, :, b * length:(b + 1) * length] - highest)
            score_ref[h, :, b * length:(b + 1) * length] = e
            total = total + jnp.sum(e, axis=1, keepdims=True)
            acc = acc + dot(e.astype(BF16), vals[b], NN)
        inv = 1.0 / total
        inverse.append(inv)
        stats = jnp.where(lane == h, highest + jnp.log2(total), stats)
        if h == 0:
            out_ref[...] = acc * inv
        else:
            out_ref[...] = jnp.where(head == h, acc * inv, out_ref[...])

    attended = out_ref[...]
    att_ref[...] = attended
    attended_b = attended.astype(BF16)
    for c in range(pieces):
        part = dot(attended_b, gout_ref[c], TN).astype(BF16)
        n = width // HD
        sums_ref[c * n:(c + 1) * n, 0:HD, :] = part.reshape(n, HD, 128)

    product = gatt_b.astype(F32) * attended
    query_t = turned_ref[...]
    gatt_t = gattt_ref[...]
    for h in range(nheads):
        gatt_h = jnp.where(head == h, gatt_b, jnp.zeros_like(gatt_b))
        row_dot = jnp.sum(jnp.where(head == h, product, 0.0), axis=1, keepdims=True)
        stats = jnp.where(lane == nheads + h, row_dot, stats)
        inv = inverse[h]
        qt = query_t[h * HD:(h + 1) * HD]
        gt = gatt_t[h * HD:(h + 1) * HD]
        acc = jnp.zeros((length, width), F32)
        for g in range(NGLOB):
            b = count - NGLOB + g
            weights = score_ref[h, :, b * length:(b + 1) * length] * inv
            gw = dot(gatt_h, vals[b], NT)
            gs = (weights * (gw - row_dot)).astype(BF16)
            acc = acc + dot(gs, keys[b], NN)
            gk = dot(qt, gs, NN) * scaling
            gv = dot(gt, weights.astype(BF16), NN)
            for a in range(length // 128):
                at = (g * (length // 128) + a) * 2 * nheads + h
                cols = slice(a * 128, (a + 1) * 128)
                sums_ref[at, HD:2 * HD, :] = gk[:, cols].astype(BF16)
                sums_ref[at + nheads, HD:2 * HD, :] = gv[:, cols].astype(BF16)
        if h == 0:
            out_ref[...] = acc
        else:
            out_ref[...] = jnp.where(head == h, acc, out_ref[...])
    stats_ref[...] = stats
    gquery_ref[...] = out_ref[...]


def backward_kernel(
    slots, pos_ref, pair_ref, own_ref, stats_ref, turned_ref, gattt_ref, gatt_ref, gsum_ref, *refs
):
    length = own_ref.shape[0] // 2
    width = own_ref.shape[1]
    nheads = width // HD
    scaling = 1.0 / math.sqrt(HD)
    base2 = scaling / math.log(2.0)
    bias = block_bias(pos_ref, pair_ref)
    inputs = sum(slot > 0 for slot in slots)
    blocks = list(refs[:inputs])
    outs, gquery_ref = refs[inputs:-1], refs[-1]
    if 0 in slots:
        blocks.insert(slots.index(0), own_ref)
    query = own_ref[:length]
    gatt_b = gatt_ref[...]
    head = lax.broadcasted_iota(jnp.int32, (1, width), 1) // HD
    query_t = turned_ref[...]
    gatt_t = gattt_ref[...]
    result = gsum_ref[...]
    for h in range(nheads):
        query_h = jnp.where(head == h, query, jnp.zeros_like(query))
        gatt_h = jnp.where(head == h, gatt_b, jnp.zeros_like(gatt_b))
        log_total = stats_ref[:, h:h + 1]
        row_dot = stats_ref[:, nheads + h:nheads + h + 1]
        qt = query_t[h * HD:(h + 1) * HD]
        gt = gatt_t[h * HD:(h + 1) * HD]
        acc = jnp.zeros((length, width), F32)
        for slot, ref, o in zip(slots, blocks, outs):
            keys = ref[:length]
            s = dot(query_h, keys, NT) * base2 + (bias[slot] - log_total)
            weights = jnp.exp2(s)
            gw = dot(gatt_h, ref[length:], NT)
            gs = (weights * (gw - row_dot)).astype(BF16)
            acc = acc + dot(gs, keys, NN)
            gk = dot(qt, gs, NN) * scaling
            gv = dot(gt, weights.astype(BF16), NN)
            o[h * HD:(h + 1) * HD, :] = gk.astype(o.dtype)
            o[width + h * HD:width + (h + 1) * HD, :] = gv.astype(o.dtype)
        result = result + jnp.where(head == h, acc, 0.0)
    gquery_ref[...] = result


def project_kernel(att_ref, w_ref, projected_ref):
    projected = jnp.zeros(projected_ref.shape, F32)
    for c in range(att_ref.shape[0]):
        projected = projected + dot(att_ref[c].astype(BF16), w_ref[c], NN)
    projected_ref[...] = projected.astype(BF16)


def finish_kernel(
    pos_ref, ids_ref, b0, b1, b2, b3, b4, gown_ref, gquery_ref, total_ref,
    gqk_ref, gval_ref, gweight_ref,
):
    length, width = gquery_ref.shape
    halves = length // 128
    rows = width * 2 // HD
    for a in range(halves):
        cols = slice(a * 128, (a + 1) * 128)
        acc = gown_ref[:, cols]
        for b in (b0, b1, b2, b3, b4):
            acc = acc + b[:, cols].astype(F32)
        for g in range(NGLOB):
            at = (g * halves + a) * rows
            term = total_ref[at:at + rows, HD:2 * HD, :].reshape(2 * width, 128).astype(F32)
            acc = acc + jnp.where(ids_ref[g] == pos_ref[0], term, 0.0)
        tokens = slice(a * 128, (a + 1) * 128)
        gqk_ref[tokens, :] = (gquery_ref[tokens, :] / math.sqrt(HD) + acc[:width].T).astype(BF16)
        gval_ref[tokens, :] = acc[width:].T.astype(BF16)
    n = width // HD
    for c in range(gweight_ref.shape[1] // 128):
        piece = total_ref[c * n:(c + 1) * n, 0:HD, :].reshape(width, 128)
        gweight_ref[:, c * 128:(c + 1) * 128] = piece.astype(F32)


def copy_all(copies):
    for copy in copies:
        copy.start()
    for copy in copies:
        copy.wait()


def pack_kernel(qk_ref, val_ref, gout_ref, w_ref, joined_ref, share_ref):
    length, width = qk_ref.shape
    blocks = length // 128
    joined_ref[:length] = qk_ref[...]
    joined_ref[length:] = val_ref[...]
    share_ref[0:blocks] = gout_ref[...].reshape(blocks, 128, width)
    for c in range(w_ref.shape[1] // 128):
        share_ref[blocks + c] = w_ref[:, c * 128:(c + 1) * 128]


def pick_kernel(ids_ref, slices_ref, out_ref, sems):
    count = out_ref.shape[0]
    copies = []
    for g in range(NGLOB):
        chosen = slices_ref.at[lax.rem(ids_ref[g], PATCH)]
        for n in range(count):
            sem = sems.at[g * count + n]
            copies.append(pltpu.make_async_copy(chosen, out_ref.at[n, g], sem))
    copy_all(copies)


def spread_kernel(ids_ref, slices_ref, out_ref, sems):
    count = out_ref.shape[0]
    copies = []
    for g in range(NGLOB):
        chosen = slices_ref.at[lax.div(ids_ref[g], PATCH), g]
        for n in range(count):
            sem = sems.at[g * count + n]
            copies.append(pltpu.make_async_copy(chosen, out_ref.at[n, g], sem))
    copy_all(copies)


def hbm():
    return pl.BlockSpec(memory_space=pltpu.HBM)


def anywhere():
    return pl.BlockSpec(memory_space=pl.ANY)


def limit(mebibytes):
    return pltpu.CompilerParams(vmem_limit_bytes=mebibytes * 1024 * 1024)


def vmem(count):
    return [pl.BlockSpec(memory_space=pltpu.VMEM)] * count


def smem():
    return pl.BlockSpec(memory_space=pltpu.SMEM)


def local(qk_vectors, token_values, grad_output, out_weight, global_ids, pair_active):
    length, width = qk_vectors.shape
    devices = lax.axis_size(CTX)
    pieces = lax.axis_size(HEAD)
    position = lax.axis_index(CTX)
    joined = jnp.concatenate([qk_vectors, token_values], axis=0)

    his, los = lax.axis_size("hi"), lax.axis_size("lo")
    step = 2 * length // los
    joined, share = pl.pallas_call(
        pack_kernel,
        out_shape=(
            jax.ShapeDtypeStruct((2 * length, width), BF16),
            jax.ShapeDtypeStruct((length // 128 + pieces, 128, width), BF16),
        ),
        in_specs=vmem(4),
        out_specs=tuple(vmem(2)),
        name="pack",
    )(qk_vectors, token_values, grad_output, out_weight)

    slices = lax.all_to_all(joined.reshape(los, step, width), "lo", 0, 0)
    portion = lax.all_gather(share, HEAD, axis=0)
    routes = [[(i, i ^ 1) for i in range(devices)]]
    other = [i + 1 if i % 2 else i - 1 for i in range(devices)]
    routes.append([(i, j) for i, j in enumerate(other) if 0 <= j < devices])
    routes += [[(i, i ^ (1 << k)) for i in range(devices)] for k in range(1, ROUNDS)]
    received = [None] * len(routes)
    for n in (4, 0):
        received[n] = lax.ppermute(joined, CTX, routes[n])
    picked = pl.pallas_call(
        pick_kernel,
        out_shape=jax.ShapeDtypeStruct((his, NGLOB, step, width), BF16),
        in_specs=[smem(), anywhere()],
        out_specs=anywhere(),
        scratch_shapes=[pltpu.SemaphoreType.DMA((NGLOB * his,))],
        compiler_params=limit(1),
        name="pick",
    )(global_ids, slices)
    picked, joined_late, received[4], received[0] = lax.optimization_barrier(
        (picked, joined, received[4], received[0])
    )
    column = lax.all_to_all(picked, "hi", 0, 0)
    for n in (3, 2):
        received[n] = lax.ppermute(joined_late, CTX, routes[n])
    portion_b, gatt, gatt_t, weight_cols = pl.pallas_call(
        cotangent_kernel,
        out_shape=(
            jax.ShapeDtypeStruct((pieces, length, width), BF16),
            jax.ShapeDtypeStruct((length, width), BF16),
            jax.ShapeDtypeStruct((width, length), BF16),
            jax.ShapeDtypeStruct((pieces, width, 128), BF16),
        ),
        in_specs=[smem(), hbm(), hbm()],
        out_specs=tuple(vmem(4)),
        scratch_shapes=[
            pltpu.VMEM((width, pieces * width), BF16),
            pltpu.SemaphoreType.DMA((1 + pieces * (length // 128 + 1),)),
        ],
        compiler_params=limit(58),
        cost_estimate=pl.CostEstimate(
            flops=600_000_000, bytes_accessed=4_000_000, transcendentals=0
        ),
        name="cotangent",
    )(lax.axis_index(HEAD)[None], portion, out_weight)
    column, portion_b, gatt, gatt_t, weight_cols = lax.optimization_barrier(
        (column, portion_b, gatt, gatt_t, weight_cols)
    )
    chosen = pl.pallas_call(
        spread_kernel,
        out_shape=jax.ShapeDtypeStruct((los, NGLOB, step, width), BF16),
        in_specs=[smem(), anywhere()],
        out_specs=anywhere(),
        scratch_shapes=[pltpu.SemaphoreType.DMA((NGLOB * los,))],
        compiler_params=limit(1),
        name="spread",
    )(global_ids, column)
    chosen, joined_late, received[3], received[2] = lax.optimization_barrier(
        (chosen, joined, received[3], received[2])
    )
    globals_all = lax.all_to_all(chosen, "lo", 0, 0)
    received[1] = lax.ppermute(joined_late, CTX, routes[1])
    nheads = width // HD
    block = jax.ShapeDtypeStruct((2 * width, length), BF16)
    square = jax.ShapeDtypeStruct((length, width), F32)
    near_stats, near_sum, turned = pl.pallas_call(
        near_kernel,
        out_shape=(square, square, jax.ShapeDtypeStruct((width, length), BF16)),
        in_specs=[smem()] * 2 + vmem(5),
        out_specs=tuple(vmem(3)),
        scratch_shapes=[pltpu.VMEM((length, 5 * length), F32)],
        compiler_params=limit(12),
        cost_estimate=pl.CostEstimate(
            flops=1_000_000_000, bytes_accessed=1_000_000, transcendentals=650_000
        ),
        name="near",
    )(position[None], pair_active, joined, received[0], *received[2:])
    globals_all, near_stats, near_sum, turned = lax.optimization_barrier(
        (globals_all, near_stats, near_sum, turned)
    )
    attended, sums, stats, gglob = pl.pallas_call(
        forward_kernel,
        out_shape=(
            square,
            jax.ShapeDtypeStruct((los, 2 * HD, 128), BF16),
            square,
            square,
        ),
        in_specs=[smem()] * 2 + vmem(9),
        out_specs=tuple(vmem(4)),
        scratch_shapes=[
            pltpu.VMEM((nheads, length, (1 + NGLOB) * length), F32),
            pltpu.VMEM((length, width), F32),
        ],
        compiler_params=limit(20),
        cost_estimate=pl.CostEstimate(
            flops=3_000_000_000, bytes_accessed=4_000_000, transcendentals=1_100_000
        ),
        name="forward",
    )(
        position[None], pair_active, joined, received[1], near_stats, near_sum, turned, gatt_t,
        globals_all, portion_b, gatt,
    )

    shares = lax.all_to_all(sums, "lo", 0, 0)
    attended_all = lax.all_gather(attended, HEAD, axis=0)
    def backward(slots, name, gsum):
        inputs = [received[slot - 1] for slot in slots if slot > 0]
        shapes = [block if slot > 0 else whole for slot in slots] + [square]
        return pl.pallas_call(
            functools.partial(backward_kernel, slots),
            out_shape=tuple(shapes),
            in_specs=[smem()] * 2 + vmem(6 + len(inputs)),
            out_specs=tuple(vmem(len(shapes))),
            compiler_params=limit(10),
            cost_estimate=pl.CostEstimate(
                flops=1_000_000, bytes_accessed=10_000, transcendentals=0
            ),
            name=name,
        )(position[None], pair_active, joined, stats, turned, gatt_t, gatt, gsum, *inputs)

    whole = jax.ShapeDtypeStruct((2 * width, length), F32)
    terms = [None] * len(routes)
    terms[0], terms[1], terms[4], gquery = backward((1, 2, 5), "backward", gglob)
    returned = [None] * len(routes)
    for n in (1, 0):
        returned[n] = lax.ppermute(terms[n], CTX, routes[n])
    shares, terms[4], gquery = lax.optimization_barrier((shares, terms[4], gquery))
    share = jnp.sum(shares.astype(F32), axis=0).astype(BF16)
    share, returned[1], returned[0] = lax.optimization_barrier((share, returned[1], returned[0]))
    column = lax.all_to_all(jnp.broadcast_to(share[None], (his,) + share.shape), "hi", 0, 0)
    terms[2], terms[3], gown, gquery = backward((3, 4, 0), "backward_rest", gquery)
    for n in (4, 2, 3):
        returned[n] = lax.ppermute(terms[n], CTX, routes[n])
    share = jnp.sum(column.astype(F32), axis=0).astype(BF16)
    share, returned[4], returned[2], attended_all = lax.optimization_barrier(
        (share, returned[4], returned[2], attended_all)
    )
    totals = lax.all_to_all(jnp.broadcast_to(share[None], (los,) + share.shape), "lo", 0, 0)

    projected = pl.pallas_call(
        project_kernel,
        out_shape=jax.ShapeDtypeStruct((length, width), BF16),
        in_specs=vmem(2),
        out_specs=vmem(1)[0],
        compiler_params=limit(4),
        cost_estimate=pl.CostEstimate(
            flops=70_000_000, bytes_accessed=1_500_000, transcendentals=0
        ),
        name="project",
    )(attended_all, weight_cols)
    gqk, gval, gweight = pl.pallas_call(
        finish_kernel,
        out_shape=(
            jax.ShapeDtypeStruct((length, width), BF16),
            jax.ShapeDtypeStruct((length, width), BF16),
            jax.ShapeDtypeStruct((width, pieces * 128), F32),
        ),
        in_specs=[smem()] * 2 + vmem(8),
        out_specs=tuple(vmem(3)),
        compiler_params=limit(6),
        cost_estimate=pl.CostEstimate(
            flops=2_000_000, bytes_accessed=2_500_000, transcendentals=0
        ),
        name="finish",
    )(position[None], global_ids, *returned, gown, gquery, totals)
    return (projected, gqk, gval, gweight)


def solution(mesh):
    ctx, head = mesh.devices.shape
    inner = Mesh(mesh.devices.reshape(ctx // PATCH, PATCH, head), CTX + (HEAD,))
    row = P(CTX, HEAD)
    return jax.shard_map(
        local,
        mesh=inner,
        in_specs=(row, row, row, P(HEAD, None), P(), P()),
        out_specs=(row, row, row, P(HEAD, None)),
        check_vma=False,
    )
```

```python
import functools
import math

import jax
import jax.numpy as jnp
from jax import lax
from jax.experimental import pallas as pl
from jax.experimental.pallas import tpu as pltpu
from jax.sharding import Mesh, PartitionSpec as P

HD = 64
NGLOB = 2
ROUNDS = 4
CTX = ("hi", "lo")
HEAD = "head"
PATCH = 16
NT = (((1,), (1,)), ((), ()))
NN = (((1,), (0,)), ((), ()))
TN = (((0,), (0,)), ((), ()))
F32 = jnp.float32
BF16 = jnp.bfloat16
MASKED = -1e30


def dot(a, b, dims):
    return lax.dot_general(a, b, dims, preferred_element_type=F32)


def block_bias(pos_ref, pair_ref):
    position = pos_ref[0]
    devices = 2 * pair_ref.shape[1]
    linked = []
    for k in range(ROUNDS):
        stride = 1 << k
        lowest = jnp.bitwise_and(position, devices - 1 - stride)
        slot = jnp.right_shift(lowest, k + 1) * stride + jnp.bitwise_and(lowest, stride - 1)
        linked.append(pair_ref[k, slot] == 1)
    inside = jnp.logical_and(position > 0, position < devices - 1)
    zero = jnp.float32(0.0)
    bias = [zero, jnp.where(linked[0], jnp.float32(1.0), zero)]
    bias += [jnp.where(m, zero, jnp.float32(MASKED)) for m in [inside] + linked[1:]]
    return bias + [zero] * NGLOB


def cotangent_kernel(
    head_ref, all_ref, w_hbm, out_ref, gatt_ref, gattt_ref, cols_ref, w_ref, sems
):
    pieces, length, width = out_ref.shape
    blocks = length // 128
    copies = [pltpu.make_async_copy(w_hbm, w_ref, sems.at[0])]
    for c in range(pieces):
        for b in range(blocks):
            copies.append(pltpu.make_async_copy(
                all_ref.at[c, b], out_ref.at[c, pl.ds(b * 128, 128)], sems.at[len(copies)]
            ))
    late = len(copies)
    for c in range(pieces):
        copies.append(pltpu.make_async_copy(
            all_ref.at[c, blocks + head_ref[0]], cols_ref.at[c], sems.at[len(copies)]
        ))
    for copy in copies:
        copy.start()
    for copy in copies[:late]:
        copy.wait()
    gatt = jnp.zeros((length, width), F32)
    for c in range(pieces):
        gatt = gatt + dot(out_ref[c], w_ref[:, c * width:(c + 1) * width], NT)
    gatt_ref[...] = gatt.astype(BF16)
    gattt_ref[...] = gatt.T.astype(BF16)
    for copy in copies[late:]:
        copy.wait()


def near_kernel(
    pos_ref, pair_ref, own_ref, p0, p2, p3, p4, stats_ref, sum_ref, turned_ref, score_ref,
):
    length = own_ref.shape[0] // 2
    width = own_ref.shape[1]
    nheads = width // HD
    base2 = 1.0 / math.sqrt(HD) / math.log(2.0)
    bias = block_bias(pos_ref, pair_ref)
    turned_ref[...] = own_ref[:length].astype(F32).T.astype(BF16)
    blocks = ((own_ref, bias[0]), (p0, bias[1]), (p2, bias[3]), (p3, bias[4]), (p4, bias[5]))
    query = own_ref[:length]
    lane = lax.broadcasted_iota(jnp.int32, (1, width), 1)
    head = lane // HD
    stats = jnp.zeros((length, width), F32)
    for h in range(nheads):
        query_h = jnp.where(head == h, query, jnp.zeros_like(query))
        highest = jnp.full((length, 1), MASKED, F32)
        for b, (ref, shift) in enumerate(blocks):
            s = dot(query_h, ref[:length], NT) * base2 + shift
            score_ref[:, b * length:(b + 1) * length] = s
            highest = jnp.maximum(highest, jnp.max(s, axis=1, keepdims=True))
        total = jnp.zeros((length, 1), F32)
        acc = jnp.zeros((length, width), F32)
        for b, (ref, _) in enumerate(blocks):
            e = jnp.exp2(score_ref[:, b * length:(b + 1) * length] - highest)
            total = total + jnp.sum(e, axis=1, keepdims=True)
            acc = acc + dot(e.astype(BF16), ref[length:], NN)
        stats = jnp.where(lane == h, highest, stats)
        stats = jnp.where(lane == nheads + h, total, stats)
        if h == 0:
            sum_ref[...] = acc
        else:
            sum_ref[...] = jnp.where(head == h, acc, sum_ref[...])
    stats_ref[...] = stats


def forward_kernel(
    pos_ref, pair_ref, own_ref, p1, near_ref, sum_ref, turned_ref, gattt_ref, glob_ref, gout_ref,
    gatt_ref,
    att_ref, sums_ref, stats_ref, gquery_ref,
    score_ref, out_ref,
):
    length = own_ref.shape[0] // 2
    width = own_ref.shape[1]
    pieces = gout_ref.shape[0]
    nheads = width // HD
    scaling = 1.0 / math.sqrt(HD)
    base2 = scaling / math.log(2.0)
    bias = block_bias(pos_ref, pair_ref)
    bias = [bias[2]] + bias[-NGLOB:]
    keys = [p1[:length]]
    vals = [p1[length:]]
    half = glob_ref.shape[0] // 2
    for g in range(NGLOB):
        keys.append(jnp.concatenate([glob_ref[p, g] for p in range(half)], axis=0))
        vals.append(jnp.concatenate([glob_ref[half + p, g] for p in range(half)], axis=0))
    count = len(keys)
    query = own_ref[:length]
    lane = lax.broadcasted_iota(jnp.int32, (1, width), 1)
    head = lane // HD
    gatt_b = gatt_ref[...]

    inverse = []
    stats = jnp.zeros((length, width), F32)
    for h in range(nheads):
        query_h = jnp.where(head == h, query, jnp.zeros_like(query))
        near = near_ref[:, h:h + 1]
        highest = near
        for b in range(count):
            s = dot(query_h, keys[b], NT) * base2 + bias[b]
            score_ref[h, :, b * length:(b + 1) * length] = s
            highest = jnp.maximum(highest, jnp.max(s, axis=1, keepdims=True))
        factor = jnp.exp2(near - highest)
        total = near_ref[:, nheads + h:nheads + h + 1] * factor
        acc = sum_ref[...] * factor
        for b in range(count):
            e = jnp.exp2(score_ref[h, :, b * length:(b + 1) * length] - highest)
            score_ref[h, :, b * length:(b + 1) * length] = e
            total = total + jnp.sum(e, axis=1, keepdims=True)
            acc = acc + dot(e.astype(BF16), vals[b], NN)
        inv = 1.0 / total
        inverse.append(inv)
        stats = jnp.where(lane == h, highest + jnp.log2(total), stats)
        if h == 0:
            out_ref[...] = acc * inv
        else:
            out_ref[...] = jnp.where(head == h, acc * inv, out_ref[...])

    attended = out_ref[...]
    att_ref[...] = attended
    attended_b = attended.astype(BF16)
    every = jnp.concatenate([gout_ref[c] for c in range(pieces)], axis=1)
    update = dot(attended_b, every, TN).astype(BF16)
    for c in range(pieces):
        part = update[:, c * 128:(c + 1) * 128]
        n = width // HD
        sums_ref[c * n:(c + 1) * n, 0:HD, :] = part.reshape(n, HD, 128)

    product = gatt_b.astype(F32) * attended
    query_t = turned_ref[...]
    gatt_t = gattt_ref[...]
    for h in range(nheads):
        gatt_h = jnp.where(head == h, gatt_b, jnp.zeros_like(gatt_b))
        row_dot = jnp.sum(jnp.where(head == h, product, 0.0), axis=1, keepdims=True)
        stats = jnp.where(lane == nheads + h, row_dot, stats)
        inv = inverse[h]
        qt = query_t[h * HD:(h + 1) * HD]
        gt = gatt_t[h * HD:(h + 1) * HD]
        acc = jnp.zeros((length, width), F32)
        for g in range(NGLOB):
            b = count - NGLOB + g
            weights = score_ref[h, :, b * length:(b + 1) * length] * inv
            gw = dot(gatt_h, vals[b], NT)
            gs = (weights * (gw - row_dot)).astype(BF16)
            acc = acc + dot(gs, keys[b], NN)
            gk = dot(qt, gs, NN) * scaling
            gv = dot(gt, weights.astype(BF16), NN)
            for a in range(length // 128):
                at = (g * (length // 128) + a) * 2 * nheads + h
                cols = slice(a * 128, (a + 1) * 128)
                sums_ref[at, HD:2 * HD, :] = gk[:, cols].astype(BF16)
                sums_ref[at + nheads, HD:2 * HD, :] = gv[:, cols].astype(BF16)
        if h == 0:
            out_ref[...] = acc
        else:
            out_ref[...] = jnp.where(head == h, acc, out_ref[...])
    stats_ref[...] = stats
    gquery_ref[...] = out_ref[...]


def backward_kernel(
    slots, pos_ref, pair_ref, own_ref, stats_ref, turned_ref, gattt_ref, gatt_ref, gsum_ref, *refs
):
    length = own_ref.shape[0] // 2
    width = own_ref.shape[1]
    nheads = width // HD
    scaling = 1.0 / math.sqrt(HD)
    base2 = scaling / math.log(2.0)
    bias = block_bias(pos_ref, pair_ref)
    inputs = sum(slot > 0 for slot in slots)
    blocks = list(refs[:inputs])
    outs, gquery_ref = refs[inputs:-1], refs[-1]
    if 0 in slots:
        blocks.insert(slots.index(0), own_ref)
    query = own_ref[:length]
    gatt_b = gatt_ref[...]
    head = lax.broadcasted_iota(jnp.int32, (1, width), 1) // HD
    query_t = turned_ref[...]
    gatt_t = gattt_ref[...]
    result = gsum_ref[...]
    for h in range(nheads):
        query_h = jnp.where(head == h, query, jnp.zeros_like(query))
        gatt_h = jnp.where(head == h, gatt_b, jnp.zeros_like(gatt_b))
        log_total = stats_ref[:, h:h + 1]
        row_dot = stats_ref[:, nheads + h:nheads + h + 1]
        qt = query_t[h * HD:(h + 1) * HD]
        gt = gatt_t[h * HD:(h + 1) * HD]
        acc = jnp.zeros((length, width), F32)
        for slot, ref, o in zip(slots, blocks, outs):
            keys = ref[:length]
            s = dot(query_h, keys, NT) * base2 + (bias[slot] - log_total)
            weights = jnp.exp2(s)
            gw = dot(gatt_h, ref[length:], NT)
            gs = (weights * (gw - row_dot)).astype(BF16)
            acc = acc + dot(gs, keys, NN)
            gk = dot(qt, gs, NN) * scaling
            gv = dot(gt, weights.astype(BF16), NN)
            o[h * HD:(h + 1) * HD, :] = gk.astype(o.dtype)
            o[width + h * HD:width + (h + 1) * HD, :] = gv.astype(o.dtype)
        result = result + jnp.where(head == h, acc, 0.0)
    gquery_ref[...] = result


def project_kernel(att_ref, w_ref, projected_ref):
    projected = jnp.zeros(projected_ref.shape, F32)
    for c in range(att_ref.shape[0]):
        projected = projected + dot(att_ref[c].astype(BF16), w_ref[c], NN)
    projected_ref[...] = projected.astype(BF16)


def finish_kernel(
    pos_ref, ids_ref, b0, b1, b2, b3, b4, gown_ref, gquery_ref, total_ref,
    gqk_ref, gval_ref, gweight_ref,
):
    length, width = gquery_ref.shape
    halves = length // 128
    rows = width * 2 // HD
    for a in range(halves):
        cols = slice(a * 128, (a + 1) * 128)
        acc = gown_ref[:, cols]
        for b in (b0, b1, b2, b3, b4):
            acc = acc + b[:, cols].astype(F32)
        for g in range(NGLOB):
            at = (g * halves + a) * rows
            term = total_ref[at:at + rows, HD:2 * HD, :].reshape(2 * width, 128).astype(F32)
            acc = acc + jnp.where(ids_ref[g] == pos_ref[0], term, 0.0)
        tokens = slice(a * 128, (a + 1) * 128)
        gqk_ref[tokens, :] = (gquery_ref[tokens, :] / math.sqrt(HD) + acc[:width].T).astype(BF16)
        gval_ref[tokens, :] = acc[width:].T.astype(BF16)
    n = width // HD
    for c in range(gweight_ref.shape[1] // 128):
        piece = total_ref[c * n:(c + 1) * n, 0:HD, :].reshape(width, 128)
        gweight_ref[:, c * 128:(c + 1) * 128] = piece.astype(F32)


def copy_all(copies):
    for copy in copies:
        copy.start()
    for copy in copies:
        copy.wait()


def pack_kernel(qk_ref, val_ref, gout_ref, w_ref, joined_ref, share_ref):
    length, width = qk_ref.shape
    blocks = length // 128
    joined_ref[:length] = qk_ref[...]
    joined_ref[length:] = val_ref[...]
    share_ref[0:blocks] = gout_ref[...].reshape(blocks, 128, width)
    for c in range(w_ref.shape[1] // 128):
        share_ref[blocks + c] = w_ref[:, c * 128:(c + 1) * 128]


def pick_kernel(ids_ref, slices_ref, out_ref, sems):
    count = out_ref.shape[0]
    copies = []
    for g in range(NGLOB):
        chosen = slices_ref.at[lax.rem(ids_ref[g], PATCH)]
        for n in range(count):
            sem = sems.at[g * count + n]
            copies.append(pltpu.make_async_copy(chosen, out_ref.at[n, g], sem))
    copy_all(copies)


def spread_kernel(ids_ref, slices_ref, out_ref, sems):
    count = out_ref.shape[0]
    copies = []
    for g in range(NGLOB):
        chosen = slices_ref.at[lax.div(ids_ref[g], PATCH), g]
        for n in range(count):
            sem = sems.at[g * count + n]
            copies.append(pltpu.make_async_copy(chosen, out_ref.at[n, g], sem))
    copy_all(copies)


def hbm():
    return pl.BlockSpec(memory_space=pltpu.HBM)


def anywhere():
    return pl.BlockSpec(memory_space=pl.ANY)


def limit(mebibytes):
    return pltpu.CompilerParams(vmem_limit_bytes=mebibytes * 1024 * 1024)


def vmem(count):
    return [pl.BlockSpec(memory_space=pltpu.VMEM)] * count


def smem():
    return pl.BlockSpec(memory_space=pltpu.SMEM)


def local(qk_vectors, token_values, grad_output, out_weight, global_ids, pair_active):
    length, width = qk_vectors.shape
    devices = lax.axis_size(CTX)
    pieces = lax.axis_size(HEAD)
    position = lax.axis_index(CTX)
    joined = jnp.concatenate([qk_vectors, token_values], axis=0)

    his, los = lax.axis_size("hi"), lax.axis_size("lo")
    step = 2 * length // los
    joined, share = pl.pallas_call(
        pack_kernel,
        out_shape=(
            jax.ShapeDtypeStruct((2 * length, width), BF16),
            jax.ShapeDtypeStruct((length // 128 + pieces, 128, width), BF16),
        ),
        in_specs=vmem(4),
        out_specs=tuple(vmem(2)),
        name="pack",
    )(qk_vectors, token_values, grad_output, out_weight)

    slices = lax.all_to_all(joined.reshape(los, step, width), "lo", 0, 0)
    portion = lax.all_gather(share, HEAD, axis=0)
    routes = [[(i, i ^ 1) for i in range(devices)]]
    other = [i + 1 if i % 2 else i - 1 for i in range(devices)]
    routes.append([(i, j) for i, j in enumerate(other) if 0 <= j < devices])
    routes += [[(i, i ^ (1 << k)) for i in range(devices)] for k in range(1, ROUNDS)]
    received = [None] * len(routes)
    for n in (4, 0):
        received[n] = lax.ppermute(joined, CTX, routes[n])
    picked = pl.pallas_call(
        pick_kernel,
        out_shape=jax.ShapeDtypeStruct((his, NGLOB, step, width), BF16),
        in_specs=[smem(), anywhere()],
        out_specs=anywhere(),
        scratch_shapes=[pltpu.SemaphoreType.DMA((NGLOB * his,))],
        compiler_params=limit(1),
        name="pick",
    )(global_ids, slices)
    picked, joined_late, received[0], received[4] = lax.optimization_barrier(
        (picked, joined, received[0], received[4])
    )
    column = lax.all_to_all(picked, "hi", 0, 0)
    for n in (3, 2):
        received[n] = lax.ppermute(joined_late, CTX, routes[n])
    portion_b, gatt, gatt_t, weight_cols = pl.pallas_call(
        cotangent_kernel,
        out_shape=(
            jax.ShapeDtypeStruct((pieces, length, width), BF16),
            jax.ShapeDtypeStruct((length, width), BF16),
            jax.ShapeDtypeStruct((width, length), BF16),
            jax.ShapeDtypeStruct((pieces, width, 128), BF16),
        ),
        in_specs=[smem(), hbm(), hbm()],
        out_specs=tuple(vmem(4)),
        scratch_shapes=[
            pltpu.VMEM((width, pieces * width), BF16),
            pltpu.SemaphoreType.DMA((1 + pieces * (length // 128 + 1),)),
        ],
        compiler_params=limit(58),
        cost_estimate=pl.CostEstimate(
            flops=600_000_000, bytes_accessed=4_000_000, transcendentals=0
        ),
        name="cotangent",
    )(lax.axis_index(HEAD)[None], portion, out_weight)
    column, portion_b, gatt, gatt_t, weight_cols = lax.optimization_barrier(
        (column, portion_b, gatt, gatt_t, weight_cols)
    )
    chosen = pl.pallas_call(
        spread_kernel,
        out_shape=jax.ShapeDtypeStruct((los, NGLOB, step, width), BF16),
        in_specs=[smem(), anywhere()],
        out_specs=anywhere(),
        scratch_shapes=[pltpu.SemaphoreType.DMA((NGLOB * los,))],
        compiler_params=limit(1),
        name="spread",
    )(global_ids, column)
    chosen, joined_late, received[2], received[3] = lax.optimization_barrier(
        (chosen, joined, received[2], received[3])
    )
    globals_all = lax.all_to_all(chosen, "lo", 0, 0)
    received[1] = lax.ppermute(joined_late, CTX, routes[1])
    nheads = width // HD
    block = jax.ShapeDtypeStruct((2 * width, length), BF16)
    square = jax.ShapeDtypeStruct((length, width), F32)
    near_stats, near_sum, turned = pl.pallas_call(
        near_kernel,
        out_shape=(square, square, jax.ShapeDtypeStruct((width, length), BF16)),
        in_specs=[smem()] * 2 + vmem(5),
        out_specs=tuple(vmem(3)),
        scratch_shapes=[pltpu.VMEM((length, 5 * length), F32)],
        compiler_params=limit(12),
        cost_estimate=pl.CostEstimate(
            flops=1_000_000_000, bytes_accessed=1_000_000, transcendentals=650_000
        ),
        name="near",
    )(position[None], pair_active, joined, received[0], *received[2:])
    globals_all, near_stats, near_sum, turned = lax.optimization_barrier(
        (globals_all, near_stats, near_sum, turned)
    )
    attended, sums, stats, gglob = pl.pallas_call(
        forward_kernel,
        out_shape=(
            square,
            jax.ShapeDtypeStruct((los, 2 * HD, 128), BF16),
            square,
            square,
        ),
        in_specs=[smem()] * 2 + vmem(9),
        out_specs=tuple(vmem(4)),
        scratch_shapes=[
            pltpu.VMEM((nheads, length, (1 + NGLOB) * length), F32),
            pltpu.VMEM((length, width), F32),
        ],
        compiler_params=limit(20),
        cost_estimate=pl.CostEstimate(
            flops=3_000_000_000, bytes_accessed=4_000_000, transcendentals=1_100_000
        ),
        name="forward",
    )(
        position[None], pair_active, joined, received[1], near_stats, near_sum, turned, gatt_t,
        globals_all, portion_b, gatt,
    )

    shares = lax.all_to_all(sums, "lo", 0, 0)
    attended_all = lax.all_gather(attended, HEAD, axis=0)
    def backward(slots, name, gsum):
        inputs = [received[slot - 1] for slot in slots if slot > 0]
        shapes = [block if slot > 0 else whole for slot in slots] + [square]
        return pl.pallas_call(
            functools.partial(backward_kernel, slots),
            out_shape=tuple(shapes),
            in_specs=[smem()] * 2 + vmem(6 + len(inputs)),
            out_specs=tuple(vmem(len(shapes))),
            compiler_params=limit(10),
            cost_estimate=pl.CostEstimate(
                flops=1_000_000, bytes_accessed=10_000, transcendentals=0
            ),
            name=name,
        )(position[None], pair_active, joined, stats, turned, gatt_t, gatt, gsum, *inputs)

    whole = jax.ShapeDtypeStruct((2 * width, length), F32)
    terms = [None] * len(routes)
    terms[0], terms[1], terms[4], gquery = backward((1, 2, 5), "backward", gglob)
    returned = [None] * len(routes)
    for n in (1, 0):
        returned[n] = lax.ppermute(terms[n], CTX, routes[n])
    shares, terms[4], gquery = lax.optimization_barrier((shares, terms[4], gquery))
    share = jnp.sum(shares.astype(F32), axis=0).astype(BF16)
    share, returned[1], returned[0] = lax.optimization_barrier((share, returned[1], returned[0]))
    column = lax.all_to_all(jnp.broadcast_to(share[None], (his,) + share.shape), "hi", 0, 0)
    terms[2], terms[3], gown, gquery = backward((3, 4, 0), "backward_rest", gquery)
    for n in (4, 2, 3):
        returned[n] = lax.ppermute(terms[n], CTX, routes[n])
    share = jnp.sum(column.astype(F32), axis=0).astype(BF16)
    share, returned[4], returned[2], attended_all = lax.optimization_barrier(
        (share, returned[4], returned[2], attended_all)
    )
    totals = lax.all_to_all(jnp.broadcast_to(share[None], (los,) + share.shape), "lo", 0, 0)

    projected = pl.pallas_call(
        project_kernel,
        out_shape=jax.ShapeDtypeStruct((length, width), BF16),
        in_specs=vmem(2),
        out_specs=vmem(1)[0],
        compiler_params=limit(4),
        cost_estimate=pl.CostEstimate(
            flops=70_000_000, bytes_accessed=1_500_000, transcendentals=0
        ),
        name="project",
    )(attended_all, weight_cols)
    gqk, gval, gweight = pl.pallas_call(
        finish_kernel,
        out_shape=(
            jax.ShapeDtypeStruct((length, width), BF16),
            jax.ShapeDtypeStruct((length, width), BF16),
            jax.ShapeDtypeStruct((width, pieces * 128), F32),
        ),
        in_specs=[smem()] * 2 + vmem(8),
        out_specs=tuple(vmem(3)),
        compiler_params=limit(6),
        cost_estimate=pl.CostEstimate(
            flops=2_000_000, bytes_accessed=2_500_000, transcendentals=0
        ),
        name="finish",
    )(position[None], global_ids, *returned, gown, gquery, totals)
    return (projected, gqk, gval, gweight)


def solution(mesh):
    ctx, head = mesh.devices.shape
    inner = Mesh(mesh.devices.reshape(ctx // PATCH, PATCH, head), CTX + (HEAD,))
    row = P(CTX, HEAD)
    return jax.shard_map(
        local,
        mesh=inner,
        in_specs=(row, row, row, P(HEAD, None), P(), P()),
        out_specs=(row, row, row, P(HEAD, None)),
        check_vma=False,
    )
```

```python
import functools
import math

import jax
import jax.numpy as jnp
from jax import lax
from jax.experimental import pallas as pl
from jax.experimental.pallas import tpu as pltpu
from jax.sharding import Mesh, PartitionSpec as P

HD = 64
NGLOB = 2
ROUNDS = 4
CTX = ("hi", "lo")
HEAD = "head"
PATCH = 16
NT = (((1,), (1,)), ((), ()))
NN = (((1,), (0,)), ((), ()))
TN = (((0,), (0,)), ((), ()))
F32 = jnp.float32
BF16 = jnp.bfloat16
MASKED = -1e30


def dot(a, b, dims):
    return lax.dot_general(a, b, dims, preferred_element_type=F32)


def block_bias(pos_ref, pair_ref):
    position = pos_ref[0]
    devices = 2 * pair_ref.shape[1]
    linked = []
    for k in range(ROUNDS):
        stride = 1 << k
        lowest = jnp.bitwise_and(position, devices - 1 - stride)
        slot = jnp.right_shift(lowest, k + 1) * stride + jnp.bitwise_and(lowest, stride - 1)
        linked.append(pair_ref[k, slot] == 1)
    inside = jnp.logical_and(position > 0, position < devices - 1)
    zero = jnp.float32(0.0)
    bias = [zero, jnp.where(linked[0], jnp.float32(1.0), zero)]
    bias += [jnp.where(m, zero, jnp.float32(MASKED)) for m in [inside] + linked[1:]]
    return bias + [zero] * NGLOB


def cotangent_kernel(
    head_ref, all_ref, w_hbm, out_ref, gatt_ref, gattt_ref, cols_ref, w_ref, sems
):
    pieces, length, width = out_ref.shape
    blocks = length // 128
    copies = [pltpu.make_async_copy(w_hbm, w_ref, sems.at[0])]
    for c in range(pieces):
        for b in range(blocks):
            copies.append(pltpu.make_async_copy(
                all_ref.at[c, b], out_ref.at[c, pl.ds(b * 128, 128)], sems.at[len(copies)]
            ))
    late = len(copies)
    for c in range(pieces):
        copies.append(pltpu.make_async_copy(
            all_ref.at[c, blocks + head_ref[0]], cols_ref.at[c], sems.at[len(copies)]
        ))
    for copy in copies:
        copy.start()
    for copy in copies[:late]:
        copy.wait()
    gatt = jnp.zeros((length, width), F32)
    for c in range(pieces):
        gatt = gatt + dot(out_ref[c], w_ref[:, c * width:(c + 1) * width], NT)
    gatt_ref[...] = gatt.astype(BF16)
    gattt_ref[...] = gatt.T.astype(BF16)
    for copy in copies[late:]:
        copy.wait()


def near_kernel(
    pos_ref, pair_ref, own_ref, p0, p2, p3, p4, stats_ref, sum_ref, turned_ref, score_ref,
):
    length = own_ref.shape[0] // 2
    width = own_ref.shape[1]
    nheads = width // HD
    base2 = 1.0 / math.sqrt(HD) / math.log(2.0)
    bias = block_bias(pos_ref, pair_ref)
    turned_ref[...] = own_ref[:length].astype(F32).T.astype(BF16)
    blocks = ((own_ref, bias[0]), (p0, bias[1]), (p2, bias[3]), (p3, bias[4]), (p4, bias[5]))
    query = own_ref[:length]
    lane = lax.broadcasted_iota(jnp.int32, (1, width), 1)
    head = lane // HD
    stats = jnp.zeros((length, width), F32)
    for h in range(nheads):
        query_h = jnp.where(head == h, query, jnp.zeros_like(query))
        highest = jnp.full((length, 1), MASKED, F32)
        for b, (ref, shift) in enumerate(blocks):
            s = dot(query_h, ref[:length], NT) * base2 + shift
            score_ref[:, b * length:(b + 1) * length] = s
            highest = jnp.maximum(highest, jnp.max(s, axis=1, keepdims=True))
        total = jnp.zeros((length, 1), F32)
        acc = jnp.zeros((length, width), F32)
        for b, (ref, _) in enumerate(blocks):
            e = jnp.exp2(score_ref[:, b * length:(b + 1) * length] - highest)
            total = total + jnp.sum(e, axis=1, keepdims=True)
            acc = acc + dot(e.astype(BF16), ref[length:], NN)
        stats = jnp.where(lane == h, highest, stats)
        stats = jnp.where(lane == nheads + h, total, stats)
        if h == 0:
            sum_ref[...] = acc
        else:
            sum_ref[...] = jnp.where(head == h, acc, sum_ref[...])
    stats_ref[...] = stats


def forward_kernel(
    pos_ref, pair_ref, own_ref, p1, near_ref, sum_ref, turned_ref, gattt_ref, glob_ref, gout_ref,
    gatt_ref,
    att_ref, sums_ref, stats_ref, gquery_ref,
    score_ref, out_ref,
):
    length = own_ref.shape[0] // 2
    width = own_ref.shape[1]
    pieces = gout_ref.shape[0]
    nheads = width // HD
    scaling = 1.0 / math.sqrt(HD)
    base2 = scaling / math.log(2.0)
    bias = block_bias(pos_ref, pair_ref)
    bias = [bias[2]] + bias[-NGLOB:]
    keys = [p1[:length]]
    vals = [p1[length:]]
    half = glob_ref.shape[0] // 2
    for g in range(NGLOB):
        keys.append(jnp.concatenate([glob_ref[p, g] for p in range(half)], axis=0))
        vals.append(jnp.concatenate([glob_ref[half + p, g] for p in range(half)], axis=0))
    count = len(keys)
    query = own_ref[:length]
    lane = lax.broadcasted_iota(jnp.int32, (1, width), 1)
    head = lane // HD
    gatt_b = gatt_ref[...]

    inverse = []
    stats = jnp.zeros((length, width), F32)
    for h in range(nheads):
        query_h = jnp.where(head == h, query, jnp.zeros_like(query))
        near = near_ref[:, h:h + 1]
        highest = near
        for b in range(count):
            s = dot(query_h, keys[b], NT) * base2 + bias[b]
            score_ref[h, :, b * length:(b + 1) * length] = s
            highest = jnp.maximum(highest, jnp.max(s, axis=1, keepdims=True))
        factor = jnp.exp2(near - highest)
        total = near_ref[:, nheads + h:nheads + h + 1] * factor
        acc = sum_ref[...] * factor
        for b in range(count):
            e = jnp.exp2(score_ref[h, :, b * length:(b + 1) * length] - highest)
            score_ref[h, :, b * length:(b + 1) * length] = e
            total = total + jnp.sum(e, axis=1, keepdims=True)
            acc = acc + dot(e.astype(BF16), vals[b], NN)
        inv = 1.0 / total
        inverse.append(inv)
        stats = jnp.where(lane == h, highest + jnp.log2(total), stats)
        if h == 0:
            out_ref[...] = acc * inv
        else:
            out_ref[...] = jnp.where(head == h, acc * inv, out_ref[...])

    attended = out_ref[...]
    att_ref[...] = attended
    attended_b = attended.astype(BF16)
    every = jnp.concatenate([gout_ref[c] for c in range(pieces)], axis=1)
    update = dot(attended_b, every, TN).astype(BF16)
    for c in range(pieces):
        part = update[:, c * 128:(c + 1) * 128]
        n = width // HD
        sums_ref[c * n:(c + 1) * n, 0:HD, :] = part.reshape(n, HD, 128)

    product = gatt_b.astype(F32) * attended
    query_t = turned_ref[...]
    gatt_t = gattt_ref[...]
    for h in range(nheads):
        gatt_h = jnp.where(head == h, gatt_b, jnp.zeros_like(gatt_b))
        row_dot = jnp.sum(jnp.where(head == h, product, 0.0), axis=1, keepdims=True)
        stats = jnp.where(lane == nheads + h, row_dot, stats)
        inv = inverse[h]
        qt = query_t[h * HD:(h + 1) * HD]
        gt = gatt_t[h * HD:(h + 1) * HD]
        acc = jnp.zeros((length, width), F32)
        for g in range(NGLOB):
            b = count - NGLOB + g
            weights = score_ref[h, :, b * length:(b + 1) * length] * inv
            gw = dot(gatt_h, vals[b], NT)
            gs = (weights * (gw - row_dot)).astype(BF16)
            acc = acc + dot(gs, keys[b], NN)
            gk = dot(qt, gs, NN) * scaling
            gv = dot(gt, weights.astype(BF16), NN)
            for a in range(length // 128):
                at = (g * (length // 128) + a) * 2 * nheads + h
                cols = slice(a * 128, (a + 1) * 128)
                sums_ref[at, HD:2 * HD, :] = gk[:, cols].astype(BF16)
                sums_ref[at + nheads, HD:2 * HD, :] = gv[:, cols].astype(BF16)
        if h == 0:
            out_ref[...] = acc
        else:
            out_ref[...] = jnp.where(head == h, acc, out_ref[...])
    stats_ref[...] = stats
    gquery_ref[...] = out_ref[...]


def backward_kernel(
    slots, pos_ref, pair_ref, own_ref, stats_ref, turned_ref, gattt_ref, gatt_ref, gsum_ref, *refs
):
    length = own_ref.shape[0] // 2
    width = own_ref.shape[1]
    nheads = width // HD
    scaling = 1.0 / math.sqrt(HD)
    base2 = scaling / math.log(2.0)
    bias = block_bias(pos_ref, pair_ref)
    inputs = sum(slot > 0 for slot in slots)
    blocks = list(refs[:inputs])
    outs, gquery_ref = refs[inputs:-1], refs[-1]
    if 0 in slots:
        blocks.insert(slots.index(0), own_ref)
    query = own_ref[:length]
    gatt_b = gatt_ref[...]
    head = lax.broadcasted_iota(jnp.int32, (1, width), 1) // HD
    query_t = turned_ref[...]
    gatt_t = gattt_ref[...]
    result = gsum_ref[...]
    for h in range(nheads):
        query_h = jnp.where(head == h, query, jnp.zeros_like(query))
        gatt_h = jnp.where(head == h, gatt_b, jnp.zeros_like(gatt_b))
        log_total = stats_ref[:, h:h + 1]
        row_dot = stats_ref[:, nheads + h:nheads + h + 1]
        qt = query_t[h * HD:(h + 1) * HD]
        gt = gatt_t[h * HD:(h + 1) * HD]
        acc = jnp.zeros((length, width), F32)
        for slot, ref, o in zip(slots, blocks, outs):
            keys = ref[:length]
            s = dot(query_h, keys, NT) * base2 + (bias[slot] - log_total)
            weights = jnp.exp2(s)
            gw = dot(gatt_h, ref[length:], NT)
            gs = (weights * (gw - row_dot)).astype(BF16)
            acc = acc + dot(gs, keys, NN)
            gk = dot(qt, gs, NN) * scaling
            gv = dot(gt, weights.astype(BF16), NN)
            o[h * HD:(h + 1) * HD, :] = gk.astype(o.dtype)
            o[width + h * HD:width + (h + 1) * HD, :] = gv.astype(o.dtype)
        result = result + jnp.where(head == h, acc, 0.0)
    gquery_ref[...] = result


def project_kernel(att_ref, w_ref, projected_ref):
    projected = jnp.zeros(projected_ref.shape, F32)
    for c in range(att_ref.shape[0]):
        projected = projected + dot(att_ref[c].astype(BF16), w_ref[c], NN)
    projected_ref[...] = projected.astype(BF16)


def finish_kernel(
    pos_ref, ids_ref, b0, b1, b2, b3, b4, gown_ref, gquery_ref, total_ref,
    gqk_ref, gval_ref, gweight_ref,
):
    length, width = gquery_ref.shape
    halves = length // 128
    rows = width * 2 // HD
    for a in range(halves):
        cols = slice(a * 128, (a + 1) * 128)
        acc = gown_ref[:, cols]
        for b in (b0, b1, b2, b3, b4):
            acc = acc + b[:, cols].astype(F32)
        for g in range(NGLOB):
            at = (g * halves + a) * rows
            term = total_ref[at:at + rows, HD:2 * HD, :].reshape(2 * width, 128).astype(F32)
            acc = acc + jnp.where(ids_ref[g] == pos_ref[0], term, 0.0)
        tokens = slice(a * 128, (a + 1) * 128)
        gqk_ref[tokens, :] = (gquery_ref[tokens, :] / math.sqrt(HD) + acc[:width].T).astype(BF16)
        gval_ref[tokens, :] = acc[width:].T.astype(BF16)
    n = width // HD
    for c in range(gweight_ref.shape[1] // 128):
        piece = total_ref[c * n:(c + 1) * n, 0:HD, :].reshape(width, 128)
        gweight_ref[:, c * 128:(c + 1) * 128] = piece.astype(F32)


def copy_all(copies):
    for copy in copies:
        copy.start()
    for copy in copies:
        copy.wait()


def pack_kernel(qk_ref, val_ref, gout_ref, w_ref, joined_ref, share_ref):
    length, width = qk_ref.shape
    blocks = length // 128
    joined_ref[:length] = qk_ref[...]
    joined_ref[length:] = val_ref[...]
    share_ref[0:blocks] = gout_ref[...].reshape(blocks, 128, width)
    for c in range(w_ref.shape[1] // 128):
        share_ref[blocks + c] = w_ref[:, c * 128:(c + 1) * 128]


def pick_kernel(ids_ref, slices_ref, out_ref, sems):
    count = out_ref.shape[0]
    copies = []
    for g in range(NGLOB):
        chosen = slices_ref.at[lax.rem(ids_ref[g], PATCH)]
        for n in range(count):
            sem = sems.at[g * count + n]
            copies.append(pltpu.make_async_copy(chosen, out_ref.at[n, g], sem))
    copy_all(copies)


def spread_kernel(ids_ref, slices_ref, out_ref, sems):
    count = out_ref.shape[0]
    copies = []
    for g in range(NGLOB):
        chosen = slices_ref.at[lax.div(ids_ref[g], PATCH), g]
        for n in range(count):
            sem = sems.at[g * count + n]
            copies.append(pltpu.make_async_copy(chosen, out_ref.at[n, g], sem))
    copy_all(copies)


def hbm():
    return pl.BlockSpec(memory_space=pltpu.HBM)


def anywhere():
    return pl.BlockSpec(memory_space=pl.ANY)


def limit(mebibytes):
    return pltpu.CompilerParams(vmem_limit_bytes=mebibytes * 1024 * 1024)


def vmem(count):
    return [pl.BlockSpec(memory_space=pltpu.VMEM)] * count


def smem():
    return pl.BlockSpec(memory_space=pltpu.SMEM)


def local(qk_vectors, token_values, grad_output, out_weight, global_ids, pair_active):
    length, width = qk_vectors.shape
    devices = lax.axis_size(CTX)
    pieces = lax.axis_size(HEAD)
    position = lax.axis_index(CTX)
    joined = jnp.concatenate([qk_vectors, token_values], axis=0)

    his, los = lax.axis_size("hi"), lax.axis_size("lo")
    step = 2 * length // los
    joined, share = pl.pallas_call(
        pack_kernel,
        out_shape=(
            jax.ShapeDtypeStruct((2 * length, width), BF16),
            jax.ShapeDtypeStruct((length // 128 + pieces, 128, width), BF16),
        ),
        in_specs=vmem(4),
        out_specs=tuple(vmem(2)),
        name="pack",
    )(qk_vectors, token_values, grad_output, out_weight)

    slices = lax.all_to_all(joined.reshape(los, step, width), "lo", 0, 0)
    portion = lax.all_gather(share, HEAD, axis=0)
    routes = [[(i, i ^ 1) for i in range(devices)]]
    other = [i + 1 if i % 2 else i - 1 for i in range(devices)]
    routes.append([(i, j) for i, j in enumerate(other) if 0 <= j < devices])
    routes += [[(i, i ^ (1 << k)) for i in range(devices)] for k in range(1, ROUNDS)]
    received = [None] * len(routes)
    for n in (3, 0):
        received[n] = lax.ppermute(joined, CTX, routes[n])
    picked = pl.pallas_call(
        pick_kernel,
        out_shape=jax.ShapeDtypeStruct((his, NGLOB, step, width), BF16),
        in_specs=[smem(), anywhere()],
        out_specs=anywhere(),
        scratch_shapes=[pltpu.SemaphoreType.DMA((NGLOB * his,))],
        compiler_params=limit(1),
        name="pick",
    )(global_ids, slices)
    picked, joined_late, received[0], received[3] = lax.optimization_barrier(
        (picked, joined, received[0], received[3])
    )
    column = lax.all_to_all(picked, "hi", 0, 0)
    for n in (4, 2):
        received[n] = lax.ppermute(joined_late, CTX, routes[n])
    portion_b, gatt, gatt_t, weight_cols = pl.pallas_call(
        cotangent_kernel,
        out_shape=(
            jax.ShapeDtypeStruct((pieces, length, width), BF16),
            jax.ShapeDtypeStruct((length, width), BF16),
            jax.ShapeDtypeStruct((width, length), BF16),
            jax.ShapeDtypeStruct((pieces, width, 128), BF16),
        ),
        in_specs=[smem(), hbm(), hbm()],
        out_specs=tuple(vmem(4)),
        scratch_shapes=[
            pltpu.VMEM((width, pieces * width), BF16),
            pltpu.SemaphoreType.DMA((1 + pieces * (length // 128 + 1),)),
        ],
        compiler_params=limit(58),
        cost_estimate=pl.CostEstimate(
            flops=600_000_000, bytes_accessed=4_000_000, transcendentals=0
        ),
        name="cotangent",
    )(lax.axis_index(HEAD)[None], portion, out_weight)
    column, portion_b, gatt, gatt_t, weight_cols = lax.optimization_barrier(
        (column, portion_b, gatt, gatt_t, weight_cols)
    )
    chosen = pl.pallas_call(
        spread_kernel,
        out_shape=jax.ShapeDtypeStruct((los, NGLOB, step, width), BF16),
        in_specs=[smem(), anywhere()],
        out_specs=anywhere(),
        scratch_shapes=[pltpu.SemaphoreType.DMA((NGLOB * los,))],
        compiler_params=limit(1),
        name="spread",
    )(global_ids, column)
    chosen, joined_late, received[2], received[4] = lax.optimization_barrier(
        (chosen, joined, received[2], received[4])
    )
    globals_all = lax.all_to_all(chosen, "lo", 0, 0)
    received[1] = lax.ppermute(joined_late, CTX, routes[1])
    nheads = width // HD
    block = jax.ShapeDtypeStruct((2 * width, length), BF16)
    square = jax.ShapeDtypeStruct((length, width), F32)
    near_stats, near_sum, turned = pl.pallas_call(
        near_kernel,
        out_shape=(square, square, jax.ShapeDtypeStruct((width, length), BF16)),
        in_specs=[smem()] * 2 + vmem(5),
        out_specs=tuple(vmem(3)),
        scratch_shapes=[pltpu.VMEM((length, 5 * length), F32)],
        compiler_params=limit(12),
        cost_estimate=pl.CostEstimate(
            flops=1_000_000_000, bytes_accessed=1_000_000, transcendentals=650_000
        ),
        name="near",
    )(position[None], pair_active, joined, received[0], *received[2:])
    globals_all, near_stats, near_sum, turned = lax.optimization_barrier(
        (globals_all, near_stats, near_sum, turned)
    )
    attended, sums, stats, gglob = pl.pallas_call(
        forward_kernel,
        out_shape=(
            square,
            jax.ShapeDtypeStruct((los, 2 * HD, 128), BF16),
            square,
            square,
        ),
        in_specs=[smem()] * 2 + vmem(9),
        out_specs=tuple(vmem(4)),
        scratch_shapes=[
            pltpu.VMEM((nheads, length, (1 + NGLOB) * length), F32),
            pltpu.VMEM((length, width), F32),
        ],
        compiler_params=limit(20),
        cost_estimate=pl.CostEstimate(
            flops=3_000_000_000, bytes_accessed=4_000_000, transcendentals=1_100_000
        ),
        name="forward",
    )(
        position[None], pair_active, joined, received[1], near_stats, near_sum, turned, gatt_t,
        globals_all, portion_b, gatt,
    )

    shares = lax.all_to_all(sums, "lo", 0, 0)
    attended_all = lax.all_gather(attended, HEAD, axis=0)
    def backward(slots, name, gsum):
        inputs = [received[slot - 1] for slot in slots if slot > 0]
        shapes = [block if slot > 0 else whole for slot in slots] + [square]
        return pl.pallas_call(
            functools.partial(backward_kernel, slots),
            out_shape=tuple(shapes),
            in_specs=[smem()] * 2 + vmem(6 + len(inputs)),
            out_specs=tuple(vmem(len(shapes))),
            compiler_params=limit(10),
            cost_estimate=pl.CostEstimate(
                flops=1_000_000, bytes_accessed=10_000, transcendentals=0
            ),
            name=name,
        )(position[None], pair_active, joined, stats, turned, gatt_t, gatt, gsum, *inputs)

    whole = jax.ShapeDtypeStruct((2 * width, length), F32)
    terms = [None] * len(routes)
    terms[0], terms[1], terms[3], gquery = backward((1, 2, 4), "backward", gglob)
    returned = [None] * len(routes)
    for n in (1, 0):
        returned[n] = lax.ppermute(terms[n], CTX, routes[n])
    shares, terms[3], gquery = lax.optimization_barrier((shares, terms[3], gquery))
    share = jnp.sum(shares.astype(F32), axis=0).astype(BF16)
    share, returned[1], returned[0] = lax.optimization_barrier((share, returned[1], returned[0]))
    column = lax.all_to_all(jnp.broadcast_to(share[None], (his,) + share.shape), "hi", 0, 0)
    terms[2], terms[4], gown, gquery = backward((3, 5, 0), "backward_rest", gquery)
    for n in (3, 2, 4):
        returned[n] = lax.ppermute(terms[n], CTX, routes[n])
    share = jnp.sum(column.astype(F32), axis=0).astype(BF16)
    share, returned[3], returned[2], attended_all = lax.optimization_barrier(
        (share, returned[3], returned[2], attended_all)
    )
    totals = lax.all_to_all(jnp.broadcast_to(share[None], (los,) + share.shape), "lo", 0, 0)

    projected = pl.pallas_call(
        project_kernel,
        out_shape=jax.ShapeDtypeStruct((length, width), BF16),
        in_specs=vmem(2),
        out_specs=vmem(1)[0],
        compiler_params=limit(4),
        cost_estimate=pl.CostEstimate(
            flops=70_000_000, bytes_accessed=1_500_000, transcendentals=0
        ),
        name="project",
    )(attended_all, weight_cols)
    gqk, gval, gweight = pl.pallas_call(
        finish_kernel,
        out_shape=(
            jax.ShapeDtypeStruct((length, width), BF16),
            jax.ShapeDtypeStruct((length, width), BF16),
            jax.ShapeDtypeStruct((width, pieces * 128), F32),
        ),
        in_specs=[smem()] * 2 + vmem(8),
        out_specs=tuple(vmem(3)),
        compiler_params=limit(6),
        cost_estimate=pl.CostEstimate(
            flops=2_000_000, bytes_accessed=2_500_000, transcendentals=0
        ),
        name="finish",
    )(position[None], global_ids, *returned, gown, gquery, totals)
    return (projected, gqk, gval, gweight)


def solution(mesh):
    ctx, head = mesh.devices.shape
    inner = Mesh(mesh.devices.reshape(ctx // PATCH, PATCH, head), CTX + (HEAD,))
    row = P(CTX, HEAD)
    return jax.shard_map(
        local,
        mesh=inner,
        in_specs=(row, row, row, P(HEAD, None), P(), P()),
        out_specs=(row, row, row, P(HEAD, None)),
        check_vma=False,
    )
```

```python
import functools
import math

import jax
import jax.numpy as jnp
from jax import lax
from jax.experimental import pallas as pl
from jax.experimental.pallas import tpu as pltpu
from jax.sharding import Mesh, PartitionSpec as P

HD = 64
NGLOB = 2
ROUNDS = 4
CTX = ("hi", "lo")
HEAD = "head"
PATCH = 16
NT = (((1,), (1,)), ((), ()))
NN = (((1,), (0,)), ((), ()))
TN = (((0,), (0,)), ((), ()))
F32 = jnp.float32
BF16 = jnp.bfloat16
MASKED = -1e30


def dot(a, b, dims):
    return lax.dot_general(a, b, dims, preferred_element_type=F32)


def block_bias(pos_ref, pair_ref):
    position = pos_ref[0]
    devices = 2 * pair_ref.shape[1]
    linked = []
    for k in range(ROUNDS):
        stride = 1 << k
        lowest = jnp.bitwise_and(position, devices - 1 - stride)
        slot = jnp.right_shift(lowest, k + 1) * stride + jnp.bitwise_and(lowest, stride - 1)
        linked.append(pair_ref[k, slot] == 1)
    inside = jnp.logical_and(position > 0, position < devices - 1)
    zero = jnp.float32(0.0)
    bias = [zero, jnp.where(linked[0], jnp.float32(1.0), zero)]
    bias += [jnp.where(m, zero, jnp.float32(MASKED)) for m in [inside] + linked[1:]]
    return bias + [zero] * NGLOB


def cotangent_kernel(
    head_ref, all_ref, w_hbm, out_ref, gatt_ref, gattt_ref, cols_ref, w_ref, sems
):
    pieces, length, width = out_ref.shape
    blocks = length // 128
    copies = [pltpu.make_async_copy(w_hbm, w_ref, sems.at[0])]
    for c in range(pieces):
        for b in range(blocks):
            copies.append(pltpu.make_async_copy(
                all_ref.at[c, b], out_ref.at[c, pl.ds(b * 128, 128)], sems.at[len(copies)]
            ))
    late = len(copies)
    for c in range(pieces):
        copies.append(pltpu.make_async_copy(
            all_ref.at[c, blocks + head_ref[0]], cols_ref.at[c], sems.at[len(copies)]
        ))
    for copy in copies:
        copy.start()
    for copy in copies[:late]:
        copy.wait()
    gatt = jnp.zeros((length, width), F32)
    for c in range(pieces):
        gatt = gatt + dot(out_ref[c], w_ref[:, c * width:(c + 1) * width], NT)
    gatt_ref[...] = gatt.astype(BF16)
    gattt_ref[...] = gatt.T.astype(BF16)
    for copy in copies[late:]:
        copy.wait()


def near_kernel(
    pos_ref, pair_ref, own_ref, p0, p2, p3, p4, stats_ref, sum_ref, turned_ref, score_ref,
):
    length = own_ref.shape[0] // 2
    width = own_ref.shape[1]
    nheads = width // HD
    base2 = 1.0 / math.sqrt(HD) / math.log(2.0)
    bias = block_bias(pos_ref, pair_ref)
    turned_ref[...] = own_ref[:length].astype(F32).T.astype(BF16)
    blocks = ((own_ref, bias[0]), (p0, bias[1]), (p2, bias[3]), (p3, bias[4]), (p4, bias[5]))
    query = own_ref[:length]
    lane = lax.broadcasted_iota(jnp.int32, (1, width), 1)
    head = lane // HD
    stats = jnp.zeros((length, width), F32)
    for h in range(nheads):
        query_h = jnp.where(head == h, query, jnp.zeros_like(query))
        highest = jnp.full((length, 1), MASKED, F32)
        for b, (ref, shift) in enumerate(blocks):
            s = dot(query_h, ref[:length], NT) * base2 + shift
            score_ref[:, b * length:(b + 1) * length] = s
            highest = jnp.maximum(highest, jnp.max(s, axis=1, keepdims=True))
        total = jnp.zeros((length, 1), F32)
        acc = jnp.zeros((length, width), F32)
        for b, (ref, _) in enumerate(blocks):
            e = jnp.exp2(score_ref[:, b * length:(b + 1) * length] - highest)
            total = total + jnp.sum(e, axis=1, keepdims=True)
            acc = acc + dot(e.astype(BF16), ref[length:], NN)
        stats = jnp.where(lane == h, highest, stats)
        stats = jnp.where(lane == nheads + h, total, stats)
        if h == 0:
            sum_ref[...] = acc
        else:
            sum_ref[...] = jnp.where(head == h, acc, sum_ref[...])
    stats_ref[...] = stats


def forward_kernel(
    pos_ref, pair_ref, own_ref, p1, near_ref, sum_ref, turned_ref, gattt_ref, glob_ref, gout_ref,
    gatt_ref,
    att_ref, sums_ref, stats_ref, gquery_ref,
    score_ref, out_ref,
):
    length = own_ref.shape[0] // 2
    width = own_ref.shape[1]
    pieces = gout_ref.shape[0]
    nheads = width // HD
    scaling = 1.0 / math.sqrt(HD)
    base2 = scaling / math.log(2.0)
    bias = block_bias(pos_ref, pair_ref)
    bias = [bias[2]] + bias[-NGLOB:]
    keys = [p1[:length]]
    vals = [p1[length:]]
    half = glob_ref.shape[0] // 2
    for g in range(NGLOB):
        keys.append(jnp.concatenate([glob_ref[p, g] for p in range(half)], axis=0))
        vals.append(jnp.concatenate([glob_ref[half + p, g] for p in range(half)], axis=0))
    count = len(keys)
    query = own_ref[:length]
    lane = lax.broadcasted_iota(jnp.int32, (1, width), 1)
    head = lane // HD
    gatt_b = gatt_ref[...]

    inverse = []
    stats = jnp.zeros((length, width), F32)
    for h in range(nheads):
        query_h = jnp.where(head == h, query, jnp.zeros_like(query))
        near = near_ref[:, h:h + 1]
        highest = near
        for b in range(count):
            s = dot(query_h, keys[b], NT) * base2 + bias[b]
            score_ref[h, :, b * length:(b + 1) * length] = s
            highest = jnp.maximum(highest, jnp.max(s, axis=1, keepdims=True))
        factor = jnp.exp2(near - highest)
        total = near_ref[:, nheads + h:nheads + h + 1] * factor
        acc = sum_ref[...] * factor
        for b in range(count):
            e = jnp.exp2(score_ref[h, :, b * length:(b + 1) * length] - highest)
            score_ref[h, :, b * length:(b + 1) * length] = e
            total = total + jnp.sum(e, axis=1, keepdims=True)
            acc = acc + dot(e.astype(BF16), vals[b], NN)
        inv = 1.0 / total
        inverse.append(inv)
        stats = jnp.where(lane == h, highest + jnp.log2(total), stats)
        if h == 0:
            out_ref[...] = acc * inv
        else:
            out_ref[...] = jnp.where(head == h, acc * inv, out_ref[...])

    attended = out_ref[...]
    att_ref[...] = attended
    attended_b = attended.astype(BF16)
    every = jnp.concatenate([gout_ref[c] for c in range(pieces)], axis=1)
    update = dot(attended_b, every, TN).astype(BF16)
    for c in range(pieces):
        part = update[:, c * 128:(c + 1) * 128]
        n = width // HD
        sums_ref[c * n:(c + 1) * n, 0:HD, :] = part.reshape(n, HD, 128)

    product = gatt_b.astype(F32) * attended
    query_t = turned_ref[...]
    gatt_t = gattt_ref[...]
    for h in range(nheads):
        gatt_h = jnp.where(head == h, gatt_b, jnp.zeros_like(gatt_b))
        row_dot = jnp.sum(jnp.where(head == h, product, 0.0), axis=1, keepdims=True)
        stats = jnp.where(lane == nheads + h, row_dot, stats)
        inv = inverse[h]
        qt = query_t[h * HD:(h + 1) * HD]
        gt = gatt_t[h * HD:(h + 1) * HD]
        acc = jnp.zeros((length, width), F32)
        for g in range(NGLOB):
            b = count - NGLOB + g
            weights = score_ref[h, :, b * length:(b + 1) * length] * inv
            gw = dot(gatt_h, vals[b], NT)
            gs = (weights * (gw - row_dot)).astype(BF16)
            acc = acc + dot(gs, keys[b], NN)
            gk = dot(qt, gs, NN) * scaling
            gv = dot(gt, weights.astype(BF16), NN)
            for a in range(length // 128):
                at = (g * (length // 128) + a) * 2 * nheads + h
                cols = slice(a * 128, (a + 1) * 128)
                sums_ref[at, HD:2 * HD, :] = gk[:, cols].astype(BF16)
                sums_ref[at + nheads, HD:2 * HD, :] = gv[:, cols].astype(BF16)
        if h == 0:
            out_ref[...] = acc
        else:
            out_ref[...] = jnp.where(head == h, acc, out_ref[...])
    stats_ref[...] = stats
    gquery_ref[...] = out_ref[...]


def backward_kernel(
    slots, pos_ref, pair_ref, own_ref, stats_ref, turned_ref, gattt_ref, gatt_ref, gsum_ref, *refs
):
    length = own_ref.shape[0] // 2
    width = own_ref.shape[1]
    nheads = width // HD
    scaling = 1.0 / math.sqrt(HD)
    base2 = scaling / math.log(2.0)
    bias = block_bias(pos_ref, pair_ref)
    inputs = sum(slot > 0 for slot in slots)
    blocks = list(refs[:inputs])
    outs, gquery_ref = refs[inputs:-1], refs[-1]
    if 0 in slots:
        blocks.insert(slots.index(0), own_ref)
    query = own_ref[:length]
    gatt_b = gatt_ref[...]
    head = lax.broadcasted_iota(jnp.int32, (1, width), 1) // HD
    query_t = turned_ref[...]
    gatt_t = gattt_ref[...]
    result = gsum_ref[...]
    for h in range(nheads):
        query_h = jnp.where(head == h, query, jnp.zeros_like(query))
        gatt_h = jnp.where(head == h, gatt_b, jnp.zeros_like(gatt_b))
        log_total = stats_ref[:, h:h + 1]
        row_dot = stats_ref[:, nheads + h:nheads + h + 1]
        qt = query_t[h * HD:(h + 1) * HD]
        gt = gatt_t[h * HD:(h + 1) * HD]
        acc = jnp.zeros((length, width), F32)
        for slot, ref, o in zip(slots, blocks, outs):
            keys = ref[:length]
            s = dot(query_h, keys, NT) * base2 + (bias[slot] - log_total)
            weights = jnp.exp2(s)
            gw = dot(gatt_h, ref[length:], NT)
            gs = (weights * (gw - row_dot)).astype(BF16)
            acc = acc + dot(gs, keys, NN)
            gk = dot(qt, gs, NN) * scaling
            gv = dot(gt, weights.astype(BF16), NN)
            o[h * HD:(h + 1) * HD, :] = gk.astype(o.dtype)
            o[width + h * HD:width + (h + 1) * HD, :] = gv.astype(o.dtype)
        result = result + jnp.where(head == h, acc, 0.0)
    gquery_ref[...] = result


def project_kernel(att_ref, w_ref, projected_ref):
    projected = jnp.zeros(projected_ref.shape, F32)
    for c in range(att_ref.shape[0]):
        projected = projected + dot(att_ref[c].astype(BF16), w_ref[c], NN)
    projected_ref[...] = projected.astype(BF16)


def finish_kernel(
    pos_ref, ids_ref, b0, b1, b2, b3, b4, gown_ref, gquery_ref, total_ref,
    gqk_ref, gval_ref, gweight_ref,
):
    length, width = gquery_ref.shape
    halves = length // 128
    rows = width * 2 // HD
    for a in range(halves):
        cols = slice(a * 128, (a + 1) * 128)
        acc = gown_ref[:, cols]
        for b in (b0, b1, b2, b3, b4):
            acc = acc + b[:, cols].astype(F32)
        for g in range(NGLOB):
            at = (g * halves + a) * rows
            term = total_ref[at:at + rows, HD:2 * HD, :].reshape(2 * width, 128).astype(F32)
            acc = acc + jnp.where(ids_ref[g] == pos_ref[0], term, 0.0)
        tokens = slice(a * 128, (a + 1) * 128)
        gqk_ref[tokens, :] = (gquery_ref[tokens, :] / math.sqrt(HD) + acc[:width].T).astype(BF16)
        gval_ref[tokens, :] = acc[width:].T.astype(BF16)
    n = width // HD
    for c in range(gweight_ref.shape[1] // 128):
        piece = total_ref[c * n:(c + 1) * n, 0:HD, :].reshape(width, 128)
        gweight_ref[:, c * 128:(c + 1) * 128] = piece.astype(F32)


def copy_all(copies):
    for copy in copies:
        copy.start()
    for copy in copies:
        copy.wait()


def pack_kernel(qk_ref, val_ref, gout_ref, w_ref, joined_ref, share_ref):
    length, width = qk_ref.shape
    blocks = length // 128
    joined_ref[:length] = qk_ref[...]
    joined_ref[length:] = val_ref[...]
    share_ref[0:blocks] = gout_ref[...].reshape(blocks, 128, width)
    for c in range(w_ref.shape[1] // 128):
        share_ref[blocks + c] = w_ref[:, c * 128:(c + 1) * 128]


def pick_kernel(ids_ref, slices_ref, out_ref, sems):
    count = out_ref.shape[0]
    copies = []
    for g in range(NGLOB):
        chosen = slices_ref.at[lax.rem(ids_ref[g], PATCH)]
        for n in range(count):
            sem = sems.at[g * count + n]
            copies.append(pltpu.make_async_copy(chosen, out_ref.at[n, g], sem))
    copy_all(copies)


def spread_kernel(ids_ref, slices_ref, out_ref, sems):
    count = out_ref.shape[0]
    copies = []
    for g in range(NGLOB):
        chosen = slices_ref.at[lax.div(ids_ref[g], PATCH), g]
        for n in range(count):
            sem = sems.at[g * count + n]
            copies.append(pltpu.make_async_copy(chosen, out_ref.at[n, g], sem))
    copy_all(copies)


def hbm():
    return pl.BlockSpec(memory_space=pltpu.HBM)


def anywhere():
    return pl.BlockSpec(memory_space=pl.ANY)


def limit(mebibytes):
    return pltpu.CompilerParams(vmem_limit_bytes=mebibytes * 1024 * 1024)


def vmem(count):
    return [pl.BlockSpec(memory_space=pltpu.VMEM)] * count


def smem():
    return pl.BlockSpec(memory_space=pltpu.SMEM)


def local(qk_vectors, token_values, grad_output, out_weight, global_ids, pair_active):
    length, width = qk_vectors.shape
    devices = lax.axis_size(CTX)
    pieces = lax.axis_size(HEAD)
    position = lax.axis_index(CTX)
    joined = jnp.concatenate([qk_vectors, token_values], axis=0)

    his, los = lax.axis_size("hi"), lax.axis_size("lo")
    step = 2 * length // los
    joined, share = pl.pallas_call(
        pack_kernel,
        out_shape=(
            jax.ShapeDtypeStruct((2 * length, width), BF16),
            jax.ShapeDtypeStruct((length // 128 + pieces, 128, width), BF16),
        ),
        in_specs=vmem(4),
        out_specs=tuple(vmem(2)),
        name="pack",
    )(qk_vectors, token_values, grad_output, out_weight)

    slices = lax.all_to_all(joined.reshape(los, step, width), "lo", 0, 0)
    portion = lax.all_gather(share, HEAD, axis=0)
    routes = [[(i, i ^ 1) for i in range(devices)]]
    other = [i + 1 if i % 2 else i - 1 for i in range(devices)]
    routes.append([(i, j) for i, j in enumerate(other) if 0 <= j < devices])
    routes += [[(i, i ^ (1 << k)) for i in range(devices)] for k in range(1, ROUNDS)]
    received = [None] * len(routes)
    for n in (4, 0):
        received[n] = lax.ppermute(joined, CTX, routes[n])
    picked = pl.pallas_call(
        pick_kernel,
        out_shape=jax.ShapeDtypeStruct((his, NGLOB, step, width), BF16),
        in_specs=[smem(), anywhere()],
        out_specs=anywhere(),
        scratch_shapes=[pltpu.SemaphoreType.DMA((NGLOB * his,))],
        compiler_params=limit(1),
        name="pick",
    )(global_ids, slices)
    picked, joined_late, received[0], received[4] = lax.optimization_barrier(
        (picked, joined, received[0], received[4])
    )
    column = lax.all_to_all(picked, "hi", 0, 0)
    for n in (3, 2):
        received[n] = lax.ppermute(joined_late, CTX, routes[n])
    portion_b, gatt, gatt_t, weight_cols = pl.pallas_call(
        cotangent_kernel,
        out_shape=(
            jax.ShapeDtypeStruct((pieces, length, width), BF16),
            jax.ShapeDtypeStruct((length, width), BF16),
            jax.ShapeDtypeStruct((width, length), BF16),
            jax.ShapeDtypeStruct((pieces, width, 128), BF16),
        ),
        in_specs=[smem(), hbm(), hbm()],
        out_specs=tuple(vmem(4)),
        scratch_shapes=[
            pltpu.VMEM((width, pieces * width), BF16),
            pltpu.SemaphoreType.DMA((1 + pieces * (length // 128 + 1),)),
        ],
        compiler_params=limit(58),
        cost_estimate=pl.CostEstimate(
            flops=600_000_000, bytes_accessed=4_000_000, transcendentals=0
        ),
        name="cotangent",
    )(lax.axis_index(HEAD)[None], portion, out_weight)
    column, portion_b, gatt, gatt_t, weight_cols = lax.optimization_barrier(
        (column, portion_b, gatt, gatt_t, weight_cols)
    )
    chosen = pl.pallas_call(
        spread_kernel,
        out_shape=jax.ShapeDtypeStruct((los, NGLOB, step, width), BF16),
        in_specs=[smem(), anywhere()],
        out_specs=anywhere(),
        scratch_shapes=[pltpu.SemaphoreType.DMA((NGLOB * los,))],
        compiler_params=limit(1),
        name="spread",
    )(global_ids, column)
    chosen, joined_late, received[2], received[3] = lax.optimization_barrier(
        (chosen, joined, received[2], received[3])
    )
    globals_all = lax.all_to_all(chosen, "lo", 0, 0)
    received[1] = lax.ppermute(joined_late, CTX, routes[1])
    nheads = width // HD
    block = jax.ShapeDtypeStruct((2 * width, length), BF16)
    square = jax.ShapeDtypeStruct((length, width), F32)
    near_stats, near_sum, turned = pl.pallas_call(
        near_kernel,
        out_shape=(square, square, jax.ShapeDtypeStruct((width, length), BF16)),
        in_specs=[smem()] * 2 + vmem(5),
        out_specs=tuple(vmem(3)),
        scratch_shapes=[pltpu.VMEM((length, 5 * length), F32)],
        compiler_params=limit(12),
        cost_estimate=pl.CostEstimate(
            flops=1_000_000_000, bytes_accessed=1_000_000, transcendentals=650_000
        ),
        name="near",
    )(position[None], pair_active, joined, received[0], *received[2:])
    globals_all, near_stats, near_sum, turned = lax.optimization_barrier(
        (globals_all, near_stats, near_sum, turned)
    )
    attended, sums, stats, gglob = pl.pallas_call(
        forward_kernel,
        out_shape=(
            square,
            jax.ShapeDtypeStruct((los, 2 * HD, 128), BF16),
            square,
            square,
        ),
        in_specs=[smem()] * 2 + vmem(9),
        out_specs=tuple(vmem(4)),
        scratch_shapes=[
            pltpu.VMEM((nheads, length, (1 + NGLOB) * length), F32),
            pltpu.VMEM((length, width), F32),
        ],
        compiler_params=limit(20),
        cost_estimate=pl.CostEstimate(
            flops=3_000_000_000, bytes_accessed=4_000_000, transcendentals=1_100_000
        ),
        name="forward",
    )(
        position[None], pair_active, joined, received[1], near_stats, near_sum, turned, gatt_t,
        globals_all, portion_b, gatt,
    )

    shares = lax.all_to_all(sums, "lo", 0, 0)
    attended_all = lax.all_gather(attended, HEAD, axis=0)
    def backward(slots, name, gsum):
        inputs = [received[slot - 1] for slot in slots if slot > 0]
        shapes = [block if slot > 0 else whole for slot in slots] + [square]
        return pl.pallas_call(
            functools.partial(backward_kernel, slots),
            out_shape=tuple(shapes),
            in_specs=[smem()] * 2 + vmem(6 + len(inputs)),
            out_specs=tuple(vmem(len(shapes))),
            compiler_params=limit(10),
            cost_estimate=pl.CostEstimate(
                flops=1_000_000, bytes_accessed=10_000, transcendentals=0
            ),
            name=name,
        )(position[None], pair_active, joined, stats, turned, gatt_t, gatt, gsum, *inputs)

    whole = jax.ShapeDtypeStruct((2 * width, length), F32)
    terms = [None] * len(routes)
    terms[0], terms[1], terms[4], gquery = backward((1, 2, 5), "backward", gglob)
    returned = [None] * len(routes)
    for n in (1, 0):
        returned[n] = lax.ppermute(terms[n], CTX, routes[n])
    shares, terms[4], gquery = lax.optimization_barrier((shares, terms[4], gquery))
    share = jnp.sum(shares.astype(F32), axis=0).astype(BF16)
    share, returned[1], returned[0] = lax.optimization_barrier((share, returned[1], returned[0]))
    column = lax.all_to_all(jnp.broadcast_to(share[None], (his,) + share.shape), "hi", 0, 0)
    terms[2], terms[3], gown, gquery = backward((3, 4, 0), "backward_rest", gquery)
    for n in (4, 3, 2):
        returned[n] = lax.ppermute(terms[n], CTX, routes[n])
    share = jnp.sum(column.astype(F32), axis=0).astype(BF16)
    share, returned[4], returned[3], attended_all = lax.optimization_barrier(
        (share, returned[4], returned[3], attended_all)
    )
    totals = lax.all_to_all(jnp.broadcast_to(share[None], (los,) + share.shape), "lo", 0, 0)

    projected = pl.pallas_call(
        project_kernel,
        out_shape=jax.ShapeDtypeStruct((length, width), BF16),
        in_specs=vmem(2),
        out_specs=vmem(1)[0],
        compiler_params=limit(4),
        cost_estimate=pl.CostEstimate(
            flops=70_000_000, bytes_accessed=1_500_000, transcendentals=0
        ),
        name="project",
    )(attended_all, weight_cols)
    gqk, gval, gweight = pl.pallas_call(
        finish_kernel,
        out_shape=(
            jax.ShapeDtypeStruct((length, width), BF16),
            jax.ShapeDtypeStruct((length, width), BF16),
            jax.ShapeDtypeStruct((width, pieces * 128), F32),
        ),
        in_specs=[smem()] * 2 + vmem(8),
        out_specs=tuple(vmem(3)),
        compiler_params=limit(6),
        cost_estimate=pl.CostEstimate(
            flops=2_000_000, bytes_accessed=2_500_000, transcendentals=0
        ),
        name="finish",
    )(position[None], global_ids, *returned, gown, gquery, totals)
    return (projected, gqk, gval, gweight)


def solution(mesh):
    ctx, head = mesh.devices.shape
    inner = Mesh(mesh.devices.reshape(ctx // PATCH, PATCH, head), CTX + (HEAD,))
    row = P(CTX, HEAD)
    return jax.shard_map(
        local,
        mesh=inner,
        in_specs=(row, row, row, P(HEAD, None), P(), P()),
        out_specs=(row, row, row, P(HEAD, None)),
        check_vma=False,
    )
```
